32 devices in a mesh: ctx: 4 (over y, x), head: 8 (over z, core).
Axes of the slice: x: 2, y: 2, z: 4, core: 2. Of those that a mesh axis runs over, the one named last changes fastest.
Arguments:
- tokens: bfloat16 [2048, 8192], P('ctx'), may hold values from -6 to 6
- w_zx: bfloat16 [8192, 2, 8192], P('ctx', None, 'head'), may hold values from -0.0625 to 0.0625
- zx_scale: float32 [2, 8192], P(None, 'head'), may hold values from 0.5 to 2
- w_bc: bfloat16 [8192, 8, 512], P('ctx'), may hold values from -0.0625 to 0.0625
- bc_scale: float32 [8, 512], replicated, may hold values from 0.5 to 2
- w_dt: bfloat16 [8192, 128], P('ctx', 'head'), may hold values from -0.0625 to 0.0625
- conv_x: float32 [5, 8192], P(None, 'head'), may hold values from -3 to 3
- conv_bc: float32 [5, 8, 512], replicated, may hold values from -3 to 3
- tail_x: bfloat16 [3, 8192], P(None, 'head'), may hold values from -6 to 6
- tail_bc: bfloat16 [3, 8, 512], replicated, may hold values from -6 to 6
- head_params: float32 [3, 128], P(None, 'head'), may hold values from -12 to 2, as said below
- init_state: float32 [128, 64, 256], P('head'), may hold values from -1.5 to 1.5
- norm_gain: float32 [8192], P('head'), may hold values from 0.5 to 1.5
Outputs:
- mixed: bfloat16 [2048, 8192], P('ctx', 'head')
The draws below stay inside these ranges and needn't reach their ends.
Inputs may be any that keep to these rules, and one draw needn't show every extreme that they name: `head_params`: row 0 lies in -3.5 to -2.5 and row 2 in 0.5 to 1.5.
All inputs are finite; a program needn't handle non-finite values.
Results may differ from the reference program's by a relative error of at most 0.0052.
Values may be sent and summed in bfloat16 or wider, within the bound.
No kernel may reach another device: no remote copies, remote signals or barrier semaphores. Data moves between devices by JAX's collectives and lax.ppermute only.
A program may use at most 256 MiB of HBM per device.

```python
import math
import jax
import jax.numpy as jnp
from jax import lax

D = 8192
H = 128
P_SIZE = 64
N = 256
G = 8
K = 4
TOK_DEV = 512
TOKENS = 2048
DI = 8192


def draw_head_params(key, part):
    keys = jax.random.split(key, 5)
    quick_share = 0.5
    quick = jax.random.bernoulli(keys[0], quick_share, (H,))
    bias_row = jax.random.uniform(keys[1], (H,), jnp.float32, -3.5, -2.5)
    quick_rate = jnp.exp(jax.random.uniform(keys[2], (H,), jnp.float32, jnp.log(0.4), jnp.log(1.2)))
    slow_rate = jnp.exp(jax.random.uniform(keys[3], (H,), jnp.float32, jnp.log(0.2), jnp.log(1.0))) / (0.07 * TOKENS)
    rate_row = jnp.log(jnp.where(quick, quick_rate, slow_rate))
    skip_row = jax.random.uniform(keys[4], (H,), jnp.float32, 0.5, 1.5)
    return jnp.stack([bias_row, rate_row, skip_row]).astype(jnp.float32)


def steps_of(own_key, extent, cuts, smallest, largest):
    level, own = 1.0, jax.random.fold_in(own_key, 6)
    for dim, parts in cuts:
        draws = jnp.exp(jax.random.uniform(jax.random.fold_in(own, dim), (parts,), jnp.float32, smallest / len(cuts), largest / len(cuts)))
        level = level * jnp.repeat(draws, extent[dim] // parts).reshape([-1 if axis == dim else 1 for axis in range(len(extent))])
    return level


def centred(rng, dims, scale, reach, cuts=(), dtype=jnp.bfloat16):
    drawn = scale * jax.random.normal(rng, dims, jnp.float32)
    if cuts:
        drawn = drawn * steps_of(rng, dims, cuts, -0.22, 0.18)
    return jnp.clip(drawn, -reach, reach).astype(dtype)


def setup_inputs(seed: int = 0) -> dict:
    splits = jax.random.split(jax.random.key(seed), 14)
    tokens = centred(splits[0], (TOKENS, D), 1.0, 6.0, ((0, 4),))
    w_zx = centred(splits[1], (D, 2, DI), D ** -0.5, 0.0625, ((0, 4), (2, 8)))
    zx_scale = jnp.clip(jnp.exp(math.log(2.0) - 1.3862944 * jax.random.uniform(splits[2], (2, DI), jnp.float32) ** steps_of(splits[2], (2, DI), ((1, 8),), -0.2, 0.2)), 0.5, 2.0)
    w_bc = centred(splits[3], (D, G, 2 * N), D ** -0.5, 0.0625, ((0, 4),))
    bc_scale = jnp.clip(jnp.exp(jax.random.uniform(splits[4], (G, 2 * N), jnp.float32, math.log(0.5), math.log(2.0))), 0.5, 2.0)
    w_dt = centred(splits[5], (D, H), D ** -0.5, 0.0625, ((0, 4), (1, 8)))
    conv_x = centred(splits[6], (K + 1, DI), 0.5, 3.0, ((1, 8),), jnp.float32)
    conv_bc = centred(splits[7], (K + 1, G, 2 * N), 0.5, 3.0, (), jnp.float32)
    tail_x = centred(splits[8], (K - 1, DI), 1.0, 6.0, ((1, 8),))
    tail_bc = centred(splits[9], (K - 1, G, 2 * N), 1.0, 6.0)
    head_params = draw_head_params(jax.random.fold_in(splits[13], 71), 0)
    init_state = centred(splits[11], (H, P_SIZE, N), 0.1, 1.5, ((0, 8),), jnp.float32)
    norm_gain = jnp.clip(1.0 + 0.1 * jax.random.normal(splits[12], (DI,), jnp.float32), 0.5, 1.5)
    return dict(tokens=tokens, w_zx=w_zx, zx_scale=zx_scale, w_bc=w_bc, bc_scale=bc_scale, w_dt=w_dt, conv_x=conv_x, conv_bc=conv_bc, tail_x=tail_x, tail_bc=tail_bc, head_params=head_params, init_state=init_state, norm_gain=norm_gain)


def conv_silu(values, before, taps):
    length = values.shape[0]
    padded = jnp.concatenate([before, values], 0).astype(jnp.float32)
    summed = taps[K]
    for tap_index in range(K):
        summed = summed + taps[tap_index] * padded[tap_index:tap_index + length]
    return jax.nn.silu(summed).astype(jnp.bfloat16)

def block_step(state, inputs):
    x_blk, b_blk, c_blk, rate_blk, step_blk = inputs
    highest = lax.Precision.HIGHEST
    cumul = jnp.cumsum(rate_blk, 0)
    length = x_blk.shape[0]
    order = jnp.arange(length)
    lower = (order[:, None] >= order[None, :])[:, :, None, None]
    spread = cumul[:, None] - cumul[None, :]
    decay = jnp.where(lower, jnp.exp(jnp.minimum(spread, 0.0)), 0.0)
    scores = jnp.einsum('tgn,sgn->tsg', c_blk, b_blk, precision=highest)
    weights = decay * scores[:, :, :, None] * step_blk[None]
    inner = jnp.einsum('tsgh,sghp->tghp', weights, x_blk, precision=highest)
    carried = jnp.einsum('tgn,ghpn->tghp', c_blk, state, precision=highest) * jnp.exp(cumul)[..., None]
    final = cumul[length - 1]
    fade = jnp.exp(final[None] - cumul) * step_blk
    new_state = jnp.exp(final)[..., None, None] * state + jnp.einsum('sgh,sghp,sgn->ghpn', fade, x_blk, b_blk, precision=highest)
    return (new_state, inner + carried)

def reference(tokens, w_zx, zx_scale, w_bc, bc_scale, w_dt, conv_x, conv_bc, tail_x, tail_bc, head_params, init_state, norm_gain):
    per_group = H // G
    zx_val = jnp.dot(tokens, w_zx.reshape(D, 2 * DI), preferred_element_type=jnp.float32).reshape(TOKENS, 2, DI)
    zx_val = (zx_val * zx_scale).astype(jnp.bfloat16)
    bc_val = jnp.dot(tokens, w_bc.reshape(D, G * 2 * N), preferred_element_type=jnp.float32).reshape(TOKENS, G, 2 * N)
    bc_val = (bc_val * bc_scale).astype(jnp.bfloat16)
    step_size = jax.nn.softplus(jnp.dot(tokens, w_dt, preferred_element_type=jnp.float32) + head_params[0])
    xconv = conv_silu(zx_val[:, 1], tail_x, conv_x)
    bconv = conv_silu(bc_val, tail_bc, conv_bc)
    rate = -jnp.exp(head_params[1]) * step_size
    block_len = math.gcd(TOK_DEV, 256)
    blocks = TOKENS // block_len
    x_all = xconv.astype(jnp.float32).reshape(blocks, block_len, G, per_group, P_SIZE)
    b_all = bconv[:, :, :N].astype(jnp.float32).reshape(blocks, block_len, G, N)
    c_all = bconv[:, :, N:].astype(jnp.float32).reshape(blocks, block_len, G, N)
    rate_all = rate.reshape(blocks, block_len, G, per_group)
    step_all = step_size.reshape(blocks, block_len, G, per_group)
    start = init_state.reshape(G, per_group, P_SIZE, N)
    final_state, outputs = lax.scan(block_step, start, (x_all, b_all, c_all, rate_all, step_all))
    skipped = head_params[2].reshape(G, per_group)[None, None, :, :, None] * x_all
    y_val = (outputs + skipped).reshape(TOKENS, G, per_group * P_SIZE)
    gate = zx_val[:, 0].astype(jnp.float32).reshape(TOKENS, G, per_group * P_SIZE)
    gated = y_val * jax.nn.silu(gate)
    meansq = lax.optimization_barrier(jnp.mean(gated * gated, axis=-1, keepdims=True))
    mixed = gated * lax.rsqrt(meansq + 1e-05) * norm_gain.reshape(G, per_group * P_SIZE)
    return mixed.reshape(TOKENS, DI).astype(jnp.bfloat16)
```

```python
import jax
import jax.numpy as jnp
from jax import lax
from jax.sharding import PartitionSpec as P

H = 128
P_SIZE = 64
N = 256
G = 8
K = 4
SLOTS = 4


def passed_along(x, axis, by):
    length = lax.axis_size(axis)
    pairs = [(i, i + by) for i in range(length) if 0 <= i + by < length]
    return lax.ppermute(x, axis, pairs)


def swapped(x, axis, by):
    length = lax.axis_size(axis)
    return lax.ppermute(x, axis, [(i, i ^ by) for i in range(length)])


def block_rows(values, index, size, axis):
    return lax.dynamic_slice_in_dim(values, index * size, size, axis)


def conv_silu(values, before, taps):
    length = values.shape[0]
    padded = jnp.concatenate([before, values], 0).astype(jnp.float32)
    summed = taps[K]
    for tap_index in range(K):
        summed = summed + taps[tap_index] * padded[tap_index : tap_index + length]
    return jax.nn.silu(summed).astype(jnp.bfloat16)


def pick_group(values, group_index, axis_index):
    return lax.dynamic_index_in_dim(values, group_index, axis_index, keepdims=False)


def dot32(a, b):
    return jnp.dot(a, b, preferred_element_type=jnp.float32)


def scattered_sum(rows_by_offset, weights, bits):
    n = len(rows_by_offset)
    sent = [j for j in range(n) if j & bits[0]]
    kept = [j for j in range(n) if not j & bits[0]]
    size = rows_by_offset[0].shape[0]
    out = dot32(jnp.concatenate([rows_by_offset[j] for j in sent], 0), weights).astype(jnp.bfloat16)
    own = dot32(jnp.concatenate([rows_by_offset[j] for j in kept], 0), weights)
    got = swapped(out, "ctx", bits[0])
    total = own + got.astype(jnp.float32)
    for bit in bits[1:]:
        gone = [i for i, j in enumerate(kept) if j & bit]
        stay = [i for i, j in enumerate(kept) if not j & bit]
        parts = [total[i * size : (i + 1) * size] for i in range(len(kept))]
        out = jnp.concatenate([parts[i] for i in gone], 0).astype(jnp.bfloat16)
        total = jnp.concatenate([parts[i] for i in stay], 0) + swapped(out, "ctx", bit).astype(jnp.float32)
        kept = [kept[i] for i in stay]
    return total


def body(
    tokens,
    w_zx,
    zx_scale,
    w_bc,
    bc_scale,
    w_dt,
    conv_x,
    conv_bc,
    tail_x,
    tail_bc,
    head_params,
    init_state,
    norm_gain,
):
    bf16 = jnp.bfloat16
    tok_rows = tokens.shape[0]
    depth = w_zx.shape[0]
    local_heads = head_params.shape[1]
    channels = local_heads * P_SIZE
    per_group = H // G
    n_ctx = lax.axis_size("ctx")
    me = lax.axis_index("ctx")
    head_place = lax.axis_index("head")
    group_index = head_place * local_heads // per_group
    bc_rows = pick_group(w_bc, group_index, 1)
    bc_scales = pick_group(bc_scale, group_index, 0)
    bc_taps = pick_group(conv_bc, group_index, 1)
    bc_tail = pick_group(tail_bc, group_index, 1)
    bits = [1 << i for i in range(n_ctx.bit_length() - 1)]

    dt_t = w_dt.T
    step_sum = dot32(block_rows(tokens, me, depth, 1), dt_t.T)
    for j in range(1, n_ctx):
        step_sum = step_sum + dot32(block_rows(tokens, me ^ j, depth, 1), swapped(dt_t, "ctx", j).T)

    part = tok_rows // SLOTS
    slot = head_place % SLOTS
    fetched = [
        swapped(
            lax.dynamic_slice(tokens, (slot * part, (me ^ j) * depth), (part, depth)), "ctx", j
        )
        for j in range(1, n_ctx)
    ]
    fetched = jnp.concatenate(fetched, 0)
    from_core = swapped(fetched, "head", 1)
    from_chip = swapped(fetched, "head", 2)
    from_both = swapped(from_chip, "head", 1)
    own_rows = block_rows(tokens, me, depth, 1)
    first_w = jnp.concatenate([w_zx[:, 1], bc_rows], 1)
    gate_w = w_zx[:, 0]
    firsts, gates = [], []
    for k, arrived in enumerate((fetched, from_core, from_chip, from_both)):
        rows = [block_rows(own_rows, slot ^ k, part, 0)]
        rows += [arrived[i * part : (i + 1) * part] for i in range(n_ctx - 1)]
        order = bits if k in (0, 3) else bits[::-1]
        firsts.append(scattered_sum(rows, first_w, order))
        gates.append(scattered_sum(rows, gate_w, order))

    def in_order(pieces, scale):
        whole = jnp.zeros((tok_rows, pieces[0].shape[1]), bf16)
        for k, piece in enumerate(pieces):
            whole = lax.dynamic_update_slice(
                whole, (piece * scale).astype(bf16), ((slot ^ k) * part, 0)
            )
        return whole

    first_val = in_order(firsts, jnp.concatenate([zx_scale[1], bc_scales], 0))
    gate = in_order(gates, zx_scale[0])
    step_size = jax.nn.softplus(step_sum + head_params[0])
    arrived = passed_along(first_val[tok_rows - (K - 1) :], "ctx", 1)
    previous = jnp.concatenate([tail_x, bc_tail], 1)
    arrived = jnp.where(me == 0, previous, arrived)
    conved = conv_silu(first_val, arrived, jnp.concatenate([conv_x, bc_taps], 1))
    xconv = conved[:, :channels]
    b_part = conved[:, channels : channels + N]
    c_part = conved[:, channels + N :]
    x_heads = xconv.reshape(tok_rows, local_heads, P_SIZE)
    rate = -jnp.exp(head_params[1]) * step_size
    cumul = jnp.cumsum(rate, 0)
    cumul_t = cumul.T
    log_total = cumul[tok_rows - 1]
    logs = lax.all_gather(log_total, "ctx")
    order = jnp.arange(tok_rows)
    lower = order[:, None] >= order[None, :]
    spread = cumul_t[:, :, None] - cumul_t[:, None, :]
    decay = jnp.where(lower[None], jnp.exp(jnp.minimum(spread, 0.0)), 0.0)
    scores = dot32(c_part, b_part.T)
    weights = (decay * scores[None] * step_size.T[:, None, :]).astype(bf16)
    inner = jnp.einsum("hts,shp->thp", weights, x_heads, preferred_element_type=jnp.float32)
    fade = jnp.exp(log_total[None, :] - cumul) * step_size
    faded = (fade[:, :, None] * x_heads.astype(jnp.float32)).astype(bf16)
    local_state = jnp.einsum("shp,sn->hpn", faded, b_part, preferred_element_type=jnp.float32)
    sent_state = local_state.astype(bf16)
    places = jnp.arange(n_ctx)
    incoming = jnp.exp(jnp.sum(jnp.where((places < me)[:, None], logs, 0.0), 0))[:, None, None] * init_state
    for j in range(1, n_ctx):
        between = (places < me) & (places > me - j)
        fall = jnp.exp(jnp.sum(jnp.where(between[:, None], logs, 0.0), 0))
        fall = jnp.where(me >= j, fall, 0.0)
        incoming = incoming + fall[:, None, None] * passed_along(sent_state, "ctx", j).astype(jnp.float32)
    carried = jnp.einsum(
        "tn,hpn->thp", c_part, incoming.astype(bf16), preferred_element_type=jnp.float32
    ) * jnp.exp(cumul)[:, :, None]
    y_val = inner + carried + head_params[2][None, :, None] * x_heads.astype(jnp.float32)
    gated = y_val.reshape(tok_rows, channels) * jax.nn.silu(gate.astype(jnp.float32))
    squares = jnp.sum(gated * gated, axis=1)
    if local_heads >= per_group:
        totals = squares
    else:
        slot_hits = (jnp.arange(G) == group_index).astype(jnp.float32)
        group_sums = lax.psum(slot_hits[:, None] * squares[None, :], "head")
        totals = lax.dynamic_index_in_dim(group_sums, group_index, 0, keepdims=False)
    meansq = totals / (per_group * P_SIZE)
    mixed = gated * lax.rsqrt(meansq + 1e-05)[:, None] * norm_gain
    return mixed.astype(bf16)


def solution(mesh):
    return jax.shard_map(
        body,
        mesh=mesh,
        in_specs=(
            P("ctx", None),
            P("ctx", None, "head"),
            P(None, "head"),
            P("ctx", None, None),
            P(),
            P("ctx", "head"),
            P(None, "head"),
            P(),
            P(None, "head"),
            P(),
            P(None, "head"),
            P("head", None, None),
            P("head"),
        ),
        out_specs=P("ctx", "head"),
        check_vma=False,
    )
```

```python
import functools
import jax
import jax.numpy as jnp
from jax import lax
from jax.experimental import pallas as pl
from jax.experimental.pallas import tpu as pltpu
from jax.sharding import PartitionSpec as P

H = 128
P_SIZE = 64
N = 256
G = 8
K = 4
SLOTS = 4
LANES = 128
EDGE = 8
TILE = 512
MIB = 1 << 20
BF16 = jnp.bfloat16
F32 = jnp.float32
VMEM = pl.BlockSpec(memory_space=pltpu.VMEM)
SMEM = pl.BlockSpec(memory_space=pltpu.SMEM)
ANY = pl.BlockSpec(memory_space=pl.ANY)


def shape_of(shape, dtype):
    return jax.ShapeDtypeStruct(shape, dtype)


def params(mib):
    return pltpu.CompilerParams(vmem_limit_bytes=mib * MIB)


def passed_along(x, axis, by):
    length = lax.axis_size(axis)
    pairs = [(i, i + by) for i in range(length) if 0 <= i + by < length]
    return lax.ppermute(x, axis, pairs)


def swapped(x, axis, by):
    length = lax.axis_size(axis)
    return lax.ppermute(x, axis, [(i, i ^ by) for i in range(length)])


def pick_group(values, group_index, axis_index):
    return lax.dynamic_index_in_dim(values, group_index, axis_index, keepdims=False)


def dot32(a, b):
    return jnp.dot(a, b, preferred_element_type=F32)


def silu(v):
    return v / (1.0 + jnp.exp(-v))


def sent_kernel(count, main_tiles, *refs):
    rows, (w_ref, side_ref), out_ref = refs[:count], refs[count : count + 2], refs[-1]
    tile = pl.program_id(0)

    def product(weights):
        x = jnp.concatenate([r[...] for r in rows], 0)
        out_ref[...] = dot32(x, weights[...]).astype(BF16)

    pl.when(tile < main_tiles)(lambda: product(w_ref))
    pl.when(tile >= main_tiles)(lambda: product(side_ref))


def weight_specs(depth, first_tile, main_tiles):
    return [
        pl.BlockSpec((depth, TILE), lambda i, *_: (0, first_tile + jnp.minimum(i, main_tiles - 1))),
        pl.BlockSpec((depth, TILE), lambda i, *_: (0, 0)),
    ]


def sent_product(rows, w_all, side, first_tile, tiles, after):
    depth = w_all.shape[0]
    part = rows[0].shape[0]
    main_tiles = tiles[0]
    total = sum(tiles)
    return pl.pallas_call(
        functools.partial(sent_kernel, len(rows), main_tiles),
        grid=(total,),
        in_specs=[pl.BlockSpec((part, depth), lambda i: (0, 0))] * len(rows)
        + weight_specs(depth, first_tile, main_tiles)
        + [ANY] * len(after),
        out_specs=pl.BlockSpec((part * len(rows), TILE), lambda i: (0, i)),
        out_shape=shape_of((part * len(rows), TILE * total), BF16),
        compiler_params=params(32),
    )(*rows, w_all, side, *after)


def kept_kernel(count, main_tiles, stay, gone, place_ref, *refs):
    rows, (w_ref, side_ref, got_ref) = refs[:count], refs[count : count + 3]
    stay_ref, gone_ref = refs[-2:]
    tile = pl.program_id(0)
    part = rows[0].shape[0]

    def product(weights):
        x = jnp.concatenate([r[...] for r in rows], 0)
        total = dot32(x, weights[...]) + got_ref[...].astype(F32)
        for to, i in enumerate(stay):
            stay_ref[to * part : (to + 1) * part] = total[i * part : (i + 1) * part]
        for to, i in enumerate(gone):
            gone_ref[to * part : (to + 1) * part] = total[i * part : (i + 1) * part].astype(BF16)

    pl.when(tile < main_tiles)(lambda: product(w_ref))
    pl.when(tile >= main_tiles)(lambda: product(side_ref))


def kept_product(place, tokens, rows, w_all, side, got, first_tile, tiles, stay, gone):
    depth = w_all.shape[0]
    part = tokens.shape[0] // SLOTS
    main_tiles = tiles[0]
    total = sum(tiles)
    count = len(rows) + 1
    return pl.pallas_call(
        functools.partial(kept_kernel, count, main_tiles, stay, gone),
        grid_spec=pltpu.PrefetchScalarGridSpec(
            num_scalar_prefetch=1,
            grid=(total,),
            in_specs=[pl.BlockSpec((part, depth), lambda i, place: (place[0], place[1]))]
            + [pl.BlockSpec((part, depth), lambda i, place: (0, 0))] * len(rows)
            + weight_specs(depth, first_tile, main_tiles)
            + [pl.BlockSpec((part * count, TILE), lambda i, place: (0, i))],
            out_specs=[
                pl.BlockSpec((part * len(stay), TILE), lambda i, place: (0, i)),
                pl.BlockSpec((part * len(gone), TILE), lambda i, place: (0, i)),
            ],
        ),
        out_shape=[
            shape_of((part * len(stay), TILE * total), F32),
            shape_of((part * len(gone), TILE * total), BF16),
        ],
        compiler_params=params(32),
    )(place, tokens, *rows, w_all, side, got)


class Reduction:
    def __init__(self, rows, bits, first_tile, tiles, w_all, side):
        self.rows, self.bits, self.first_tile, self.tiles = rows, bits, first_tile, tiles
        self.w_all, self.side = w_all, side
        self.n = len(rows) + 1

    def send(self, after=()):
        sent = [j for j in range(self.n) if j & self.bits[0]]
        self.sent = sent_product(
            [self.rows[j] for j in sent], self.w_all, self.side, self.first_tile, self.tiles, after
        )
        self.got = swapped(self.sent, "ctx", self.bits[0])

    def keep(self, place, tokens):
        kept = [j for j in range(self.n) if not j & self.bits[0]]
        bit = self.bits[1]
        gone = [i for i, j in enumerate(kept) if j & bit]
        stay = [i for i, j in enumerate(kept) if not j & bit]
        total, out = kept_product(
            place,
            tokens,
            [self.rows[j] for j in kept[1:]],
            self.w_all,
            self.side,
            self.got,
            self.first_tile,
            self.tiles,
            stay,
            gone,
        )
        self.kept = total
        kept = [kept[i] for i in stay]
        got = swapped(out, "ctx", bit)
        size = total.shape[0] // len(kept)
        for bit in self.bits[2:]:
            total = total + got.astype(F32)
            gone = [i for i, j in enumerate(kept) if j & bit]
            stay = [i for i, j in enumerate(kept) if not j & bit]
            parts = [total[i * size : (i + 1) * size] for i in range(len(kept))]
            out = jnp.concatenate([parts[i] for i in gone], 0).astype(BF16)
            total = jnp.concatenate([parts[i] for i in stay], 0)
            got = swapped(out, "ctx", bit)
            kept = [kept[i] for i in stay]
        self.total, self.last = total, got


def step_kernel(me_ref, tok_ref, w_ref, heads_ref, *refs):
    cum_t_ref, shift_t_ref, cum_ref, fade_ref, log_ref, acc = refs[-6:]
    j = pl.program_id(0)

    @pl.when(j == 0)
    def _():
        acc[...] = jnp.zeros_like(acc)

    acc[...] += lax.dot_general(
        w_ref[0], tok_ref[...], (((1,), (1,)), ((), ())), preferred_element_type=F32
    )

    @pl.when(j == pl.num_programs(0) - 1)
    def _():
        v = acc[...] + heads_ref[:, 0:1]
        step = jnp.maximum(v, 0.0) + jnp.log1p(jnp.exp(-jnp.abs(v)))
        rate = -jnp.exp(heads_ref[:, 1:2]) * step
        rows = rate.shape[1]
        up_to = lax.broadcasted_iota(jnp.int32, (rows, rows), 0) <= lax.broadcasted_iota(
            jnp.int32, (rows, rows), 1
        )
        cum = jnp.dot(
            rate, up_to.astype(F32), precision=lax.Precision.HIGHEST, preferred_element_type=F32
        )
        last = cum[:, rows - 1 : rows]
        cum_t_ref[...] = cum
        shift_t_ref[...] = cum - jnp.log(step)
        cum_ref[...] = cum.T
        fade_ref[...] = (jnp.exp(last - cum) * step).T
        log_ref[...] = jnp.broadcast_to(last, log_ref.shape)


def step_sizes(me, tokens, w_dt_all, heads, after):
    n, local_heads, depth = w_dt_all.shape
    rows = tokens.shape[0]
    return pl.pallas_call(
        step_kernel,
        grid_spec=pltpu.PrefetchScalarGridSpec(
            num_scalar_prefetch=1,
            grid=(n,),
            in_specs=[
                pl.BlockSpec((rows, depth), lambda j, me: (0, me[0] ^ j)),
                pl.BlockSpec((1, local_heads, depth), lambda j, me: (j, 0, 0)),
                pl.BlockSpec((local_heads, 3), lambda j, me: (0, 0)),
            ]
            + [ANY] * len(after),
            out_specs=[
                pl.BlockSpec((local_heads, rows), lambda j, me: (0, 0)),
                pl.BlockSpec((local_heads, rows), lambda j, me: (0, 0)),
                pl.BlockSpec((rows, local_heads), lambda j, me: (0, 0)),
                pl.BlockSpec((rows, local_heads), lambda j, me: (0, 0)),
                pl.BlockSpec((local_heads, LANES), lambda j, me: (0, 0)),
            ],
            scratch_shapes=[pltpu.VMEM((local_heads, rows), F32)],
        ),
        out_shape=[
            shape_of((local_heads, rows), F32),
            shape_of((local_heads, rows), F32),
            shape_of((rows, local_heads), F32),
            shape_of((rows, local_heads), F32),
            shape_of((local_heads, LANES), F32),
        ],
        compiler_params=params(32),
    )(me, tokens, w_dt_all, heads, *after)


def head_spread(local_heads):
    channels = local_heads * P_SIZE
    hit = (
        lax.broadcasted_iota(jnp.int32, (local_heads, channels), 1) // P_SIZE
        == lax.broadcasted_iota(jnp.int32, (local_heads, channels), 0)
    )
    return hit.astype(F32).astype(BF16)


def spread_heads(values, hits):
    high = values.astype(BF16)
    low = (values - high.astype(F32)).astype(BF16)
    return dot32(high, hits) + dot32(low, hits)


def conv_kernel(place_ref, *refs):
    totals, lasts = refs[:SLOTS], refs[SLOTS : 2 * SLOTS]
    edge_ref, scale_ref, taps_ref, fade_ref = refs[2 * SLOTS : 2 * SLOTS + 4]
    conv_ref, state_ref, vals = refs[-3:]
    part, width = totals[0].shape
    rows = part * SLOTS
    channels = width - 2 * N
    slot = place_ref[0]
    vals[:EDGE] = edge_ref[...]
    for k in range(SLOTS):
        start = pl.multiple_of(EDGE + (slot ^ k) * part, EDGE)
        whole = (totals[k][...] + lasts[k][...].astype(F32)) * scale_ref[...]
        vals[pl.ds(start, part)] = whole.astype(BF16).astype(F32)
    for c in range(0, width, 2 * LANES):
        cols = slice(c, c + 2 * LANES)
        for r in range(0, rows, part):
            summed = taps_ref[K : K + 1, cols]
            for tap in range(K):
                at = r + EDGE - (K - 1) + tap
                summed = summed + taps_ref[tap : tap + 1, cols] * vals[at : at + part, cols]
            conv_ref[r : r + part, cols] = silu(summed).astype(BF16)
    hits = head_spread(channels // P_SIZE)
    faded = spread_heads(fade_ref[...], hits) * conv_ref[:, :channels].astype(F32)
    state_ref[...] = lax.dot_general(
        conv_ref[:, channels : channels + N],
        faded.astype(BF16),
        (((0,), (0,)), ((), ())),
        preferred_element_type=F32,
    ).astype(BF16)


def conv_and_state(slot, totals, lasts, edge, scale, taps, fade):
    part, width = totals[0].shape
    rows = part * SLOTS
    return pl.pallas_call(
        conv_kernel,
        in_specs=[SMEM] + [VMEM] * (2 * SLOTS + 4),
        out_specs=[VMEM, VMEM],
        out_shape=[shape_of((rows, width), BF16), shape_of((N, width - 2 * N), BF16)],
        scratch_shapes=[pltpu.VMEM((rows + EDGE, width), F32)],
        compiler_params=params(40),
    )(slot, *totals, *lasts, edge, scale, taps, fade)


def inner_kernel(conv_ref, cum_ref, shift_t_ref, skip_ref, y_ref, scores):
    rows, width = conv_ref.shape
    channels = width - 2 * N
    size = LANES
    blocks = rows // size
    nt = (((1,), (1,)), ((), ()))
    scores[...] = lax.dot_general(
        conv_ref[:, channels + N :], conv_ref[:, channels : channels + N], nt, preferred_element_type=F32
    )
    lower = lax.broadcasted_iota(jnp.int32, (size, size), 0) >= lax.broadcasted_iota(
        jnp.int32, (size, size), 1
    )
    left = lax.broadcasted_iota(jnp.int32, (size, 2 * P_SIZE), 1) < P_SIZE
    for pair in range(channels // (2 * P_SIZE)):
        cols = slice(pair * 2 * P_SIZE, (pair + 1) * 2 * P_SIZE)
        for a in range(blocks):
            t = slice(a * size, (a + 1) * size)
            products = []
            for h in (2 * pair, 2 * pair + 1):
                here = cum_ref[t, h : h + 1]
                own = jnp.where(lower, here - shift_t_ref[h : h + 1, t], -jnp.inf)
                weights = jnp.exp(own) * scores[t, t]
                if a > 0:
                    before = slice(0, a * size)
                    earlier = jnp.exp(here - shift_t_ref[h : h + 1, before]) * scores[t, before]
                    weights = jnp.concatenate([earlier, weights], 1)
                products.append(dot32(weights.astype(BF16), conv_ref[: (a + 1) * size, cols]))
            y_ref[t, cols] = jnp.where(left, products[0], products[1]) + skip_ref[:, cols] * conv_ref[
                t, cols
            ].astype(F32)


def inner_output(conved, cum, shift_t, skip):
    rows, width = conved.shape
    channels = width - 2 * N
    return pl.pallas_call(
        inner_kernel,
        in_specs=[VMEM] * 4,
        out_specs=VMEM,
        out_shape=shape_of((rows, channels), F32),
        scratch_shapes=[pltpu.VMEM((rows, rows), F32)],
        compiler_params=params(32),
    )(conved, cum, shift_t, skip)


def final_kernel(whole_group, place_ref, *refs):
    totals, lasts = refs[:SLOTS], refs[SLOTS : 2 * SLOTS]
    y_ref, c_ref, state_ref, cum_ref, scale_ref, gain_ref = refs[2 * SLOTS : 2 * SLOTS + 6]
    outs = refs[2 * SLOTS + 6 :]
    part, channels = totals[0].shape
    slot = place_ref[0]
    hits = head_spread(channels // P_SIZE)
    for k in range(SLOTS):
        at = pl.ds(pl.multiple_of((slot ^ k) * part, part), part)
        carried = dot32(c_ref[at], state_ref[...])
        y = y_ref[at] + carried * spread_heads(jnp.exp(cum_ref[at]), hits)
        gate = ((totals[k][...] + lasts[k][...].astype(F32)) * scale_ref[...]).astype(BF16).astype(F32)
        gated = y * silu(gate)
        squares = jnp.sum(gated * gated, axis=1, keepdims=True)
        if whole_group:
            meansq = squares / (H // G * P_SIZE)
            outs[0][at] = (gated * lax.rsqrt(meansq + 1e-05) * gain_ref[...]).astype(BF16)
        else:
            outs[0][at] = gated
            outs[1][at] = jnp.broadcast_to(squares, (part, LANES))


def final_output(whole_group, slot, totals, lasts, y, c_part, state, cum, scale, gain):
    rows, channels = y.shape
    if whole_group:
        outs = [shape_of((rows, channels), BF16)]
    else:
        outs = [shape_of((rows, channels), F32), shape_of((rows, LANES), F32)]
    return pl.pallas_call(
        functools.partial(final_kernel, whole_group),
        in_specs=[SMEM] + [VMEM] * (2 * SLOTS + 6),
        out_specs=[VMEM] * len(outs),
        out_shape=outs,
        compiler_params=params(40),
    )(slot, *totals, *lasts, y, c_part, state, cum, scale, gain)


def body(
    tokens,
    w_zx,
    zx_scale,
    w_bc,
    bc_scale,
    w_dt,
    conv_x,
    conv_bc,
    tail_x,
    tail_bc,
    head_params,
    init_state,
    norm_gain,
):
    tok_rows = tokens.shape[0]
    depth = w_zx.shape[0]
    local_heads = head_params.shape[1]
    channels = local_heads * P_SIZE
    per_group = H // G
    n_ctx = lax.axis_size("ctx")
    me = lax.axis_index("ctx")
    head_place = lax.axis_index("head")
    group_index = head_place * local_heads // per_group
    bits = [1 << i for i in range(n_ctx.bit_length() - 1)]
    part = tok_rows // SLOTS
    slot = head_place % SLOTS
    slot_ref = slot[None].astype(jnp.int32)

    fetched = [None] + [
        swapped(lax.dynamic_slice(tokens, (slot * part, (me ^ j) * depth), (part, depth)), "ctx", j)
        for j in range(1, n_ctx)
    ]
    from_core = [None] + [swapped(a, "head", 1) for a in fetched[1:]]
    from_chip = [None] + [swapped(a, "head", 2) for a in fetched[1:]]
    from_both = [None] + [swapped(a, "head", 1) for a in from_chip[1:]]
    quarters = (fetched, from_core, from_chip, from_both)

    w_all = w_zx.reshape(depth, 2 * channels)
    bc_rows = pick_group(w_bc, group_index, 1)
    main = channels // TILE
    firsts, gates = [], []
    for k, rows in enumerate(quarters):
        order = bits if k in (0, 3) else bits[::-1]
        rows = dict(enumerate(rows))
        rows.pop(0)
        firsts.append(Reduction(rows, order, main, (main, 2 * N // TILE), w_all, bc_rows))
        gates.append(Reduction(rows, order, 0, (main, 0), w_all, bc_rows))
    places = [jnp.stack([slot ^ k, me]).astype(jnp.int32) for k in range(SLOTS)]
    firsts[0].send()
    firsts[1].send(after=(firsts[0].sent,))

    dt_t = w_dt.T
    w_dt_all = jnp.stack([dt_t] + [swapped(dt_t, "ctx", j) for j in range(1, n_ctx)])
    cum_t, shift_t, cum, fade, logs = step_sizes(
        me[None].astype(jnp.int32), tokens, w_dt_all, head_params.T, (firsts[1].sent,)
    )

    firsts[0].keep(places[0], tokens)
    gates[0].send(after=(firsts[0].kept,))
    firsts[1].keep(places[1], tokens)
    gates[1].send(after=(firsts[1].kept,))
    firsts[2].send(after=(firsts[0].kept,))
    firsts[3].send(after=(firsts[1].kept,))
    gates[0].keep(places[0], tokens)
    gates[1].keep(places[1], tokens)
    firsts[2].keep(places[2], tokens)
    firsts[3].keep(places[3], tokens)
    gates[2].send(after=(firsts[2].kept,))
    gates[3].send(after=(firsts[3].kept,))
    gates[2].keep(places[2], tokens)
    gates[3].keep(places[3], tokens)

    scale = jnp.concatenate([zx_scale[1], pick_group(bc_scale, group_index, 0)], 0)[None]
    taps = jnp.concatenate([conv_x, pick_group(conv_bc, group_index, 1)], 1)
    edge = jnp.zeros((K - 1, scale.shape[1]), F32)
    for k, one in enumerate(firsts):
        rows = one.total[part - (K - 1) :] + one.last[part - (K - 1) :].astype(F32)
        edge = jnp.where((slot ^ k) == SLOTS - 1, rows, edge)
    arrived = passed_along((edge * scale).astype(BF16), "ctx", 1)
    previous = jnp.concatenate([tail_x, pick_group(tail_bc, group_index, 1)], 1)
    arrived = jnp.where(me == 0, previous, arrived).astype(F32)
    arrived = jnp.concatenate([jnp.zeros((EDGE - (K - 1), arrived.shape[1]), F32), arrived], 0)
    conved, local_state = conv_and_state(
        slot_ref, [f.total for f in firsts], [f.last for f in firsts], arrived, scale, taps, fade
    )
    y_local = inner_output(conved, cum, shift_t, jnp.repeat(head_params[2], P_SIZE)[None])

    log_total = logs[:, 0]
    log_by = [log_total] + [swapped(log_total, "ctx", j) for j in range(1, n_ctx)]

    def fall(offsets, only_before):
        total = jnp.zeros_like(log_total)
        for j in offsets:
            total = total + (jnp.where((me ^ j) < me, log_by[j], 0.0) if only_before else log_by[j])
        return jnp.repeat(jnp.exp(total), P_SIZE)[None]

    init_t = init_state.reshape(channels, N).T
    incoming = fall(range(1, n_ctx), True) * init_t
    run = local_state
    for bit in bits:
        later = (me & bit) > 0
        if bit == bits[-1]:
            got = passed_along(run, "ctx", bit).astype(F32)
        else:
            got = swapped(run, "ctx", bit).astype(F32)
        incoming = incoming + jnp.where(later, fall(range(1, bit), True) * got, 0.0)
        if bit != bits[-1]:
            own_fall, got_fall = fall(range(bit), False), fall(range(bit, 2 * bit), False)
            run = jnp.where(
                later, own_fall * got + run.astype(F32), got_fall * run.astype(F32) + got
            ).astype(BF16)

    whole_group = local_heads >= per_group
    outs = final_output(
        whole_group,
        slot_ref,
        [g.total for g in gates],
        [g.last for g in gates],
        y_local,
        conved[:, channels + N :],
        incoming.astype(BF16),
        cum,
        zx_scale[0:1],
        norm_gain[None],
    )
    if whole_group:
        return outs[0]
    gated, squares = outs
    slot_hits = (jnp.arange(G) == group_index).astype(F32)
    group_sums = lax.psum(slot_hits[:, None] * squares[:, 0][None, :], "head")
    totals = lax.dynamic_index_in_dim(group_sums, group_index, 0, keepdims=False)
    meansq = totals / (per_group * P_SIZE)
    return (gated * lax.rsqrt(meansq + 1e-05)[:, None] * norm_gain).astype(BF16)


def solution(mesh):
    return jax.shard_map(
        body,
        mesh=mesh,
        in_specs=(
            P("ctx", None),
            P("ctx", None, "head"),
            P(None, "head"),
            P("ctx", None, None),
            P(),
            P("ctx", "head"),
            P(None, "head"),
            P(),
            P(None, "head"),
            P(),
            P(None, "head"),
            P("head", None, None),
            P("head"),
        ),
        out_specs=P("ctx", "head"),
        check_vma=False,
    )
```

```python
import functools
import jax
import jax.numpy as jnp
from jax import lax
from jax.experimental import pallas as pl
from jax.experimental.pallas import tpu as pltpu
from jax.sharding import PartitionSpec as P

H = 128
P_SIZE = 64
N = 256
G = 8
K = 4
SLOTS = 4
LANES = 128
EDGE = 8
LOG_ROWS = 16
LOG_PARTS = 3
EARLY = 2
TILE = 512
MIB = 1 << 20
VMEM_MIB = 58
SCALE = 64
BF16 = jnp.bfloat16
F32 = jnp.float32
VMEM = pl.BlockSpec(memory_space=pltpu.VMEM)
SMEM = pl.BlockSpec(memory_space=pltpu.SMEM)
ANY = pl.BlockSpec(memory_space=pl.ANY)


def shape_of(shape, dtype):
    return jax.ShapeDtypeStruct(shape, dtype)


def params():
    return pltpu.CompilerParams(vmem_limit_bytes=VMEM_MIB * MIB)


def cost(flops, moved, transcendentals=0):
    return pl.CostEstimate(
        flops=int(flops) // SCALE, bytes_accessed=int(moved) // SCALE, transcendentals=int(transcendentals) // SCALE
    )


def chained(values, after):
    return lax.optimization_barrier((*values, after))[: len(values)]


def passed_along(x, axis, by):
    length = lax.axis_size(axis)
    pairs = [(i, i + by) for i in range(length) if 0 <= i + by < length]
    return lax.ppermute(x, axis, pairs)


def swapped(x, axis, by):
    length = lax.axis_size(axis)
    return lax.ppermute(x, axis, [(i, i ^ by) for i in range(length)])


def pick_group(values, group_index, axis_index):
    return lax.dynamic_index_in_dim(values, group_index, axis_index, keepdims=False)


def dot32(a, b):
    return jnp.dot(a, b, preferred_element_type=F32)


def silu(v):
    return v / (1.0 + jnp.exp(-v))


def copy_all(pairs, sems):
    copies = [pltpu.make_async_copy(src, dst, sems.at[i]) for i, (src, dst) in enumerate(pairs)]
    for one in copies:
        one.start()
    for one in copies:
        one.wait()


def pack_kernel(place_ref, tok_ref, dt_ref, *refs):
    outs, sems = refs[:-1], refs[-1]
    local_heads, depth = dt_ref.shape
    part = outs[0].shape[0] - local_heads
    rows = pl.ds(pl.multiple_of(place_ref[0] * part, part), part)
    pairs = []
    for j, out in enumerate(outs, 1):
        cols = pl.ds(pl.multiple_of((place_ref[1] ^ j) * depth, depth), depth)
        pairs.append((tok_ref.at[rows, cols], out.at[:part]))
        pairs.append((dt_ref, out.at[part:]))
    copy_all(pairs, sems)


def pack(place, tokens, dt_t, n):
    local_heads, depth = dt_t.shape
    part = tokens.shape[0] // SLOTS
    return pl.pallas_call(
        pack_kernel,
        in_specs=[SMEM, ANY, ANY],
        out_specs=[ANY] * (n - 1),
        out_shape=[shape_of((part + local_heads, depth), BF16)] * (n - 1),
        scratch_shapes=[pltpu.SemaphoreType.DMA((2 * (n - 1),))],
        name="pack",
        compiler_params=params(),
    )(place, tokens, dt_t)


def join_kernel(part, count, *refs):
    blocks, out, sems = refs[:count], refs[-2], refs[-1]
    copy_all([(b.at[:part], out.at[i * part : (i + 1) * part]) for i, b in enumerate(blocks)], sems)


def join(blocks, part, after):
    depth = blocks[0].shape[1]
    return pl.pallas_call(
        functools.partial(join_kernel, part, len(blocks)),
        in_specs=[ANY] * (len(blocks) + len(after)),
        out_specs=ANY,
        out_shape=shape_of((part * len(blocks), depth), BF16),
        scratch_shapes=[pltpu.SemaphoreType.DMA((len(blocks),))],
        name="join",
        compiler_params=params(),
    )(*blocks, *after)


def sent_kernel(counts, main_tiles, *refs):
    total = sum(counts)
    rows, (w_ref, side_ref), outs = refs[:total], refs[total : total + 2], refs[-len(counts) :]
    tile = pl.program_id(0)

    def product(weights):
        x = jnp.concatenate([r[...] for r in rows], 0)
        result = dot32(x, weights[...]).astype(BF16)
        at = 0
        for out in outs:
            out[...] = result[at : at + out.shape[0]]
            at += out.shape[0]

    pl.when(tile < main_tiles)(lambda: product(w_ref))
    pl.when(tile >= main_tiles)(lambda: product(side_ref))


def weight_specs(depth, first_tile, main_tiles):
    return [
        pl.BlockSpec((depth, TILE), lambda i, *_: (0, first_tile + jnp.minimum(i, main_tiles - 1))),
        pl.BlockSpec((depth, TILE), lambda i, *_: (0, jnp.maximum(i - main_tiles, 0))),
    ]


def block_spec(part, depth, block):
    return pl.BlockSpec((part, depth), lambda i, *_: (block, 0))


def sent_product(name, part, rows, w_all, side, first_tile, tiles, after):
    depth = w_all.shape[0]
    main_tiles, total = tiles[0], sum(tiles)
    counts = [len(r) for r in rows]
    flat = [one for r in rows for one in r]
    return pl.pallas_call(
        functools.partial(sent_kernel, counts, main_tiles),
        grid=(total,),
        in_specs=[block_spec(part, depth, block) for _, block in flat]
        + weight_specs(depth, first_tile, main_tiles)
        + [ANY] * len(after),
        out_specs=[pl.BlockSpec((part * count, TILE), lambda i: (0, i)) for count in counts],
        out_shape=[shape_of((part * count, TILE * total), BF16) for count in counts],
        cost_estimate=cost(
            2 * part * len(flat) * depth * TILE * total, 2 * depth * (TILE * total + part * len(flat))
        ),
        name=name,
        compiler_params=params(),
    )(*[array for array, _ in flat], w_all, side, *after)


def kept_kernel(counts, main_tiles, stays, gones, place_ref, *refs):
    total, quarters = sum(counts), len(counts)
    rows, (w_ref, side_ref) = refs[:total], refs[total : total + 2]
    gots, outs = refs[total + 2 : total + 2 + quarters], refs[-2 * quarters :]
    tile = pl.program_id(0)
    part = rows[0].shape[0]

    def product(weights):
        x = jnp.concatenate([r[...] for r in rows], 0)
        result = dot32(x, weights[...])
        at = 0
        for q in range(quarters):
            whole = result[at : at + counts[q] * part] + gots[q][...].astype(F32)
            at += counts[q] * part
            for to, i in enumerate(stays[q]):
                outs[2 * q][to * part : (to + 1) * part] = whole[i * part : (i + 1) * part]
            for to, i in enumerate(gones[q]):
                outs[2 * q + 1][to * part : (to + 1) * part] = whole[i * part : (i + 1) * part].astype(BF16)

    pl.when(tile < main_tiles)(lambda: product(w_ref))
    pl.when(tile >= main_tiles)(lambda: product(side_ref))


def kept_product(name, part, place, tokens, rows, w_all, side, gots, first_tile, tiles, stays, gones, after):
    depth = w_all.shape[0]
    main_tiles, total = tiles[0], sum(tiles)
    counts = [len(r) + 1 for r in rows]
    arrays, specs, out_specs, out_shapes = [], [], [], []
    for q, quarter in enumerate(rows):
        arrays.append(tokens)
        specs.append(pl.BlockSpec((part, depth), lambda i, place, q=q: (place[1 + q], place[0])))
        for array, block in quarter:
            arrays.append(array)
            specs.append(block_spec(part, depth, block))
        for count, dtype in ((len(stays[q]), F32), (len(gones[q]), BF16)):
            out_specs.append(pl.BlockSpec((part * count, TILE), lambda i, place: (0, i)))
            out_shapes.append(shape_of((part * count, TILE * total), dtype))
    height = part * sum(counts)
    return pl.pallas_call(
        functools.partial(kept_kernel, counts, main_tiles, stays, gones),
        grid_spec=pltpu.PrefetchScalarGridSpec(
            num_scalar_prefetch=1,
            grid=(total,),
            in_specs=specs
            + weight_specs(depth, first_tile, main_tiles)
            + [pl.BlockSpec((part * count, TILE), lambda i, place: (0, i)) for count in counts]
            + [ANY] * len(after),
            out_specs=out_specs,
        ),
        out_shape=out_shapes,
        cost_estimate=cost(
            2 * height * depth * TILE * total, 2 * depth * (TILE * total + height) + 6 * height * TILE * total
        ),
        name=name,
        compiler_params=params(),
    )(place, *arrays, w_all, side, *gots, *after)


class Reduction:
    def __init__(self, name, part, quarters, first_tile, tiles, w_all, side):
        self.name, self.part, self.quarters = name, part, quarters
        self.first_tile, self.tiles = first_tile, tiles
        self.w_all, self.side = w_all, side
        self.n = len(quarters[0][1]) + 1

    def send(self, after):
        rows = [
            [blocks[j] for j in range(self.n) if j & order[0]] for _, blocks, order in self.quarters
        ]
        outs = sent_product(
            "sent_" + self.name, self.part, rows, self.w_all, self.side, self.first_tile, self.tiles, (after,)
        )
        self.gots = [swapped(out, "ctx", q[2][0]) for out, q in zip(outs, self.quarters)]
        return outs[0]

    def keep(self, slot, me, tokens, after):
        place = jnp.stack([me] + [slot ^ q[0] for q in self.quarters]).astype(jnp.int32)
        kept = [[j for j in range(self.n) if not j & order[0]] for _, _, order in self.quarters]
        gones = [[i for i, j in enumerate(k) if j & q[2][1]] for k, q in zip(kept, self.quarters)]
        stays = [[i for i, j in enumerate(k) if not j & q[2][1]] for k, q in zip(kept, self.quarters)]
        outs = kept_product(
            "kept_" + self.name,
            self.part,
            place,
            tokens,
            [[q[1][j] for j in k[1:]] for k, q in zip(kept, self.quarters)],
            self.w_all,
            self.side,
            self.gots,
            self.first_tile,
            self.tiles,
            stays,
            gones,
            (after,),
        )
        self.totals, self.lasts = [], []
        size = self.part
        for at, (k, stay, (_, _, order)) in enumerate(zip(kept, stays, self.quarters)):
            total, out = outs[2 * at : 2 * at + 2]
            k = [k[i] for i in stay]
            got = swapped(out, "ctx", order[1])
            for bit in order[2:]:
                total = total + got.astype(F32)
                gone = [i for i, j in enumerate(k) if j & bit]
                stay = [i for i, j in enumerate(k) if not j & bit]
                parts = [total[i * size : (i + 1) * size] for i in range(len(k))]
                out = jnp.concatenate([parts[i] for i in gone], 0).astype(BF16)
                total = jnp.concatenate([parts[i] for i in stay], 0)
                got = swapped(out, "ctx", bit)
                k = [k[i] for i in stay]
            self.totals.append(total)
            self.lasts.append(got)
        return outs[1]


def finished(total, last, scale):
    return ((total + last.astype(F32)) * scale).astype(BF16)


def finish_kernel(count, *refs):
    totals, lasts, scale_ref, outs = refs[:count], refs[count : 2 * count], refs[2 * count], refs[-count:]
    for total, last, out in zip(totals, lasts, outs):
        out[...] = finished(total[...], last[...], scale_ref[...])


def finish(name, totals, lasts, scale, after):
    count = len(totals)
    return pl.pallas_call(
        functools.partial(finish_kernel, count),
        in_specs=[VMEM] * (2 * count + 1) + [ANY] * len(after),
        out_specs=[VMEM] * count,
        out_shape=[shape_of(t.shape, BF16) for t in totals],
        cost_estimate=cost(4 * count * totals[0].size, 8 * count * totals[0].size),
        name=name,
        compiler_params=params(),
    )(*totals, *lasts, scale, *after)


def quarter_values(values, totals, lasts, scale):
    early = [v[...] for v in values]
    return early + [finished(t[...], l[...], scale) for t, l in zip(totals, lasts)]


def step_kernel(n, me_ref, tok_ref, *refs):
    weights, heads_ref = refs[:n], refs[n]
    shift_t_ref, cum_ref, fade_ref, log_ref, acc = refs[-5:]
    j = pl.program_id(0)

    @pl.when(j == 0)
    def _():
        acc[...] = jnp.zeros_like(acc)

    for i in range(n):

        @pl.when(j == i)
        def _():
            acc[...] += lax.dot_general(
                weights[i][...], tok_ref[...], (((1,), (1,)), ((), ())), preferred_element_type=F32
            )

    @pl.when(j == pl.num_programs(0) - 1)
    def _():
        v = acc[...] + heads_ref[:, 0:1]
        step = jnp.maximum(v, 0.0) + jnp.log1p(jnp.exp(-jnp.abs(v)))
        rate = -jnp.exp(heads_ref[:, 1:2]) * step
        rows = rate.shape[1]
        up_to = lax.broadcasted_iota(jnp.int32, (rows, rows), 0) <= lax.broadcasted_iota(
            jnp.int32, (rows, rows), 1
        )
        cum = jnp.dot(
            rate, up_to.astype(F32), precision=lax.Precision.HIGHEST, preferred_element_type=F32
        )
        last = cum[:, rows - 1 : rows]
        shift_t_ref[...] = cum - jnp.log(step)
        cum_ref[...] = cum.T
        fade_ref[...] = (jnp.exp(last - cum) * step).T
        log_ref[...] = jnp.broadcast_to(last.T, log_ref.shape)


def step_sizes(me, tokens, dt_t, payloads, heads, after):
    local_heads, depth = dt_t.shape
    n = len(payloads) + 1
    rows = tokens.shape[0]
    last = payloads[0].shape[0] // local_heads - 1
    whole = lambda shape: pl.BlockSpec(shape, lambda j, me: (0, 0))
    return pl.pallas_call(
        functools.partial(step_kernel, n),
        grid_spec=pltpu.PrefetchScalarGridSpec(
            num_scalar_prefetch=1,
            grid=(n,),
            in_specs=[
                pl.BlockSpec((rows, depth), lambda j, me: (0, me[0] ^ j)),
                whole((local_heads, depth)),
            ]
            + [pl.BlockSpec((local_heads, depth), lambda j, me: (last, 0))] * (n - 1)
            + [whole((local_heads, 3))]
            + [ANY] * len(after),
            out_specs=[
                whole((local_heads, rows)),
                whole((rows, local_heads)),
                whole((rows, local_heads)),
                whole((EDGE, local_heads)),
            ],
            scratch_shapes=[pltpu.VMEM((local_heads, rows), F32)],
        ),
        out_shape=[
            shape_of((local_heads, rows), F32),
            shape_of((rows, local_heads), F32),
            shape_of((rows, local_heads), F32),
            shape_of((EDGE, local_heads), F32),
        ],
        cost_estimate=cost(2 * n * rows * depth * LANES, 2 * n * rows * depth),
        name="steps",
        compiler_params=params(),
    )(me, tokens, dt_t, *payloads, heads, *after)


def write_logs(state_ref, parts):
    rows = lax.broadcasted_iota(jnp.int32, (LOG_ROWS, state_ref.shape[1]), 0)
    block = jnp.zeros((LOG_ROWS, state_ref.shape[1]), F32)
    for i, one in enumerate(parts):
        block = jnp.where(rows == i, one, block)
    state_ref[N:] = block.astype(BF16)


def read_logs(state_ref):
    block = state_ref[N:].astype(F32)
    return sum(block[i : i + 1] for i in range(LOG_PARTS))


def split_logs(logs):
    parts = []
    for _ in range(LOG_PARTS):
        parts.append(logs.astype(BF16).astype(F32))
        logs = logs - parts[-1]
    return parts


def head_spread(local_heads):
    channels = local_heads * P_SIZE
    hit = (
        lax.broadcasted_iota(jnp.int32, (local_heads, channels), 1) // P_SIZE
        == lax.broadcasted_iota(jnp.int32, (local_heads, channels), 0)
    )
    return hit.astype(F32).astype(BF16)


def spread_heads(values, hits):
    high = values.astype(BF16)
    low = (values - high.astype(F32)).astype(BF16)
    return dot32(high, hits) + dot32(low, hits)


def conv_kernel(place_ref, *refs):
    values, totals, lasts = refs[:EARLY], refs[EARLY:SLOTS], refs[SLOTS : 2 * SLOTS - EARLY]
    edge_ref, scale_ref, taps_ref, fade_ref, log_ref = refs[2 * SLOTS - EARLY : 2 * SLOTS - EARLY + 5]
    conv_ref, state_ref, vals = refs[-3:]
    part, width = totals[0].shape
    rows = part * SLOTS
    channels = width - 2 * N
    slot = place_ref[0]
    vals[:EDGE] = edge_ref[...]
    for k, value in enumerate(quarter_values(values, totals, lasts, scale_ref[...])):
        start = pl.multiple_of(EDGE + (slot ^ k) * part, EDGE)
        vals[pl.ds(start, part)] = value.astype(F32)
    for c in range(0, width, 2 * LANES):
        cols = slice(c, c + 2 * LANES)
        for r in range(0, rows, part):
            summed = taps_ref[K : K + 1, cols]
            for tap in range(K):
                at = r + EDGE - (K - 1) + tap
                summed = summed + taps_ref[tap : tap + 1, cols] * vals[at : at + part, cols]
            conv_ref[r : r + part, cols] = silu(summed).astype(BF16)
    hits = head_spread(channels // P_SIZE)
    faded = spread_heads(fade_ref[...], hits) * conv_ref[:, :channels].astype(F32)
    state_ref[:N] = lax.dot_general(
        conv_ref[:, channels : channels + N],
        faded.astype(BF16),
        (((0,), (0,)), ((), ())),
        preferred_element_type=F32,
    ).astype(BF16)
    left, parts = log_ref[...], []
    for _ in range(LOG_PARTS):
        parts.append(left.astype(BF16))
        left = left - parts[-1].astype(F32)
    spread = [dot32(one, hits)[0:1] for one in parts]
    write_logs(state_ref, spread)


def conv_and_state(slot, values, totals, lasts, edge, scale, taps, fade, logs, after):
    part, width = totals[0].shape
    rows = part * SLOTS
    return pl.pallas_call(
        conv_kernel,
        in_specs=[SMEM] + [VMEM] * (2 * SLOTS - EARLY + 5) + [ANY] * len(after),
        out_specs=[VMEM, VMEM],
        out_shape=[shape_of((rows, width), BF16), shape_of((N + LOG_ROWS, width - 2 * N), BF16)],
        scratch_shapes=[pltpu.VMEM((rows + EDGE, width), F32)],
        cost_estimate=cost(30 * rows * width, 12 * rows * width, 2 * rows * width),
        name="conv",
        compiler_params=params(),
    )(slot, *values, *totals, *lasts, edge, scale, taps, fade, logs, *after)


def inner_kernel(conv_ref, cum_ref, shift_t_ref, skip_ref, *refs):
    y_ref, scores = refs[-2:]
    rows, width = conv_ref.shape
    channels = width - 2 * N
    size = LANES
    blocks = rows // size
    nt = (((1,), (1,)), ((), ()))
    scores[...] = lax.dot_general(
        conv_ref[:, channels + N :], conv_ref[:, channels : channels + N], nt, preferred_element_type=F32
    )
    lower = lax.broadcasted_iota(jnp.int32, (size, size), 0) >= lax.broadcasted_iota(
        jnp.int32, (size, size), 1
    )
    left = lax.broadcasted_iota(jnp.int32, (size, 2 * P_SIZE), 1) < P_SIZE
    for pair in range(channels // (2 * P_SIZE)):
        cols = slice(pair * 2 * P_SIZE, (pair + 1) * 2 * P_SIZE)
        for a in range(blocks):
            t = slice(a * size, (a + 1) * size)
            products = []
            for h in (2 * pair, 2 * pair + 1):
                here = cum_ref[t, h : h + 1]
                own = jnp.where(lower, here - shift_t_ref[h : h + 1, t], -jnp.inf)
                weights = jnp.exp(own) * scores[t, t]
                if a > 0:
                    before = slice(0, a * size)
                    earlier = jnp.exp(here - shift_t_ref[h : h + 1, before]) * scores[t, before]
                    weights = jnp.concatenate([earlier, weights], 1)
                products.append(dot32(weights.astype(BF16), conv_ref[: (a + 1) * size, cols]))
            y_ref[t, cols] = jnp.where(left, products[0], products[1]) + skip_ref[:, cols] * conv_ref[
                t, cols
            ].astype(F32)


def inner_output(conved, cum, shift_t, skip, after):
    rows, width = conved.shape
    channels = width - 2 * N
    return pl.pallas_call(
        inner_kernel,
        in_specs=[VMEM] * 4 + [ANY] * len(after),
        out_specs=VMEM,
        out_shape=shape_of((rows, channels), F32),
        scratch_shapes=[pltpu.VMEM((rows, rows), F32)],
        cost_estimate=cost(2 * rows * rows * channels, 8 * rows * width, rows * rows * channels // P_SIZE),
        name="inner",
        compiler_params=params(),
    )(conved, cum, shift_t, skip, *after)


def merge_kernel(later_ref, own_ref, got_ref, *refs):
    out_ref = refs[-1]
    own_log, got_log = read_logs(own_ref), read_logs(got_ref)
    own, got = own_ref[:N].astype(F32), got_ref[:N].astype(F32)
    later = later_ref[0] > 0
    own_fall = jnp.where(later, 1.0, jnp.exp(got_log))
    got_fall = jnp.where(later, jnp.exp(own_log), 1.0)
    out_ref[:N] = (own_fall * own + got_fall * got).astype(BF16)
    write_logs(out_ref, split_logs(own_log + got_log))


def merged(later, own, got, after):
    return pl.pallas_call(
        merge_kernel,
        in_specs=[SMEM, VMEM, VMEM] + [ANY] * len(after),
        out_specs=VMEM,
        out_shape=shape_of(own.shape, BF16),
        cost_estimate=cost(4 * own.size, 6 * own.size),
        name="merge",
        compiler_params=params(),
    )(later, own, got, *after)


def final_kernel(whole_group, rounds, place_ref, *refs):
    values, totals, lasts = refs[:EARLY], refs[EARLY:SLOTS], refs[SLOTS : 2 * SLOTS - EARLY]
    refs = refs[2 * SLOTS - EARLY :]
    gots, refs = refs[:rounds], refs[rounds:]
    y_ref, conv_ref, init_ref, cum_ref, scale_ref, gain_ref = refs[:6]
    outs = refs[6:]
    part, channels = totals[0].shape
    slot = place_ref[0]
    hits = head_spread(channels // P_SIZE)
    state = jnp.zeros((N, channels), F32)
    log = jnp.zeros((1, channels), F32)
    for i, got in enumerate(gots):
        later = place_ref[1 + i] > 0
        state = state + jnp.where(later, jnp.exp(log), 0.0) * got[:N].astype(F32)
        log = log + jnp.where(later, read_logs(got), 0.0)
    state = state.astype(BF16)
    init = init_ref[...].astype(BF16)
    init_fall = jnp.exp(log)
    nt = (((1,), (1,)), ((), ()))
    for k, value in enumerate(quarter_values(values, totals, lasts, scale_ref[...])):
        at = pl.ds(pl.multiple_of((slot ^ k) * part, part), part)
        c_part = conv_ref[at, channels + N :]
        carried = dot32(c_part, state)
        carried = carried + init_fall * lax.dot_general(c_part, init, nt, preferred_element_type=F32)
        y = y_ref[at] + carried * spread_heads(jnp.exp(cum_ref[at]), hits)
        gated = y * silu(value.astype(F32))
        squares = jnp.sum(gated * gated, axis=1, keepdims=True)
        if whole_group:
            meansq = squares / (H // G * P_SIZE)
            outs[0][at] = (gated * lax.rsqrt(meansq + 1e-05) * gain_ref[...]).astype(BF16)
        else:
            outs[0][at] = gated
            outs[1][at] = jnp.broadcast_to(squares, (part, LANES))


def final_output(whole_group, place, values, totals, lasts, gots, y, conved, init, cum, scale, gain):
    rows, channels = y.shape
    if whole_group:
        outs = [shape_of((rows, channels), BF16)]
    else:
        outs = [shape_of((rows, channels), F32), shape_of((rows, LANES), F32)]
    return pl.pallas_call(
        functools.partial(final_kernel, whole_group, len(gots)),
        in_specs=[SMEM] + [VMEM] * (2 * SLOTS - EARLY + 6 + len(gots)),
        out_specs=[VMEM] * len(outs),
        out_shape=outs,
        cost_estimate=cost(2 * rows * channels * N, 12 * rows * channels, 2 * rows * channels),
        name="final",
        compiler_params=params(),
    )(place, *values, *totals, *lasts, *gots, y, conved, init, cum, scale, gain)


def body(
    tokens,
    w_zx,
    zx_scale,
    w_bc,
    bc_scale,
    w_dt,
    conv_x,
    conv_bc,
    tail_x,
    tail_bc,
    head_params,
    init_state,
    norm_gain,
):
    tok_rows = tokens.shape[0]
    depth = w_zx.shape[0]
    local_heads = head_params.shape[1]
    channels = local_heads * P_SIZE
    per_group = H // G
    n_ctx = lax.axis_size("ctx")
    me = lax.axis_index("ctx")
    head_place = lax.axis_index("head")
    group_index = head_place * local_heads // per_group
    bits = [1 << i for i in range(n_ctx.bit_length() - 1)]
    part = tok_rows // SLOTS
    slot = head_place % SLOTS
    slot_ref = slot[None].astype(jnp.int32)

    dt_t = w_dt.T
    payloads = pack(jnp.stack([slot, me]).astype(jnp.int32), tokens, dt_t, n_ctx)
    payloads = [swapped(one, "ctx", j) for j, one in enumerate(payloads, 1)]
    w_all = w_zx.reshape(depth, 2 * channels)
    bc_rows = pick_group(w_bc, group_index, 1)
    fetched = join(payloads, part, (w_all, bc_rows))
    from_chip = swapped(fetched, "head", 2)
    from_core = swapped(fetched, "head", 1)

    main = channels // TILE

    def quarter(k, rows):
        order = bits if k in (0, 3) else bits[::-1]
        return k, {j: (rows, j - 1) for j in range(1, n_ctx)}, order

    def first_of(*quarters):
        tiles = (main, 2 * N // TILE)
        name = "first" + "".join(str(q[0]) for q in quarters)
        return Reduction(name, part, quarters, main, tiles, w_all, bc_rows)

    def gate_of(*quarters):
        name = "gate" + "".join(str(q[0]) for q in quarters)
        return Reduction(name, part, quarters, 0, (main, 0), w_all, bc_rows)

    q0 = (0, {j: (one, 0) for j, one in enumerate(payloads, 1)}, bits)
    q1 = quarter(1, from_core)
    first0, first1, gate01 = first_of(q0), first_of(q1), gate_of(q0, q1)
    mark = first0.send(fetched)
    mark = first1.send(mark)
    mark = gate01.send(mark)
    shift_t, cum, fade, logs = step_sizes(
        me[None].astype(jnp.int32), tokens, dt_t, payloads, head_params.T, (mark,)
    )
    mark = first0.keep(slot, me, tokens, cum)
    mark = first1.keep(slot, me, tokens, mark)
    mark = gate01.keep(slot, me, tokens, mark)
    scale = jnp.concatenate([zx_scale[1], pick_group(bc_scale, group_index, 0)], 0)[None]
    firsts01 = finish(
        "fin_first", first0.totals + first1.totals, first0.lasts + first1.lasts, scale, (mark,)
    )
    mark = firsts01[0]
    from_both = swapped(chained([from_chip], mark)[0], "head", 1)
    q2, q3 = quarter(2, from_chip), quarter(3, from_both)
    first2, first3, gate23 = first_of(q2), first_of(q3), gate_of(q2, q3)
    mark = first2.send(mark)
    mark = first3.send(mark)
    gates01 = finish("fin_gate", gate01.totals, gate01.lasts, zx_scale[0:1], (mark,))
    mark = gates01[0]
    mark = first2.keep(slot, me, tokens, mark)
    mark = first3.keep(slot, me, tokens, mark)
    mark = gate23.send(mark)

    taps = jnp.concatenate([conv_x, pick_group(conv_bc, group_index, 1)], 1)
    edge = jnp.zeros((K - 1, scale.shape[1]), BF16)
    late = (first2, first3)
    for k in range(SLOTS):
        if k < EARLY:
            rows = firsts01[k][part - (K - 1) :]
        else:
            one = late[k - EARLY]
            rows = finished(one.totals[0][part - (K - 1) :], one.lasts[0][part - (K - 1) :], scale)
        edge = jnp.where((slot ^ k) == SLOTS - 1, rows, edge)
    arrived = passed_along(edge, "ctx", 1)
    previous = jnp.concatenate([tail_x, pick_group(tail_bc, group_index, 1)], 1)
    arrived = jnp.where(me == 0, previous, arrived).astype(F32)
    arrived = jnp.concatenate([jnp.zeros((EDGE - (K - 1), arrived.shape[1]), F32), arrived], 0)
    conved, local_state = conv_and_state(
        slot_ref, firsts01, first2.totals + first3.totals, first2.lasts + first3.lasts, arrived, scale, taps, fade, logs, (mark,)
    )
    mark = gate23.keep(slot, me, tokens, conved)
    y_local = inner_output(conved, cum, shift_t, jnp.repeat(head_params[2], P_SIZE)[None], (mark,))

    run, gots = local_state, []
    later = [((me & bit) > 0).astype(jnp.int32) for bit in bits]
    for i, bit in enumerate(bits):
        if bit == bits[-1]:
            gots.append(passed_along(run, "ctx", bit))
        else:
            gots.append(swapped(run, "ctx", bit))
            run = merged(later[i][None], run, gots[-1], (mark,))

    whole_group = local_heads >= per_group
    outs = final_output(
        whole_group,
        jnp.stack([slot.astype(jnp.int32)] + later),
        gates01,
        gate23.totals,
        gate23.lasts,
        gots,
        y_local,
        conved,
        init_state.reshape(channels, N),
        cum,
        zx_scale[0:1],
        norm_gain[None],
    )
    if whole_group:
        return outs[0]
    gated, squares = outs
    slot_hits = (jnp.arange(G) == group_index).astype(F32)
    group_sums = lax.psum(slot_hits[:, None] * squares[:, 0][None, :], "head")
    totals = lax.dynamic_index_in_dim(group_sums, group_index, 0, keepdims=False)
    meansq = totals / (per_group * P_SIZE)
    return (gated * lax.rsqrt(meansq + 1e-05)[:, None] * norm_gain).astype(BF16)


def solution(mesh):
    return jax.shard_map(
        body,
        mesh=mesh,
        in_specs=(
            P("ctx", None),
            P("ctx", None, "head"),
            P(None, "head"),
            P("ctx", None, None),
            P(),
            P("ctx", "head"),
            P(None, "head"),
            P(),
            P(None, "head"),
            P(),
            P(None, "head"),
            P("head", None, None),
            P("head"),
        ),
        out_specs=P("ctx", "head"),
        check_vma=False,
    )
```

```python
import functools
import jax
import jax.numpy as jnp
from jax import lax
from jax.experimental import pallas as pl
from jax.experimental.pallas import tpu as pltpu
from jax.sharding import PartitionSpec as P

H = 128
P_SIZE = 64
N = 256
G = 8
K = 4
SLOTS = 4
LANES = 128
EDGE = 8
LOG_ROWS = 16
LOG_PARTS = 3
EARLY = 2
MIB = 1 << 20
MAIN_MIB = 32
SCALE = 64
BF16 = jnp.bfloat16
F32 = jnp.float32
VMEM = pl.BlockSpec(memory_space=pltpu.VMEM)
SMEM = pl.BlockSpec(memory_space=pltpu.SMEM)
ANY = pl.BlockSpec(memory_space=pl.ANY)


def shape_of(shape, dtype):
    return jax.ShapeDtypeStruct(shape, dtype)


def params(mib):
    return pltpu.CompilerParams(vmem_limit_bytes=mib * MIB)


def cost(flops, moved, transcendentals=0):
    return pl.CostEstimate(
        flops=int(flops) // SCALE, bytes_accessed=int(moved) // SCALE, transcendentals=int(transcendentals) // SCALE
    )


def chained(values, after):
    return lax.optimization_barrier((*values, after))[: len(values)]


def passed_along(x, axis, by):
    length = lax.axis_size(axis)
    pairs = [(i, i + by) for i in range(length) if 0 <= i + by < length]
    return lax.ppermute(x, axis, pairs)


def swapped(x, axis, by):
    length = lax.axis_size(axis)
    return lax.ppermute(x, axis, [(i, i ^ by) for i in range(length)])


def pick_group(values, group_index, axis_index):
    return lax.dynamic_index_in_dim(values, group_index, axis_index, keepdims=False)


def dot32(a, b):
    return jnp.dot(a, b, preferred_element_type=F32)


def silu(v):
    return v / (1.0 + jnp.exp(-v))


def pack_kernel(n, place_ref, *refs):
    blocks, dt_ref, outs = refs[: n - 1], refs[n - 1], refs[n:]
    part = blocks[0].shape[0]
    for block, out in zip(blocks, outs):
        out[:part] = block[...]
        out[part:] = dt_ref[...]


def pack(place, tokens, dt_t, n):
    local_heads, depth = dt_t.shape
    part = tokens.shape[0] // SLOTS
    height = part + local_heads
    return pl.pallas_call(
        functools.partial(pack_kernel, n),
        grid_spec=pltpu.PrefetchScalarGridSpec(
            num_scalar_prefetch=1,
            grid=(1,),
            in_specs=[
                pl.BlockSpec((part, depth), lambda i, place, j=j: (place[0], place[1] ^ j))
                for j in range(1, n)
            ]
            + [pl.BlockSpec((local_heads, depth), lambda i, place: (0, 0))],
            out_specs=[pl.BlockSpec((height, depth), lambda i, place: (0, 0))] * (n - 1),
        ),
        out_shape=[shape_of((height, depth), BF16)] * (n - 1),
        name="pack",
        compiler_params=params(58),
    )(place, *[tokens] * (n - 1), dt_t)


def join_kernel(part, count, *refs):
    blocks, out = refs[:count], refs[-1]
    for i, block in enumerate(blocks):
        out[i * part : (i + 1) * part] = block[:part]


def join(blocks, part, after):
    depth = blocks[0].shape[1]
    return pl.pallas_call(
        functools.partial(join_kernel, part, len(blocks)),
        in_specs=[VMEM] * len(blocks) + [ANY] * len(after),
        out_specs=VMEM,
        out_shape=shape_of((part * len(blocks), depth), BF16),
        name="join",
        compiler_params=params(MAIN_MIB),
    )(*blocks, *after)


class Reduction:
    def __init__(self, blocks, order, weights):
        self.blocks, self.order, self.weights = blocks, order, weights
        self.part = blocks[0].shape[0]

    def rows(self, offsets, after):
        return chained([jnp.concatenate([self.blocks[j] for j in offsets], 0)], after)[0]

    def send(self, after):
        offsets = [j for j in range(len(self.blocks)) if j & self.order[0]]
        out = dot32(self.rows(offsets, after), self.weights).astype(BF16)
        self.got = swapped(out, "ctx", self.order[0])
        return out

    def keep(self, after):
        kept = [j for j in range(len(self.blocks)) if not j & self.order[0]]
        size = self.part
        got = [self.got[i * size : (i + 1) * size] for i in range(len(kept))]
        bit = self.order[1]
        gone = [i for i, j in enumerate(kept) if j & bit]
        stay = [i for i, j in enumerate(kept) if not j & bit]
        rows = self.rows([kept[i] for i in gone], after)
        out = (dot32(rows, self.weights) + jnp.concatenate([got[i] for i in gone], 0)).astype(BF16)
        mark = out
        arrived = swapped(out, "ctx", bit)
        rows = self.rows([kept[i] for i in stay], after)
        total = dot32(rows, self.weights) + jnp.concatenate([got[i] for i in stay], 0)
        kept = [kept[i] for i in stay]
        for bit in self.order[2:]:
            total = total + arrived.astype(F32)
            gone = [i for i, j in enumerate(kept) if j & bit]
            stay = [i for i, j in enumerate(kept) if not j & bit]
            parts = [total[i * size : (i + 1) * size] for i in range(len(kept))]
            out = jnp.concatenate([parts[i] for i in gone], 0).astype(BF16)
            total = jnp.concatenate([parts[i] for i in stay], 0)
            arrived = swapped(out, "ctx", bit)
            kept = [kept[i] for i in stay]
        self.total, self.last = total, arrived
        return mark


def finished(total, last, scale):
    return ((total + last.astype(F32)) * scale).astype(BF16)


def finish_kernel(count, *refs):
    totals, lasts, scale_ref, outs = refs[:count], refs[count : 2 * count], refs[2 * count], refs[-count:]
    for total, last, out in zip(totals, lasts, outs):
        out[...] = finished(total[...], last[...], scale_ref[...])


def finish(name, totals, lasts, scale, after):
    count = len(totals)
    return pl.pallas_call(
        functools.partial(finish_kernel, count),
        in_specs=[VMEM] * (2 * count + 1) + [ANY] * len(after),
        out_specs=[VMEM] * count,
        out_shape=[shape_of(t.shape, BF16) for t in totals],
        cost_estimate=cost(4 * count * totals[0].size, 8 * count * totals[0].size),
        name=name,
        compiler_params=params(MAIN_MIB),
    )(*totals, *lasts, scale, *after)


def quarter_values(values, totals, lasts, scale):
    early = [v[...] for v in values]
    return early + [finished(t[...], l[...], scale) for t, l in zip(totals, lasts)]


def step_kernel(n, me_ref, tok_ref, *refs):
    weights, heads_ref = refs[:n], refs[n]
    shift_t_ref, cum_ref, fade_ref, log_ref, acc = refs[-5:]
    j = pl.program_id(0)

    @pl.when(j == 0)
    def _():
        acc[...] = jnp.zeros_like(acc)

    for i in range(n):

        @pl.when(j == i)
        def _():
            acc[...] += lax.dot_general(
                weights[i][...], tok_ref[...], (((1,), (1,)), ((), ())), preferred_element_type=F32
            )

    @pl.when(j == pl.num_programs(0) - 1)
    def _():
        v = acc[...] + heads_ref[:, 0:1]
        step = jnp.maximum(v, 0.0) + jnp.log1p(jnp.exp(-jnp.abs(v)))
        rate = -jnp.exp(heads_ref[:, 1:2]) * step
        rows = rate.shape[1]
        up_to = lax.broadcasted_iota(jnp.int32, (rows, rows), 0) <= lax.broadcasted_iota(
            jnp.int32, (rows, rows), 1
        )
        cum = jnp.dot(
            rate, up_to.astype(F32), precision=lax.Precision.HIGHEST, preferred_element_type=F32
        )
        last = cum[:, rows - 1 : rows]
        shift_t_ref[...] = cum - jnp.log(step)
        cum_ref[...] = cum.T
        fade_ref[...] = (jnp.exp(last - cum) * step).T
        log_ref[...] = jnp.broadcast_to(last.T, log_ref.shape)


def step_sizes(me, tokens, dt_t, payloads, heads, after):
    local_heads, depth = dt_t.shape
    n = len(payloads) + 1
    rows = tokens.shape[0]
    last = payloads[0].shape[0] // local_heads - 1
    whole = lambda shape: pl.BlockSpec(shape, lambda j, me: (0, 0))
    return pl.pallas_call(
        functools.partial(step_kernel, n),
        grid_spec=pltpu.PrefetchScalarGridSpec(
            num_scalar_prefetch=1,
            grid=(n,),
            in_specs=[
                pl.BlockSpec((rows, depth), lambda j, me: (0, me[0] ^ j)),
                whole((local_heads, depth)),
            ]
            + [pl.BlockSpec((local_heads, depth), lambda j, me: (last, 0))] * (n - 1)
            + [whole((local_heads, 3))]
            + [ANY] * len(after),
            out_specs=[
                whole((local_heads, rows)),
                whole((rows, local_heads)),
                whole((rows, local_heads)),
                whole((EDGE, local_heads)),
            ],
            scratch_shapes=[pltpu.VMEM((local_heads, rows), F32)],
        ),
        out_shape=[
            shape_of((local_heads, rows), F32),
            shape_of((rows, local_heads), F32),
            shape_of((rows, local_heads), F32),
            shape_of((EDGE, local_heads), F32),
        ],
        cost_estimate=cost(2 * n * rows * depth * LANES, 2 * n * rows * depth),
        name="steps",
        compiler_params=params(MAIN_MIB),
    )(me, tokens, dt_t, *payloads, heads, *after)


def write_logs(state_ref, parts):
    rows = lax.broadcasted_iota(jnp.int32, (LOG_ROWS, state_ref.shape[1]), 0)
    block = jnp.zeros((LOG_ROWS, state_ref.shape[1]), F32)
    for i, one in enumerate(parts):
        block = jnp.where(rows == i, one, block)
    state_ref[N:] = block.astype(BF16)


def read_logs(state_ref):
    block = state_ref[N:].astype(F32)
    return sum(block[i : i + 1] for i in range(LOG_PARTS))


def split_logs(logs):
    parts = []
    for _ in range(LOG_PARTS):
        parts.append(logs.astype(BF16).astype(F32))
        logs = logs - parts[-1]
    return parts


def head_spread(local_heads):
    channels = local_heads * P_SIZE
    hit = (
        lax.broadcasted_iota(jnp.int32, (local_heads, channels), 1) // P_SIZE
        == lax.broadcasted_iota(jnp.int32, (local_heads, channels), 0)
    )
    return hit.astype(F32).astype(BF16)


def spread_heads(values, hits):
    high = values.astype(BF16)
    low = (values - high.astype(F32)).astype(BF16)
    return dot32(high, hits) + dot32(low, hits)


def conv_kernel(place_ref, *refs):
    values, totals, lasts = refs[:EARLY], refs[EARLY:SLOTS], refs[SLOTS : 2 * SLOTS - EARLY]
    edge_ref, scale_ref, taps_ref, fade_ref, log_ref = refs[2 * SLOTS - EARLY : 2 * SLOTS - EARLY + 5]
    conv_ref, state_ref, vals = refs[-3:]
    part, width = totals[0].shape
    rows = part * SLOTS
    channels = width - 2 * N
    slot = place_ref[0]
    vals[:EDGE] = edge_ref[...]
    for k, value in enumerate(quarter_values(values, totals, lasts, scale_ref[...])):
        start = pl.multiple_of(EDGE + (slot ^ k) * part, EDGE)
        vals[pl.ds(start, part)] = value.astype(F32)
    for c in range(0, width, 2 * LANES):
        cols = slice(c, c + 2 * LANES)
        for r in range(0, rows, part):
            summed = taps_ref[K : K + 1, cols]
            for tap in range(K):
                at = r + EDGE - (K - 1) + tap
                summed = summed + taps_ref[tap : tap + 1, cols] * vals[at : at + part, cols]
            conv_ref[r : r + part, cols] = silu(summed).astype(BF16)
    hits = head_spread(channels // P_SIZE)
    faded = spread_heads(fade_ref[...], hits) * conv_ref[:, :channels].astype(F32)
    state_ref[:N] = lax.dot_general(
        conv_ref[:, channels : channels + N],
        faded.astype(BF16),
        (((0,), (0,)), ((), ())),
        preferred_element_type=F32,
    ).astype(BF16)
    left, parts = log_ref[...], []
    for _ in range(LOG_PARTS):
        parts.append(left.astype(BF16))
        left = left - parts[-1].astype(F32)
    spread = [dot32(one, hits)[0:1] for one in parts]
    write_logs(state_ref, spread)


def conv_and_state(slot, values, totals, lasts, edge, scale, taps, fade, logs, after):
    part, width = totals[0].shape
    rows = part * SLOTS
    return pl.pallas_call(
        conv_kernel,
        in_specs=[SMEM] + [VMEM] * (2 * SLOTS - EARLY + 5) + [ANY] * len(after),
        out_specs=[VMEM, VMEM],
        out_shape=[shape_of((rows, width), BF16), shape_of((N + LOG_ROWS, width - 2 * N), BF16)],
        scratch_shapes=[pltpu.VMEM((rows + EDGE, width), F32)],
        cost_estimate=cost(30 * rows * width, 12 * rows * width, 2 * rows * width),
        name="conv",
        compiler_params=params(MAIN_MIB),
    )(slot, *values, *totals, *lasts, edge, scale, taps, fade, logs, *after)


def inner_kernel(conv_ref, cum_ref, shift_t_ref, skip_ref, *refs):
    y_ref, scores = refs[-2:]
    rows, width = conv_ref.shape
    channels = width - 2 * N
    size = LANES
    blocks = rows // size
    nt = (((1,), (1,)), ((), ()))
    scores[...] = lax.dot_general(
        conv_ref[:, channels + N :], conv_ref[:, channels : channels + N], nt, preferred_element_type=F32
    )
    lower = lax.broadcasted_iota(jnp.int32, (size, size), 0) >= lax.broadcasted_iota(
        jnp.int32, (size, size), 1
    )
    left = lax.broadcasted_iota(jnp.int32, (size, 2 * P_SIZE), 1) < P_SIZE
    for pair in range(channels // (2 * P_SIZE)):
        cols = slice(pair * 2 * P_SIZE, (pair + 1) * 2 * P_SIZE)
        for a in range(blocks):
            t = slice(a * size, (a + 1) * size)
            products = []
            for h in (2 * pair, 2 * pair + 1):
                here = cum_ref[t, h : h + 1]
                own = jnp.where(lower, here - shift_t_ref[h : h + 1, t], -jnp.inf)
                weights = jnp.exp(own) * scores[t, t]
                if a > 0:
                    before = slice(0, a * size)
                    earlier = jnp.exp(here - shift_t_ref[h : h + 1, before]) * scores[t, before]
                    weights = jnp.concatenate([earlier, weights], 1)
                products.append(dot32(weights.astype(BF16), conv_ref[: (a + 1) * size, cols]))
            y_ref[t, cols] = jnp.where(left, products[0], products[1]) + skip_ref[:, cols] * conv_ref[
                t, cols
            ].astype(F32)


def inner_output(conved, cum, shift_t, skip, after):
    rows, width = conved.shape
    channels = width - 2 * N
    return pl.pallas_call(
        inner_kernel,
        in_specs=[VMEM] * 4 + [ANY] * len(after),
        out_specs=VMEM,
        out_shape=shape_of((rows, channels), F32),
        scratch_shapes=[pltpu.VMEM((rows, rows), F32)],
        cost_estimate=cost(2 * rows * rows * channels, 8 * rows * width, rows * rows * channels // P_SIZE),
        name="inner",
        compiler_params=params(MAIN_MIB),
    )(conved, cum, shift_t, skip, *after)


def merge_kernel(later_ref, own_ref, got_ref, *refs):
    out_ref = refs[-1]
    own_log, got_log = read_logs(own_ref), read_logs(got_ref)
    own, got = own_ref[:N].astype(F32), got_ref[:N].astype(F32)
    later = later_ref[0] > 0
    own_fall = jnp.where(later, 1.0, jnp.exp(got_log))
    got_fall = jnp.where(later, jnp.exp(own_log), 1.0)
    out_ref[:N] = (own_fall * own + got_fall * got).astype(BF16)
    write_logs(out_ref, split_logs(own_log + got_log))


def merged(later, own, got, after):
    return pl.pallas_call(
        merge_kernel,
        in_specs=[SMEM, VMEM, VMEM] + [ANY] * len(after),
        out_specs=VMEM,
        out_shape=shape_of(own.shape, BF16),
        cost_estimate=cost(4 * own.size, 6 * own.size),
        name="merge",
        compiler_params=params(MAIN_MIB),
    )(later, own, got, *after)


def final_kernel(whole_group, rounds, place_ref, *refs):
    values, totals, lasts = refs[:EARLY], refs[EARLY:SLOTS], refs[SLOTS : 2 * SLOTS - EARLY]
    refs = refs[2 * SLOTS - EARLY :]
    gots, refs = refs[:rounds], refs[rounds:]
    y_ref, conv_ref, init_ref, cum_ref, scale_ref, gain_ref = refs[:6]
    outs = refs[6:]
    part, channels = totals[0].shape
    slot = place_ref[0]
    hits = head_spread(channels // P_SIZE)
    state = jnp.zeros((N, channels), F32)
    log = jnp.zeros((1, channels), F32)
    for i, got in enumerate(gots):
        later = place_ref[1 + i] > 0
        state = state + jnp.where(later, jnp.exp(log), 0.0) * got[:N].astype(F32)
        log = log + jnp.where(later, read_logs(got), 0.0)
    state = state.astype(BF16)
    init = init_ref[...].astype(BF16)
    init_fall = jnp.exp(log)
    nt = (((1,), (1,)), ((), ()))
    for k, value in enumerate(quarter_values(values, totals, lasts, scale_ref[...])):
        at = pl.ds(pl.multiple_of((slot ^ k) * part, part), part)
        c_part = conv_ref[at, channels + N :]
        carried = dot32(c_part, state)
        carried = carried + init_fall * lax.dot_general(c_part, init, nt, preferred_element_type=F32)
        y = y_ref[at] + carried * spread_heads(jnp.exp(cum_ref[at]), hits)
        gated = y * silu(value.astype(F32))
        squares = jnp.sum(gated * gated, axis=1, keepdims=True)
        if whole_group:
            meansq = squares / (H // G * P_SIZE)
            outs[0][at] = (gated * lax.rsqrt(meansq + 1e-05) * gain_ref[...]).astype(BF16)
        else:
            outs[0][at] = gated
            outs[1][at] = jnp.broadcast_to(squares, (part, LANES))


def final_output(whole_group, place, values, totals, lasts, gots, y, conved, init, cum, scale, gain):
    rows, channels = y.shape
    if whole_group:
        outs = [shape_of((rows, channels), BF16)]
    else:
        outs = [shape_of((rows, channels), F32), shape_of((rows, LANES), F32)]
    return pl.pallas_call(
        functools.partial(final_kernel, whole_group, len(gots)),
        in_specs=[SMEM] + [VMEM] * (2 * SLOTS - EARLY + 6 + len(gots)),
        out_specs=[VMEM] * len(outs),
        out_shape=outs,
        cost_estimate=cost(2 * rows * channels * N, 12 * rows * channels, 2 * rows * channels),
        name="final",
        compiler_params=params(MAIN_MIB),
    )(place, *values, *totals, *lasts, *gots, y, conved, init, cum, scale, gain)


def body(
    tokens,
    w_zx,
    zx_scale,
    w_bc,
    bc_scale,
    w_dt,
    conv_x,
    conv_bc,
    tail_x,
    tail_bc,
    head_params,
    init_state,
    norm_gain,
):
    tok_rows = tokens.shape[0]
    depth = w_zx.shape[0]
    local_heads = head_params.shape[1]
    channels = local_heads * P_SIZE
    per_group = H // G
    n_ctx = lax.axis_size("ctx")
    me = lax.axis_index("ctx")
    head_place = lax.axis_index("head")
    group_index = head_place * local_heads // per_group
    bits = [1 << i for i in range(n_ctx.bit_length() - 1)]
    part = tok_rows // SLOTS
    slot = head_place % SLOTS
    slot_ref = slot[None].astype(jnp.int32)

    dt_t = w_dt.T
    payloads = pack(jnp.stack([slot, me]).astype(jnp.int32), tokens, dt_t, n_ctx)
    payloads = [swapped(one, "ctx", j) for j, one in enumerate(payloads, 1)]
    w_all = w_zx.reshape(depth, 2 * channels)
    bc_rows = pick_group(w_bc, group_index, 1)
    gate_w = w_all[:, :channels]
    first_w = jnp.concatenate([w_all[:, channels:], bc_rows], 1)
    fetched = join(payloads, part, (gate_w, first_w))
    from_chip = swapped(fetched, "head", 2)
    from_core = swapped(fetched, "head", 1)


    own_rows = lax.dynamic_slice_in_dim(tokens, me * depth, depth, 1)

    def quarter(k, rows):
        order = bits if k in (0, 3) else bits[::-1]
        blocks = [lax.dynamic_slice_in_dim(own_rows, (slot ^ k) * part, part, 0), *rows]
        return Reduction(blocks, order, first_w), Reduction(blocks, order, gate_w)

    def blocks_of(rows):
        return [rows[i * part : (i + 1) * part] for i in range(n_ctx - 1)]

    first0, gate0 = quarter(0, [one[:part] for one in payloads])
    first1, gate1 = quarter(1, blocks_of(from_core))
    mark = first0.send(fetched)
    mark = first1.send(mark)
    mark = gate0.send(mark)
    mark = gate1.send(mark)
    shift_t, cum, fade, logs = step_sizes(
        me[None].astype(jnp.int32), tokens, dt_t, payloads, head_params.T, (mark,)
    )
    mark = first0.keep(cum)
    mark = first1.keep(mark)
    mark = gate0.keep(mark)
    mark = gate1.keep(mark)
    scale = jnp.concatenate([zx_scale[1], pick_group(bc_scale, group_index, 0)], 0)[None]
    firsts01 = finish(
        "fin_first", (first0.total, first1.total), (first0.last, first1.last), scale, (mark,)
    )
    mark = firsts01[0]
    from_both = swapped(chained([from_chip], mark)[0], "head", 1)
    first2, gate2 = quarter(2, blocks_of(from_chip))
    first3, gate3 = quarter(3, blocks_of(from_both))
    mark = first2.send(mark)
    mark = first3.send(mark)
    gates01 = finish("fin_gate", (gate0.total, gate1.total), (gate0.last, gate1.last), zx_scale[0:1], (mark,))
    mark = gates01[0]
    mark = first2.keep(mark)
    mark = first3.keep(mark)
    mark = gate2.send(mark)
    mark = gate3.send(mark)

    taps = jnp.concatenate([conv_x, pick_group(conv_bc, group_index, 1)], 1)
    edge = jnp.zeros((K - 1, scale.shape[1]), BF16)
    late = (first2, first3)
    for k in range(SLOTS):
        if k < EARLY:
            rows = firsts01[k][part - (K - 1) :]
        else:
            one = late[k - EARLY]
            rows = finished(one.total[part - (K - 1) :], one.last[part - (K - 1) :], scale)
        edge = jnp.where((slot ^ k) == SLOTS - 1, rows, edge)
    arrived = passed_along(edge, "ctx", 1)
    previous = jnp.concatenate([tail_x, pick_group(tail_bc, group_index, 1)], 1)
    arrived = jnp.where(me == 0, previous, arrived).astype(F32)
    arrived = jnp.concatenate([jnp.zeros((EDGE - (K - 1), arrived.shape[1]), F32), arrived], 0)
    conved, local_state = conv_and_state(
        slot_ref, firsts01, (first2.total, first3.total), (first2.last, first3.last), arrived, scale, taps, fade, logs, (mark,)
    )
    mark = gate2.keep(conved)
    mark = gate3.keep(mark)
    y_local = inner_output(conved, cum, shift_t, jnp.repeat(head_params[2], P_SIZE)[None], (mark,))

    run, gots = local_state, []
    later = [((me & bit) > 0).astype(jnp.int32) for bit in bits]
    for i, bit in enumerate(bits):
        if bit == bits[-1]:
            gots.append(passed_along(run, "ctx", bit))
        else:
            gots.append(swapped(run, "ctx", bit))
            run = merged(later[i][None], run, gots[-1], (mark,))

    whole_group = local_heads >= per_group
    outs = final_output(
        whole_group,
        jnp.stack([slot.astype(jnp.int32)] + later),
        gates01,
        (gate2.total, gate3.total),
        (gate2.last, gate3.last),
        gots,
        y_local,
        conved,
        init_state.reshape(channels, N),
        cum,
        zx_scale[0:1],
        norm_gain[None],
    )
    if whole_group:
        return outs[0]
    gated, squares = outs
    slot_hits = (jnp.arange(G) == group_index).astype(F32)
    group_sums = lax.psum(slot_hits[:, None] * squares[:, 0][None, :], "head")
    totals = lax.dynamic_index_in_dim(group_sums, group_index, 0, keepdims=False)
    meansq = totals / (per_group * P_SIZE)
    return (gated * lax.rsqrt(meansq + 1e-05)[:, None] * norm_gain).astype(BF16)


def solution(mesh):
    return jax.shard_map(
        body,
        mesh=mesh,
        in_specs=(
            P("ctx", None),
            P("ctx", None, "head"),
            P(None, "head"),
            P("ctx", None, None),
            P(),
            P("ctx", "head"),
            P(None, "head"),
            P(),
            P(None, "head"),
            P(),
            P(None, "head"),
            P("head", None, None),
            P("head"),
        ),
        out_specs=P("ctx", "head"),
        check_vma=False,
    )
```

```python
import functools
import jax
import jax.numpy as jnp
from jax import lax
from jax.experimental import pallas as pl
from jax.experimental.pallas import tpu as pltpu
from jax.sharding import PartitionSpec as P

H = 128
P_SIZE = 64
N = 256
G = 8
K = 4
SLOTS = 4
LANES = 128
EDGE = 16
LOG_ROWS = 16
LOG_PARTS = 3
EARLY = 2
MIB = 1 << 20
MAIN_MIB = 32
SCALE = 64
BF16 = jnp.bfloat16
F32 = jnp.float32
VMEM = pl.BlockSpec(memory_space=pltpu.VMEM)
SMEM = pl.BlockSpec(memory_space=pltpu.SMEM)
ANY = pl.BlockSpec(memory_space=pl.ANY)


def shape_of(shape, dtype):
    return jax.ShapeDtypeStruct(shape, dtype)


def params(mib):
    return pltpu.CompilerParams(vmem_limit_bytes=mib * MIB)


def cost(flops, moved, transcendentals=0):
    return pl.CostEstimate(
        flops=int(flops) // SCALE, bytes_accessed=int(moved) // SCALE, transcendentals=int(transcendentals) // SCALE
    )


def chained(values, after):
    return lax.optimization_barrier((*values, after))[: len(values)]


def passed_along(x, axis, by):
    length = lax.axis_size(axis)
    pairs = [(i, i + by) for i in range(length) if 0 <= i + by < length]
    return lax.ppermute(x, axis, pairs)


def swapped(x, axis, by):
    length = lax.axis_size(axis)
    return lax.ppermute(x, axis, [(i, i ^ by) for i in range(length)])


def pick_group(values, group_index, axis_index):
    return lax.dynamic_index_in_dim(values, group_index, axis_index, keepdims=False)


def dot32(a, b):
    return jnp.dot(a, b, preferred_element_type=F32)


def silu(v):
    return v / (1.0 + jnp.exp(-v))


def pack_kernel(n, place_ref, *refs):
    blocks, tails, dt_ref, outs = refs[: n - 1], refs[n - 1 : 2 * n - 2], refs[2 * n - 2], refs[2 * n - 1 :]
    part, edge = blocks[0].shape[0], tails[0].shape[0]
    for block, tail, out in zip(blocks, tails, outs):
        out[:part] = block[...]
        out[part : part + edge] = tail[...]
        out[part + edge :] = dt_ref[...]


def pack(place, tokens, dt_t, n):
    dt_rows, depth = dt_t.shape
    part = tokens.shape[0] // SLOTS
    height = part + EDGE + dt_rows
    last = tokens.shape[0] // EDGE - 1
    return pl.pallas_call(
        functools.partial(pack_kernel, n),
        grid_spec=pltpu.PrefetchScalarGridSpec(
            num_scalar_prefetch=1,
            grid=(1,),
            in_specs=[
                pl.BlockSpec((part, depth), lambda i, place, j=j: (place[0], place[1] ^ j))
                for j in range(1, n)
            ]
            + [pl.BlockSpec((EDGE, depth), lambda i, place, j=j: (last, place[1] ^ j)) for j in range(1, n)]
            + [pl.BlockSpec((dt_rows, depth), lambda i, place: (0, 0))],
            out_specs=[pl.BlockSpec((height, depth), lambda i, place: (0, 0))] * (n - 1),
        ),
        out_shape=[shape_of((height, depth), BF16)] * (n - 1),
        name="pack",
        compiler_params=params(58),
    )(place, *[tokens] * (2 * n - 2), dt_t)


def join_kernel(part, count, *refs):
    blocks, out = refs[:count], refs[-1]
    for i, block in enumerate(blocks):
        out[i * part : (i + 1) * part] = block[:part]


def join(blocks, part, after):
    depth = blocks[0].shape[1]
    return pl.pallas_call(
        functools.partial(join_kernel, part, len(blocks)),
        in_specs=[VMEM] * len(blocks) + [ANY] * len(after),
        out_specs=VMEM,
        out_shape=shape_of((part * len(blocks), depth), BF16),
        name="join",
        compiler_params=params(MAIN_MIB),
    )(*blocks, *after)


class Reduction:
    def __init__(self, blocks, order, weights):
        self.blocks, self.order, self.weights = blocks, order, weights
        self.part = blocks[0].shape[0]

    def rows(self, offsets, after):
        return chained([jnp.concatenate([self.blocks[j] for j in offsets], 0)], after)[0]

    def send(self, after):
        offsets = [j for j in range(len(self.blocks)) if j & self.order[0]]
        out = dot32(self.rows(offsets, after), self.weights).astype(BF16)
        self.got = swapped(out, "ctx", self.order[0])
        return out

    def keep(self, after):
        kept = [j for j in range(len(self.blocks)) if not j & self.order[0]]
        size = self.part
        got = [self.got[i * size : (i + 1) * size] for i in range(len(kept))]
        bit = self.order[1]
        gone = [i for i, j in enumerate(kept) if j & bit]
        stay = [i for i, j in enumerate(kept) if not j & bit]
        rows = self.rows([kept[i] for i in gone], after)
        out = (dot32(rows, self.weights) + jnp.concatenate([got[i] for i in gone], 0)).astype(BF16)
        mark = out
        arrived = swapped(out, "ctx", bit)
        rows = self.rows([kept[i] for i in stay], after)
        total = dot32(rows, self.weights) + jnp.concatenate([got[i] for i in stay], 0)
        kept = [kept[i] for i in stay]
        for bit in self.order[2:]:
            total = total + arrived.astype(F32)
            gone = [i for i, j in enumerate(kept) if j & bit]
            stay = [i for i, j in enumerate(kept) if not j & bit]
            parts = [total[i * size : (i + 1) * size] for i in range(len(kept))]
            out = jnp.concatenate([parts[i] for i in gone], 0).astype(BF16)
            total = jnp.concatenate([parts[i] for i in stay], 0)
            arrived = swapped(out, "ctx", bit)
            kept = [kept[i] for i in stay]
        self.total, self.last = total, arrived
        return mark


def finished(total, last, scale):
    return ((total + last.astype(F32)) * scale).astype(BF16)


def finish_kernel(count, *refs):
    totals, lasts, scale_ref, outs = refs[:count], refs[count : 2 * count], refs[2 * count], refs[-count:]
    for total, last, out in zip(totals, lasts, outs):
        out[...] = finished(total[...], last[...], scale_ref[...])


def finish(name, totals, lasts, scale, after):
    count = len(totals)
    return pl.pallas_call(
        functools.partial(finish_kernel, count),
        in_specs=[VMEM] * (2 * count + 1) + [ANY] * len(after),
        out_specs=[VMEM] * count,
        out_shape=[shape_of(t.shape, BF16) for t in totals],
        cost_estimate=cost(4 * count * totals[0].size, 8 * count * totals[0].size),
        name=name,
        compiler_params=params(MAIN_MIB),
    )(*totals, *lasts, scale, *after)


def quarter_values(values, totals, lasts, scale):
    early = [v[...] for v in values]
    return early + [finished(t[...], l[...], scale) for t, l in zip(totals, lasts)]


def step_kernel(n, me_ref, tok_ref, *refs):
    weights, heads_ref = refs[:n], refs[n]
    shift_t_ref, cum_ref, fade_ref, log_ref, acc = refs[-5:]
    j = pl.program_id(0)

    @pl.when(j == 0)
    def _():
        acc[...] = jnp.zeros_like(acc)

    for i in range(n):

        @pl.when(j == i)
        def _():
            acc[...] += lax.dot_general(
                weights[i][...], tok_ref[...], (((1,), (1,)), ((), ())), preferred_element_type=F32
            )

    @pl.when(j == pl.num_programs(0) - 1)
    def _():
        v = acc[: heads_ref.shape[0]] + heads_ref[:, 0:1]
        step = jnp.maximum(v, 0.0) + jnp.log1p(jnp.exp(-jnp.abs(v)))
        rate = -jnp.exp(heads_ref[:, 1:2]) * step
        rows = rate.shape[1]
        up_to = lax.broadcasted_iota(jnp.int32, (rows, rows), 0) <= lax.broadcasted_iota(
            jnp.int32, (rows, rows), 1
        )
        cum = jnp.dot(
            rate, up_to.astype(F32), precision=lax.Precision.HIGHEST, preferred_element_type=F32
        )
        last = cum[:, rows - 1 : rows]
        shift_t_ref[...] = cum - jnp.log(step)
        cum_ref[...] = cum.T
        fade_ref[...] = (jnp.exp(last - cum) * step).T
        log_ref[...] = jnp.broadcast_to(last.T, log_ref.shape)


def step_sizes(place, tokens, dt_t, payloads, heads, after):
    dt_rows, depth = dt_t.shape
    local_heads = heads.shape[0]
    n = len(payloads) + 1
    rows = tokens.shape[0]
    last = payloads[0].shape[0] // dt_rows - 1
    whole = lambda shape: pl.BlockSpec(shape, lambda j, place: (0, 0))
    return pl.pallas_call(
        functools.partial(step_kernel, n),
        grid_spec=pltpu.PrefetchScalarGridSpec(
            num_scalar_prefetch=1,
            grid=(n,),
            in_specs=[
                pl.BlockSpec((rows, depth), lambda j, place: (0, place[1] ^ j)),
                whole((dt_rows, depth)),
            ]
            + [pl.BlockSpec((dt_rows, depth), lambda j, place: (last, 0))] * (n - 1)
            + [whole((local_heads, 3))]
            + [ANY] * len(after),
            out_specs=[
                whole((local_heads, rows)),
                whole((rows, local_heads)),
                whole((rows, local_heads)),
                whole((8, local_heads)),
            ],
            scratch_shapes=[pltpu.VMEM((dt_rows, rows), F32)],
        ),
        out_shape=[
            shape_of((local_heads, rows), F32),
            shape_of((rows, local_heads), F32),
            shape_of((rows, local_heads), F32),
            shape_of((8, local_heads), F32),
        ],
        cost_estimate=cost(2 * n * rows * depth * LANES, 2 * n * rows * depth),
        name="steps",
        compiler_params=params(MAIN_MIB),
    )(place, tokens, dt_t, *payloads, heads, *after)


def write_logs(state_ref, parts):
    rows = lax.broadcasted_iota(jnp.int32, (LOG_ROWS, state_ref.shape[1]), 0)
    block = jnp.zeros((LOG_ROWS, state_ref.shape[1]), F32)
    for i, one in enumerate(parts):
        block = jnp.where(rows == i, one, block)
    state_ref[N:] = block.astype(BF16)


def read_logs(state_ref):
    block = state_ref[N:].astype(F32)
    return sum(block[i : i + 1] for i in range(LOG_PARTS))


def split_logs(logs):
    parts = []
    for _ in range(LOG_PARTS):
        parts.append(logs.astype(BF16).astype(F32))
        logs = logs - parts[-1]
    return parts


def head_spread(local_heads):
    channels = local_heads * P_SIZE
    hit = (
        lax.broadcasted_iota(jnp.int32, (local_heads, channels), 1) // P_SIZE
        == lax.broadcasted_iota(jnp.int32, (local_heads, channels), 0)
    )
    return hit.astype(F32).astype(BF16)


def spread_heads(values, hits):
    high = values.astype(BF16)
    low = (values - high.astype(F32)).astype(BF16)
    return dot32(high, hits) + dot32(low, hits)


def conv_kernel(place_ref, *refs):
    values, totals, lasts = refs[:EARLY], refs[EARLY:SLOTS], refs[SLOTS : 2 * SLOTS - EARLY]
    arrived_ref, before_ref, scale_ref, taps_ref, fade_ref, log_ref = refs[2 * SLOTS - EARLY : 2 * SLOTS - EARLY + 6]
    conv_ref, state_ref, vals = refs[-3:]
    part, width = totals[0].shape
    rows = part * SLOTS
    channels = width - 2 * N
    slot = place_ref[0]
    first = place_ref[1] == 0
    vals[:EDGE] = jnp.where(first, before_ref[...].astype(F32), arrived_ref[...].astype(F32))
    for k, value in enumerate(quarter_values(values, totals, lasts, scale_ref[...])):
        start = pl.multiple_of(EDGE + (slot ^ k) * part, EDGE)
        vals[pl.ds(start, part)] = value[:part].astype(F32)
    for c in range(0, width, 2 * LANES):
        cols = slice(c, c + 2 * LANES)
        for r in range(0, rows, part):
            summed = taps_ref[K : K + 1, cols]
            for tap in range(K):
                at = r + EDGE - (K - 1) + tap
                summed = summed + taps_ref[tap : tap + 1, cols] * vals[at : at + part, cols]
            conv_ref[r : r + part, cols] = silu(summed).astype(BF16)
    hits = head_spread(channels // P_SIZE)
    faded = spread_heads(fade_ref[...], hits) * conv_ref[:, :channels].astype(F32)
    state_ref[:N] = lax.dot_general(
        conv_ref[:, channels : channels + N],
        faded.astype(BF16),
        (((0,), (0,)), ((), ())),
        preferred_element_type=F32,
    ).astype(BF16)
    left, parts = log_ref[...], []
    for _ in range(LOG_PARTS):
        parts.append(left.astype(BF16))
        left = left - parts[-1].astype(F32)
    spread = [dot32(one, hits)[0:1] for one in parts]
    write_logs(state_ref, spread)


def conv_and_state(place, values, totals, lasts, arrived, before, scale, taps, fade, logs, after):
    part, width = totals[0].shape
    rows = part * SLOTS
    return pl.pallas_call(
        conv_kernel,
        in_specs=[SMEM] + [VMEM] * (2 * SLOTS - EARLY + 6) + [ANY] * len(after),
        out_specs=[VMEM, VMEM],
        out_shape=[shape_of((rows, width), BF16), shape_of((N + LOG_ROWS, width - 2 * N), BF16)],
        scratch_shapes=[pltpu.VMEM((rows + EDGE, width), F32)],
        cost_estimate=cost(30 * rows * width, 12 * rows * width, 2 * rows * width),
        name="conv",
        compiler_params=params(MAIN_MIB),
    )(place, *values, *totals, *lasts, arrived, before, scale, taps, fade, logs, *after)


def inner_kernel(conv_ref, cum_ref, shift_t_ref, skip_ref, *refs):
    y_ref, scores = refs[-2:]
    rows, width = conv_ref.shape
    channels = width - 2 * N
    size = LANES
    blocks = rows // size
    nt = (((1,), (1,)), ((), ()))
    scores[...] = lax.dot_general(
        conv_ref[:, channels + N :], conv_ref[:, channels : channels + N], nt, preferred_element_type=F32
    )
    lower = lax.broadcasted_iota(jnp.int32, (size, size), 0) >= lax.broadcasted_iota(
        jnp.int32, (size, size), 1
    )
    left = lax.broadcasted_iota(jnp.int32, (size, 2 * P_SIZE), 1) < P_SIZE
    for pair in range(channels // (2 * P_SIZE)):
        cols = slice(pair * 2 * P_SIZE, (pair + 1) * 2 * P_SIZE)
        for a in range(blocks):
            t = slice(a * size, (a + 1) * size)
            products = []
            for h in (2 * pair, 2 * pair + 1):
                here = cum_ref[t, h : h + 1]
                own = jnp.where(lower, here - shift_t_ref[h : h + 1, t], -jnp.inf)
                weights = jnp.exp(own) * scores[t, t]
                if a > 0:
                    before = slice(0, a * size)
                    earlier = jnp.exp(here - shift_t_ref[h : h + 1, before]) * scores[t, before]
                    weights = jnp.concatenate([earlier, weights], 1)
                products.append(dot32(weights.astype(BF16), conv_ref[: (a + 1) * size, cols]))
            y_ref[t, cols] = jnp.where(left, products[0], products[1]) + skip_ref[:, cols] * conv_ref[
                t, cols
            ].astype(F32)


def inner_output(conved, cum, shift_t, skip, after):
    rows, width = conved.shape
    channels = width - 2 * N
    return pl.pallas_call(
        inner_kernel,
        in_specs=[VMEM] * 4 + [ANY] * len(after),
        out_specs=VMEM,
        out_shape=shape_of((rows, channels), F32),
        scratch_shapes=[pltpu.VMEM((rows, rows), F32)],
        cost_estimate=cost(2 * rows * rows * channels, 8 * rows * width, rows * rows * channels // P_SIZE),
        name="inner",
        compiler_params=params(MAIN_MIB),
    )(conved, cum, shift_t, skip, *after)


def merge_kernel(index, place_ref, own_ref, got_ref, *refs):
    out_ref = refs[-1]
    own_log, got_log = read_logs(own_ref), read_logs(got_ref)
    own, got = own_ref[:N].astype(F32), got_ref[:N].astype(F32)
    later = place_ref[index] > 0
    own_fall = jnp.where(later, 1.0, jnp.exp(got_log))
    got_fall = jnp.where(later, jnp.exp(own_log), 1.0)
    out_ref[:N] = (own_fall * own + got_fall * got).astype(BF16)
    write_logs(out_ref, split_logs(own_log + got_log))


def merged(index, place, own, got, after):
    return pl.pallas_call(
        functools.partial(merge_kernel, index),
        in_specs=[SMEM, VMEM, VMEM] + [ANY] * len(after),
        out_specs=VMEM,
        out_shape=shape_of(own.shape, BF16),
        cost_estimate=cost(4 * own.size, 6 * own.size),
        name="merge",
        compiler_params=params(MAIN_MIB),
    )(place, own, got, *after)


def final_kernel(whole_group, rounds, place_ref, *refs):
    values, totals, lasts = refs[:EARLY], refs[EARLY:SLOTS], refs[SLOTS : 2 * SLOTS - EARLY]
    refs = refs[2 * SLOTS - EARLY :]
    gots, refs = refs[:rounds], refs[rounds:]
    y_ref, conv_ref, init_ref, cum_ref, scale_ref, gain_ref = refs[:6]
    outs = refs[6:]
    part, channels = totals[0].shape
    slot = place_ref[0]
    hits = head_spread(channels // P_SIZE)
    state = jnp.zeros((N, channels), F32)
    log = jnp.zeros((1, channels), F32)
    for i, got in enumerate(gots):
        later = place_ref[2 + i] > 0
        state = state + jnp.where(later, jnp.exp(log), 0.0) * got[:N].astype(F32)
        log = log + jnp.where(later, read_logs(got), 0.0)
    state = state.astype(BF16)
    init = init_ref[...].astype(BF16)
    init_fall = jnp.exp(log)
    nt = (((1,), (1,)), ((), ()))
    for k, value in enumerate(quarter_values(values, totals, lasts, scale_ref[...])):
        at = pl.ds(pl.multiple_of((slot ^ k) * part, part), part)
        c_part = conv_ref[at, channels + N :]
        carried = dot32(c_part, state)
        carried = carried + init_fall * lax.dot_general(c_part, init, nt, preferred_element_type=F32)
        y = y_ref[at] + carried * spread_heads(jnp.exp(cum_ref[at]), hits)
        gated = y * silu(value.astype(F32))
        squares = jnp.sum(gated * gated, axis=1, keepdims=True)
        if whole_group:
            meansq = squares / (H // G * P_SIZE)
            outs[0][at] = (gated * lax.rsqrt(meansq + 1e-05) * gain_ref[...]).astype(BF16)
        else:
            outs[0][at] = gated
            outs[1][at] = jnp.broadcast_to(squares, (part, LANES))


def final_output(whole_group, place, values, totals, lasts, gots, y, conved, init, cum, scale, gain):
    rows, channels = y.shape
    if whole_group:
        outs = [shape_of((rows, channels), BF16)]
    else:
        outs = [shape_of((rows, channels), F32), shape_of((rows, LANES), F32)]
    return pl.pallas_call(
        functools.partial(final_kernel, whole_group, len(gots)),
        in_specs=[SMEM] + [VMEM] * (2 * SLOTS - EARLY + 6 + len(gots)),
        out_specs=[VMEM] * len(outs),
        out_shape=outs,
        cost_estimate=cost(2 * rows * channels * N, 12 * rows * channels, 2 * rows * channels),
        name="final",
        compiler_params=params(MAIN_MIB),
    )(place, *values, *totals, *lasts, *gots, y, conved, init, cum, scale, gain)


def body(
    tokens,
    w_zx,
    zx_scale,
    w_bc,
    bc_scale,
    w_dt,
    conv_x,
    conv_bc,
    tail_x,
    tail_bc,
    head_params,
    init_state,
    norm_gain,
):
    tok_rows = tokens.shape[0]
    depth = w_zx.shape[0]
    local_heads = head_params.shape[1]
    channels = local_heads * P_SIZE
    per_group = H // G
    n_ctx = lax.axis_size("ctx")
    me = lax.axis_index("ctx")
    head_place = lax.axis_index("head")
    group_index = head_place * local_heads // per_group
    bits = [1 << i for i in range(n_ctx.bit_length() - 1)]
    part = tok_rows // SLOTS
    slot = head_place % SLOTS
    later = [((me & bit) > 0).astype(jnp.int32) for bit in bits]
    place = jnp.stack([slot.astype(jnp.int32), me.astype(jnp.int32)] + later)

    dt_t = w_dt.T
    if local_heads % EDGE:
        dt_t = jnp.pad(dt_t, ((0, EDGE - local_heads % EDGE), (0, 0)))
    payloads = pack(place, tokens, dt_t, n_ctx)
    payloads = [swapped(one, "ctx", j) for j, one in enumerate(payloads, 1)]
    w_all = jnp.transpose(w_zx, (1, 0, 2))
    bc_rows = pick_group(w_bc, group_index, 1)
    gate_w = w_all[0]
    first_w = jnp.concatenate([w_all[1], bc_rows], 1)
    fetched = join(payloads, part, (w_all, first_w))
    from_chip = swapped(fetched, "head", 2)
    from_core = swapped(fetched, "head", 1)


    own_rows = lax.dynamic_slice_in_dim(tokens, me * depth, depth, 1)

    def quarter(k, rows):
        order = bits if k in (0, 3) else bits[::-1]
        own = lax.dynamic_slice_in_dim(own_rows, (slot ^ k) * part, part, 0)
        first = gate = [own, *rows]
        if k == 0:
            gate = [own, *[one[:part] for one in rows]]
            first = [jnp.concatenate([own, own_rows[tok_rows - EDGE :]], 0), *rows]
        return Reduction(first, order, first_w), Reduction(gate, order, gate_w)

    def blocks_of(rows):
        return [rows[i * part : (i + 1) * part] for i in range(n_ctx - 1)]

    first0, gate0 = quarter(0, [one[: part + EDGE] for one in payloads])
    first1, gate1 = quarter(1, blocks_of(from_core))
    mark = first0.send(fetched)
    mark = first1.send(mark)
    mark = gate0.send(mark)
    mark = gate1.send(mark)
    shift_t, cum, fade, logs = step_sizes(place, tokens, dt_t, payloads, head_params.T, (mark,))
    mark = first0.keep(cum)
    mark = first1.keep(mark)
    mark = gate0.keep(mark)
    mark = gate1.keep(mark)
    scale = jnp.concatenate([zx_scale[1], pick_group(bc_scale, group_index, 0)], 0)[None]
    firsts01 = finish(
        "fin_first", (first0.total, first1.total), (first0.last, first1.last), scale, (mark,)
    )
    mark = firsts01[0]
    arrived = passed_along(firsts01[0][part:], "ctx", 1)
    from_both = swapped(chained([from_chip], mark)[0], "head", 1)
    first2, gate2 = quarter(2, blocks_of(from_chip))
    first3, gate3 = quarter(3, blocks_of(from_both))
    mark = first2.send(mark)
    mark = first3.send(mark)
    gates01 = finish("fin_gate", (gate0.total, gate1.total), (gate0.last, gate1.last), zx_scale[0:1], (mark,))
    mark = gates01[0]
    mark = first2.keep(mark)
    mark = first3.keep(mark)
    mark = gate2.send(mark)
    mark = gate3.send(mark)

    taps = jnp.concatenate([conv_x, pick_group(conv_bc, group_index, 1)], 1)
    before = jnp.concatenate([tail_x, pick_group(tail_bc, group_index, 1)], 1)
    before = jnp.pad(before, ((EDGE - (K - 1), 0), (0, 0)))
    conved, local_state = conv_and_state(
        place, firsts01, (first2.total, first3.total), (first2.last, first3.last), arrived, before, scale, taps, fade, logs, (mark,)
    )
    mark = gate2.keep(conved)
    mark = gate3.keep(mark)
    y_local = inner_output(conved, cum, shift_t, jnp.repeat(head_params[2], P_SIZE)[None], (mark,))

    run, gots = local_state, []
    for i, bit in enumerate(bits):
        if bit == bits[-1]:
            gots.append(passed_along(run, "ctx", bit))
        else:
            gots.append(swapped(run, "ctx", bit))
            run = merged(2 + i, place, run, gots[-1], (mark,))

    whole_group = local_heads >= per_group
    outs = final_output(
        whole_group,
        place,
        gates01,
        (gate2.total, gate3.total),
        (gate2.last, gate3.last),
        gots,
        y_local,
        conved,
        init_state.reshape(channels, N),
        cum,
        zx_scale[0:1],
        norm_gain[None],
    )
    if whole_group:
        return outs[0]
    gated, squares = outs
    slot_hits = (jnp.arange(G) == group_index).astype(F32)
    group_sums = lax.psum(slot_hits[:, None] * squares[:, 0][None, :], "head")
    totals = lax.dynamic_index_in_dim(group_sums, group_index, 0, keepdims=False)
    meansq = totals / (per_group * P_SIZE)
    return (gated * lax.rsqrt(meansq + 1e-05)[:, None] * norm_gain).astype(BF16)


def solution(mesh):
    return jax.shard_map(
        body,
        mesh=mesh,
        in_specs=(
            P("ctx", None),
            P("ctx", None, "head"),
            P(None, "head"),
            P("ctx", None, None),
            P(),
            P("ctx", "head"),
            P(None, "head"),
            P(),
            P(None, "head"),
            P(),
            P(None, "head"),
            P("head", None, None),
            P("head"),
        ),
        out_specs=P("ctx", "head"),
        check_vma=False,
    )
```

```python
import functools
import jax
import jax.numpy as jnp
from jax import lax
from jax.experimental import pallas as pl
from jax.experimental.pallas import tpu as pltpu
from jax.sharding import PartitionSpec as P

H = 128
P_SIZE = 64
N = 256
G = 8
K = 4
SLOTS = 4
LANES = 128
EDGE = 16
LOG_ROWS = 16
LOG_PARTS = 3
EARLY = 2
MIB = 1 << 20
MAIN_MIB = 32
SCALE = 64
BF16 = jnp.bfloat16
F32 = jnp.float32
VMEM = pl.BlockSpec(memory_space=pltpu.VMEM)
SMEM = pl.BlockSpec(memory_space=pltpu.SMEM)
ANY = pl.BlockSpec(memory_space=pl.ANY)


def shape_of(shape, dtype):
    return jax.ShapeDtypeStruct(shape, dtype)


def params(mib):
    return pltpu.CompilerParams(vmem_limit_bytes=mib * MIB)


def cost(flops, moved, transcendentals=0):
    return pl.CostEstimate(
        flops=int(flops) // SCALE, bytes_accessed=int(moved) // SCALE, transcendentals=int(transcendentals) // SCALE
    )


def chained(values, after):
    return lax.optimization_barrier((*values, after))[: len(values)]


def passed_along(x, axis, by):
    length = lax.axis_size(axis)
    pairs = [(i, i + by) for i in range(length) if 0 <= i + by < length]
    return lax.ppermute(x, axis, pairs)


def swapped(x, axis, by):
    length = lax.axis_size(axis)
    return lax.ppermute(x, axis, [(i, i ^ by) for i in range(length)])


def pick_group(values, group_index, axis_index):
    return lax.dynamic_index_in_dim(values, group_index, axis_index, keepdims=False)


def dot32(a, b):
    return jnp.dot(a, b, preferred_element_type=F32)


def silu(v):
    return v / (1.0 + jnp.exp(-v))


def pack_kernel(n, place_ref, *refs):
    blocks, tails, dt_ref, outs = refs[: n - 1], refs[n - 1 : 2 * n - 2], refs[2 * n - 2], refs[2 * n - 1 :]
    part, edge = blocks[0].shape[0], tails[0].shape[0]
    for block, tail, out in zip(blocks, tails, outs):
        out[:part] = block[...]
        out[part : part + edge] = tail[...]
        out[part + edge :] = dt_ref[...]


def pack(place, tokens, dt_t, n):
    dt_rows, depth = dt_t.shape
    part = tokens.shape[0] // SLOTS
    height = part + EDGE + dt_rows
    last = tokens.shape[0] // EDGE - 1
    return pl.pallas_call(
        functools.partial(pack_kernel, n),
        grid_spec=pltpu.PrefetchScalarGridSpec(
            num_scalar_prefetch=1,
            grid=(1,),
            in_specs=[
                pl.BlockSpec((part, depth), lambda i, place, j=j: (place[0], place[1] ^ j))
                for j in range(1, n)
            ]
            + [pl.BlockSpec((EDGE, depth), lambda i, place, j=j: (last, place[1] ^ j)) for j in range(1, n)]
            + [pl.BlockSpec((dt_rows, depth), lambda i, place: (0, 0))],
            out_specs=[pl.BlockSpec((height, depth), lambda i, place: (0, 0))] * (n - 1),
        ),
        out_shape=[shape_of((height, depth), BF16)] * (n - 1),
        name="pack",
        compiler_params=params(58),
    )(place, *[tokens] * (2 * n - 2), dt_t)


def join_kernel(part, count, *refs):
    blocks, out = refs[:count], refs[-1]
    for i, block in enumerate(blocks):
        out[i * part : (i + 1) * part] = block[:part]


def join(blocks, part, after):
    depth = blocks[0].shape[1]
    return pl.pallas_call(
        functools.partial(join_kernel, part, len(blocks)),
        in_specs=[VMEM] * len(blocks) + [ANY] * len(after),
        out_specs=VMEM,
        out_shape=shape_of((part * len(blocks), depth), BF16),
        name="join",
        compiler_params=params(MAIN_MIB),
    )(*blocks, *after)


class Reduction:
    def __init__(self, blocks, order, weights):
        self.blocks, self.order, self.weights = blocks, order, weights
        self.part = blocks[0].shape[0]
        self.n = len(blocks) + 1

    def rows(self, offsets, after):
        return chained([jnp.concatenate([self.blocks[j - 1] for j in offsets], 0)], after)[0]

    def send(self, after):
        offsets = [j for j in range(self.n) if j & self.order[0]]
        out = dot32(self.rows(offsets, after), self.weights).astype(BF16)
        self.got = swapped(out, "ctx", self.order[0])
        return out

    def keep(self, own, after):
        self.blocks = [*self.blocks, own]
        kept = [j for j in range(self.n) if not j & self.order[0]]
        size = self.part
        got = [self.got[i * size : (i + 1) * size] for i in range(len(kept))]
        bit = self.order[1]
        gone = [i for i, j in enumerate(kept) if j & bit]
        stay = [i for i, j in enumerate(kept) if not j & bit]
        rows = self.rows([kept[i] for i in gone], after)
        out = (dot32(rows, self.weights) + jnp.concatenate([got[i] for i in gone], 0)).astype(BF16)
        mark = out
        arrived = swapped(out, "ctx", bit)
        rows = self.rows([kept[i] for i in stay], after)
        total = dot32(rows, self.weights) + jnp.concatenate([got[i] for i in stay], 0)
        kept = [kept[i] for i in stay]
        for bit in self.order[2:]:
            total = total + arrived.astype(F32)
            gone = [i for i, j in enumerate(kept) if j & bit]
            stay = [i for i, j in enumerate(kept) if not j & bit]
            parts = [total[i * size : (i + 1) * size] for i in range(len(kept))]
            out = jnp.concatenate([parts[i] for i in gone], 0).astype(BF16)
            total = jnp.concatenate([parts[i] for i in stay], 0)
            arrived = swapped(out, "ctx", bit)
            kept = [kept[i] for i in stay]
        self.total, self.last = total, arrived
        return mark


def finished(total, last, scale):
    return ((total + last.astype(F32)) * scale).astype(BF16)


def finish_kernel(count, *refs):
    totals, lasts, scale_ref, outs = refs[:count], refs[count : 2 * count], refs[2 * count], refs[-count:]
    for total, last, out in zip(totals, lasts, outs):
        out[...] = finished(total[...], last[...], scale_ref[...])


def finish(name, totals, lasts, scale, after):
    count = len(totals)
    return pl.pallas_call(
        functools.partial(finish_kernel, count),
        in_specs=[VMEM] * (2 * count + 1) + [ANY] * len(after),
        out_specs=[VMEM] * count,
        out_shape=[shape_of(t.shape, BF16) for t in totals],
        cost_estimate=cost(4 * count * totals[0].size, 8 * count * totals[0].size),
        name=name,
        compiler_params=params(MAIN_MIB),
    )(*totals, *lasts, scale, *after)


def quarter_values(values, totals, lasts, scale):
    early = [v[...] for v in values]
    return early + [finished(t[...], l[...], scale) for t, l in zip(totals, lasts)]


def step_kernel(n, me_ref, tok_ref, *refs):
    weights, heads_ref = refs[:n], refs[n]
    shift_t_ref, cum_ref, fade_ref, log_ref, acc = refs[-5:]
    j = pl.program_id(0)

    @pl.when(j == 0)
    def _():
        acc[...] = jnp.zeros_like(acc)

    for i in range(n):

        @pl.when(j == i)
        def _():
            acc[...] += lax.dot_general(
                weights[i][...], tok_ref[...], (((1,), (1,)), ((), ())), preferred_element_type=F32
            )

    @pl.when(j == pl.num_programs(0) - 1)
    def _():
        v = acc[: heads_ref.shape[0]] + heads_ref[:, 0:1]
        step = jnp.maximum(v, 0.0) + jnp.log1p(jnp.exp(-jnp.abs(v)))
        rate = -jnp.exp(heads_ref[:, 1:2]) * step
        rows = rate.shape[1]
        up_to = lax.broadcasted_iota(jnp.int32, (rows, rows), 0) <= lax.broadcasted_iota(
            jnp.int32, (rows, rows), 1
        )
        cum = jnp.dot(
            rate, up_to.astype(F32), precision=lax.Precision.HIGHEST, preferred_element_type=F32
        )
        last = cum[:, rows - 1 : rows]
        shift_t_ref[...] = cum - jnp.log(step)
        cum_ref[...] = cum.T
        fade_ref[...] = (jnp.exp(last - cum) * step).T
        log_ref[...] = jnp.broadcast_to(last.T, log_ref.shape)


def step_sizes(place, tokens, dt_t, payloads, heads, after):
    dt_rows, depth = dt_t.shape
    local_heads = heads.shape[0]
    n = len(payloads) + 1
    rows = tokens.shape[0]
    last = payloads[0].shape[0] // dt_rows - 1
    whole = lambda shape: pl.BlockSpec(shape, lambda j, place: (0, 0))
    return pl.pallas_call(
        functools.partial(step_kernel, n),
        grid_spec=pltpu.PrefetchScalarGridSpec(
            num_scalar_prefetch=1,
            grid=(n,),
            in_specs=[
                pl.BlockSpec((rows, depth), lambda j, place: (0, place[1] ^ j)),
                whole((dt_rows, depth)),
            ]
            + [pl.BlockSpec((dt_rows, depth), lambda j, place: (last, 0))] * (n - 1)
            + [whole((local_heads, 3))]
            + [ANY] * len(after),
            out_specs=[
                whole((local_heads, rows)),
                whole((rows, local_heads)),
                whole((rows, local_heads)),
                whole((8, local_heads)),
            ],
            scratch_shapes=[pltpu.VMEM((dt_rows, rows), F32)],
        ),
        out_shape=[
            shape_of((local_heads, rows), F32),
            shape_of((rows, local_heads), F32),
            shape_of((rows, local_heads), F32),
            shape_of((8, local_heads), F32),
        ],
        cost_estimate=cost(2 * n * rows * depth * LANES, 2 * n * rows * depth),
        name="steps",
        compiler_params=params(MAIN_MIB),
    )(place, tokens, dt_t, *payloads, heads, *after)


def write_logs(state_ref, parts):
    rows = lax.broadcasted_iota(jnp.int32, (LOG_ROWS, state_ref.shape[1]), 0)
    block = jnp.zeros((LOG_ROWS, state_ref.shape[1]), F32)
    for i, one in enumerate(parts):
        block = jnp.where(rows == i, one, block)
    state_ref[N:] = block.astype(BF16)


def read_logs(state_ref):
    block = state_ref[N:].astype(F32)
    return sum(block[i : i + 1] for i in range(LOG_PARTS))


def split_logs(logs):
    parts = []
    for _ in range(LOG_PARTS):
        parts.append(logs.astype(BF16).astype(F32))
        logs = logs - parts[-1]
    return parts


def head_spread(local_heads):
    channels = local_heads * P_SIZE
    hit = (
        lax.broadcasted_iota(jnp.int32, (local_heads, channels), 1) // P_SIZE
        == lax.broadcasted_iota(jnp.int32, (local_heads, channels), 0)
    )
    return hit.astype(F32).astype(BF16)


def spread_heads(values, hits):
    high = values.astype(BF16)
    low = (values - high.astype(F32)).astype(BF16)
    return dot32(high, hits) + dot32(low, hits)


def conv_kernel(place_ref, *refs):
    values, totals, lasts = refs[:EARLY], refs[EARLY:SLOTS], refs[SLOTS : 2 * SLOTS - EARLY]
    arrived_ref, before_ref, scale_ref, taps_ref, fade_ref, log_ref = refs[2 * SLOTS - EARLY : 2 * SLOTS - EARLY + 6]
    conv_ref, state_ref, vals = refs[-3:]
    part, width = totals[0].shape
    rows = part * SLOTS
    channels = width - 2 * N
    slot = place_ref[0]
    first = place_ref[1] == 0
    vals[:EDGE] = jnp.where(first, before_ref[...].astype(F32), arrived_ref[...].astype(F32))
    for k, value in enumerate(quarter_values(values, totals, lasts, scale_ref[...])):
        start = pl.multiple_of(EDGE + (slot ^ k) * part, EDGE)
        vals[pl.ds(start, part)] = value[:part].astype(F32)
    for c in range(0, width, 2 * LANES):
        cols = slice(c, c + 2 * LANES)
        for r in range(0, rows, part):
            summed = taps_ref[K : K + 1, cols]
            for tap in range(K):
                at = r + EDGE - (K - 1) + tap
                summed = summed + taps_ref[tap : tap + 1, cols] * vals[at : at + part, cols]
            conv_ref[r : r + part, cols] = silu(summed).astype(BF16)
    hits = head_spread(channels // P_SIZE)
    faded = spread_heads(fade_ref[...], hits) * conv_ref[:, :channels].astype(F32)
    state_ref[:N] = lax.dot_general(
        conv_ref[:, channels : channels + N],
        faded.astype(BF16),
        (((0,), (0,)), ((), ())),
        preferred_element_type=F32,
    ).astype(BF16)
    left, parts = log_ref[...], []
    for _ in range(LOG_PARTS):
        parts.append(left.astype(BF16))
        left = left - parts[-1].astype(F32)
    spread = [dot32(one, hits)[0:1] for one in parts]
    write_logs(state_ref, spread)


def conv_and_state(place, values, totals, lasts, arrived, before, scale, taps, fade, logs, after):
    part, width = totals[0].shape
    rows = part * SLOTS
    return pl.pallas_call(
        conv_kernel,
        in_specs=[SMEM] + [VMEM] * (2 * SLOTS - EARLY + 6) + [ANY] * len(after),
        out_specs=[VMEM, VMEM],
        out_shape=[shape_of((rows, width), BF16), shape_of((N + LOG_ROWS, width - 2 * N), BF16)],
        scratch_shapes=[pltpu.VMEM((rows + EDGE, width), F32)],
        cost_estimate=cost(30 * rows * width, 12 * rows * width, 2 * rows * width),
        name="conv",
        compiler_params=params(MAIN_MIB),
    )(place, *values, *totals, *lasts, arrived, before, scale, taps, fade, logs, *after)


def inner_kernel(conv_ref, cum_ref, shift_t_ref, skip_ref, *refs):
    y_ref, scores = refs[-2:]
    rows, width = conv_ref.shape
    channels = width - 2 * N
    size = LANES
    blocks = rows // size
    nt = (((1,), (1,)), ((), ()))
    scores[...] = lax.dot_general(
        conv_ref[:, channels + N :], conv_ref[:, channels : channels + N], nt, preferred_element_type=F32
    )
    lower = lax.broadcasted_iota(jnp.int32, (size, size), 0) >= lax.broadcasted_iota(
        jnp.int32, (size, size), 1
    )
    left = lax.broadcasted_iota(jnp.int32, (size, 2 * P_SIZE), 1) < P_SIZE
    for pair in range(channels // (2 * P_SIZE)):
        cols = slice(pair * 2 * P_SIZE, (pair + 1) * 2 * P_SIZE)
        for a in range(blocks):
            t = slice(a * size, (a + 1) * size)
            products = []
            for h in (2 * pair, 2 * pair + 1):
                here = cum_ref[t, h : h + 1]
                own = jnp.where(lower, here - shift_t_ref[h : h + 1, t], -jnp.inf)
                weights = jnp.exp(own) * scores[t, t]
                if a > 0:
                    before = slice(0, a * size)
                    earlier = jnp.exp(here - shift_t_ref[h : h + 1, before]) * scores[t, before]
                    weights = jnp.concatenate([earlier, weights], 1)
                products.append(dot32(weights.astype(BF16), conv_ref[: (a + 1) * size, cols]))
            y_ref[t, cols] = jnp.where(left, products[0], products[1]) + skip_ref[:, cols] * conv_ref[
                t, cols
            ].astype(F32)


def inner_output(conved, cum, shift_t, skip, after):
    rows, width = conved.shape
    channels = width - 2 * N
    return pl.pallas_call(
        inner_kernel,
        in_specs=[VMEM] * 4 + [ANY] * len(after),
        out_specs=VMEM,
        out_shape=shape_of((rows, channels), F32),
        scratch_shapes=[pltpu.VMEM((rows, rows), F32)],
        cost_estimate=cost(2 * rows * rows * channels, 8 * rows * width, rows * rows * channels // P_SIZE),
        name="inner",
        compiler_params=params(MAIN_MIB),
    )(conved, cum, shift_t, skip, *after)


def merge_kernel(index, place_ref, own_ref, got_ref, *refs):
    out_ref = refs[-1]
    own_log, got_log = read_logs(own_ref), read_logs(got_ref)
    own, got = own_ref[:N].astype(F32), got_ref[:N].astype(F32)
    later = place_ref[index] > 0
    own_fall = jnp.where(later, 1.0, jnp.exp(got_log))
    got_fall = jnp.where(later, jnp.exp(own_log), 1.0)
    out_ref[:N] = (own_fall * own + got_fall * got).astype(BF16)
    write_logs(out_ref, split_logs(own_log + got_log))


def merged(index, place, own, got, after):
    return pl.pallas_call(
        functools.partial(merge_kernel, index),
        in_specs=[SMEM, VMEM, VMEM] + [ANY] * len(after),
        out_specs=VMEM,
        out_shape=shape_of(own.shape, BF16),
        cost_estimate=cost(4 * own.size, 6 * own.size),
        name="merge",
        compiler_params=params(MAIN_MIB),
    )(place, own, got, *after)


def final_kernel(whole_group, rounds, place_ref, *refs):
    values, totals, lasts = refs[:EARLY], refs[EARLY:SLOTS], refs[SLOTS : 2 * SLOTS - EARLY]
    refs = refs[2 * SLOTS - EARLY :]
    gots, refs = refs[:rounds], refs[rounds:]
    y_ref, conv_ref, init_ref, cum_ref, scale_ref, gain_ref = refs[:6]
    outs = refs[6:]
    part, channels = totals[0].shape
    slot = place_ref[0]
    hits = head_spread(channels // P_SIZE)
    state = jnp.zeros((N, channels), F32)
    log = jnp.zeros((1, channels), F32)
    for i, got in enumerate(gots):
        later = place_ref[2 + i] > 0
        state = state + jnp.where(later, jnp.exp(log), 0.0) * got[:N].astype(F32)
        log = log + jnp.where(later, read_logs(got), 0.0)
    state = state.astype(BF16)
    init = init_ref[...].astype(BF16)
    init_fall = jnp.exp(log)
    nt = (((1,), (1,)), ((), ()))
    for k, value in enumerate(quarter_values(values, totals, lasts, scale_ref[...])):
        at = pl.ds(pl.multiple_of((slot ^ k) * part, part), part)
        c_part = conv_ref[at, channels + N :]
        carried = dot32(c_part, state)
        carried = carried + init_fall * lax.dot_general(c_part, init, nt, preferred_element_type=F32)
        y = y_ref[at] + carried * spread_heads(jnp.exp(cum_ref[at]), hits)
        gated = y * silu(value.astype(F32))
        squares = jnp.sum(gated * gated, axis=1, keepdims=True)
        if whole_group:
            meansq = squares / (H // G * P_SIZE)
            outs[0][at] = (gated * lax.rsqrt(meansq + 1e-05) * gain_ref[...]).astype(BF16)
        else:
            outs[0][at] = gated
            outs[1][at] = jnp.broadcast_to(squares, (part, LANES))


def final_output(whole_group, place, values, totals, lasts, gots, y, conved, init, cum, scale, gain):
    rows, channels = y.shape
    if whole_group:
        outs = [shape_of((rows, channels), BF16)]
    else:
        outs = [shape_of((rows, channels), F32), shape_of((rows, LANES), F32)]
    return pl.pallas_call(
        functools.partial(final_kernel, whole_group, len(gots)),
        in_specs=[SMEM] + [VMEM] * (2 * SLOTS - EARLY + 6 + len(gots)),
        out_specs=[VMEM] * len(outs),
        out_shape=outs,
        cost_estimate=cost(2 * rows * channels * N, 12 * rows * channels, 2 * rows * channels),
        name="final",
        compiler_params=params(MAIN_MIB),
    )(place, *values, *totals, *lasts, *gots, y, conved, init, cum, scale, gain)


def body(
    tokens,
    w_zx,
    zx_scale,
    w_bc,
    bc_scale,
    w_dt,
    conv_x,
    conv_bc,
    tail_x,
    tail_bc,
    head_params,
    init_state,
    norm_gain,
):
    tok_rows = tokens.shape[0]
    depth = w_zx.shape[0]
    local_heads = head_params.shape[1]
    channels = local_heads * P_SIZE
    per_group = H // G
    n_ctx = lax.axis_size("ctx")
    me = lax.axis_index("ctx")
    head_place = lax.axis_index("head")
    group_index = head_place * local_heads // per_group
    bits = [1 << i for i in range(n_ctx.bit_length() - 1)]
    part = tok_rows // SLOTS
    slot = head_place % SLOTS
    later = [((me & bit) > 0).astype(jnp.int32) for bit in bits]
    place = jnp.stack([slot.astype(jnp.int32), me.astype(jnp.int32)] + later)

    dt_t = w_dt.T
    if local_heads % EDGE:
        dt_t = jnp.pad(dt_t, ((0, EDGE - local_heads % EDGE), (0, 0)))
    payloads = pack(place, tokens, dt_t, n_ctx)
    payloads = [swapped(one, "ctx", j) for j, one in enumerate(payloads, 1)]
    w_all = jnp.transpose(w_zx, (1, 0, 2))
    bc_rows = pick_group(w_bc, group_index, 1)
    gate_w = w_all[0]
    fetched = join(payloads, part, (gate_w, bc_rows))
    from_chip = swapped(fetched, "head", 2)
    from_core = swapped(fetched, "head", 1)

    def blocks_of(rows):
        return [rows[i * part : (i + 1) * part] for i in range(n_ctx - 1)]

    gate0 = Reduction([one[:part] for one in payloads], bits, gate_w)
    gate1 = Reduction(blocks_of(from_core), bits[::-1], gate_w)
    mark = gate0.send(fetched)
    mark = gate1.send(mark)
    first_w = jnp.concatenate([w_all[1], chained([bc_rows], mark)[0]], 1)
    first0 = Reduction([one[: part + EDGE] for one in payloads], bits, first_w)
    first1 = Reduction(blocks_of(from_core), bits[::-1], first_w)
    mark = first0.send(mark)
    mark = first1.send(mark)
    own_rows = lax.dynamic_slice_in_dim(chained([tokens], mark)[0], me * depth, depth, 1)
    own = [lax.dynamic_slice_in_dim(own_rows, (slot ^ k) * part, part, 0) for k in range(SLOTS)]
    shift_t, cum, fade, logs = step_sizes(place, tokens, dt_t, payloads, head_params.T, (mark,))
    mark = gate0.keep(own[0], cum)
    mark = gate1.keep(own[1], mark)
    mark = first0.keep(jnp.concatenate([own[0], own_rows[tok_rows - EDGE :]], 0), mark)
    mark = first1.keep(own[1], mark)
    gates01 = finish("fin_gate", (gate0.total, gate1.total), (gate0.last, gate1.last), zx_scale[0:1], (mark,))
    mark = gates01[0]
    from_both = swapped(chained([from_chip], mark)[0], "head", 1)
    first2, gate2 = (Reduction(blocks_of(from_chip), bits[::-1], w) for w in (first_w, gate_w))
    first3, gate3 = (Reduction(blocks_of(from_both), bits, w) for w in (first_w, gate_w))
    mark = first2.send(mark)
    mark = first3.send(mark)
    scale = jnp.concatenate([zx_scale[1], pick_group(bc_scale, group_index, 0)], 0)[None]
    firsts01 = finish(
        "fin_first", (first0.total, first1.total), (first0.last, first1.last), scale, (mark,)
    )
    mark = firsts01[0]
    arrived = passed_along(firsts01[0][part:], "ctx", 1)
    mark = first2.keep(own[2], mark)
    mark = first3.keep(own[3], mark)
    mark = gate2.send(mark)
    mark = gate3.send(mark)

    taps = jnp.concatenate([conv_x, pick_group(conv_bc, group_index, 1)], 1)
    before = jnp.concatenate([tail_x, pick_group(tail_bc, group_index, 1)], 1)
    before = jnp.pad(before, ((EDGE - (K - 1), 0), (0, 0)))
    conved, local_state = conv_and_state(
        place, firsts01, (first2.total, first3.total), (first2.last, first3.last), arrived, before, scale, taps, fade, logs, (mark,)
    )
    mark = gate2.keep(own[2], conved)
    mark = gate3.keep(own[3], mark)
    y_local = inner_output(conved, cum, shift_t, jnp.repeat(head_params[2], P_SIZE)[None], (mark,))

    run, gots = local_state, []
    for i, bit in enumerate(bits):
        if bit == bits[-1]:
            gots.append(passed_along(run, "ctx", bit))
        else:
            gots.append(swapped(run, "ctx", bit))
            run = merged(2 + i, place, run, gots[-1], (mark,))

    whole_group = local_heads >= per_group
    outs = final_output(
        whole_group,
        place,
        gates01,
        (gate2.total, gate3.total),
        (gate2.last, gate3.last),
        gots,
        y_local,
        conved,
        init_state.reshape(channels, N),
        cum,
        zx_scale[0:1],
        norm_gain[None],
    )
    if whole_group:
        return outs[0]
    gated, squares = outs
    slot_hits = (jnp.arange(G) == group_index).astype(F32)
    group_sums = lax.psum(slot_hits[:, None] * squares[:, 0][None, :], "head")
    totals = lax.dynamic_index_in_dim(group_sums, group_index, 0, keepdims=False)
    meansq = totals / (per_group * P_SIZE)
    return (gated * lax.rsqrt(meansq + 1e-05)[:, None] * norm_gain).astype(BF16)


def solution(mesh):
    return jax.shard_map(
        body,
        mesh=mesh,
        in_specs=(
            P("ctx", None),
            P("ctx", None, "head"),
            P(None, "head"),
            P("ctx", None, None),
            P(),
            P("ctx", "head"),
            P(None, "head"),
            P(),
            P(None, "head"),
            P(),
            P(None, "head"),
            P("head", None, None),
            P("head"),
        ),
        out_specs=P("ctx", "head"),
        check_vma=False,
    )
```

```python
import functools
import jax
import jax.numpy as jnp
from jax import lax
from jax.experimental import pallas as pl
from jax.experimental.pallas import tpu as pltpu
from jax.sharding import PartitionSpec as P

H = 128
P_SIZE = 64
N = 256
G = 8
K = 4
SLOTS = 4
LANES = 128
EDGE = 16
EARLY = 2
LOG_PARTS = 3
MIB = 1 << 20
MAIN_MIB = 32
SCALE = 64
BF16 = jnp.bfloat16
F32 = jnp.float32
VMEM = pl.BlockSpec(memory_space=pltpu.VMEM)
SMEM = pl.BlockSpec(memory_space=pltpu.SMEM)
ANY = pl.BlockSpec(memory_space=pl.ANY)


def shape_of(shape, dtype):
    return jax.ShapeDtypeStruct(shape, dtype)


def params(mib):
    return pltpu.CompilerParams(vmem_limit_bytes=mib * MIB)


def cost(flops, moved, transcendentals=0):
    return pl.CostEstimate(
        flops=int(flops) // SCALE, bytes_accessed=int(moved) // SCALE, transcendentals=int(transcendentals) // SCALE
    )


def chained(values, after):
    return lax.optimization_barrier((*values, after))[: len(values)]


def passed_along(x, axis, by):
    length = lax.axis_size(axis)
    pairs = [(i, i + by) for i in range(length) if 0 <= i + by < length]
    return lax.ppermute(x, axis, pairs)


def swapped(x, axis, by):
    length = lax.axis_size(axis)
    return lax.ppermute(x, axis, [(i, i ^ by) for i in range(length)])


def pick_group(values, group_index, axis_index):
    return lax.dynamic_index_in_dim(values, group_index, axis_index, keepdims=False)


def dot32(a, b):
    return jnp.dot(a, b, preferred_element_type=F32)


def silu(v):
    return v / (1.0 + jnp.exp(-v))


def pack_kernel(n, place_ref, *refs):
    blocks, tails, dt_ref, outs = refs[: n - 1], refs[n - 1 : 2 * n - 2], refs[2 * n - 2], refs[2 * n - 1 :]
    part, edge = blocks[0].shape[0], tails[0].shape[0]
    for block, tail, out in zip(blocks, tails, outs):
        out[:part] = block[...]
        out[part : part + edge] = tail[...]
        out[part + edge :] = dt_ref[...]


def pack(place, tokens, dt_t, n):
    dt_rows, depth = dt_t.shape
    part = tokens.shape[0] // SLOTS
    height = part + EDGE + dt_rows
    last = tokens.shape[0] // EDGE - 1
    return pl.pallas_call(
        functools.partial(pack_kernel, n),
        grid_spec=pltpu.PrefetchScalarGridSpec(
            num_scalar_prefetch=1,
            grid=(1,),
            in_specs=[
                pl.BlockSpec((part, depth), lambda i, place, j=j: (place[0], place[1] ^ j))
                for j in range(1, n)
            ]
            + [pl.BlockSpec((EDGE, depth), lambda i, place, j=j: (last, place[1] ^ j)) for j in range(1, n)]
            + [pl.BlockSpec((dt_rows, depth), lambda i, place: (0, 0))],
            out_specs=[pl.BlockSpec((height, depth), lambda i, place: (0, 0))] * (n - 1),
        ),
        out_shape=[shape_of((height, depth), BF16)] * (n - 1),
        name="pack",
        compiler_params=params(58),
    )(place, *[tokens] * (2 * n - 2), dt_t)


def join_kernel(part, count, *refs):
    blocks, out = refs[:count], refs[-1]
    for i, block in enumerate(blocks):
        out[i * part : (i + 1) * part] = block[:part]


def join(blocks, part, after):
    depth = blocks[0].shape[1]
    return pl.pallas_call(
        functools.partial(join_kernel, part, len(blocks)),
        in_specs=[VMEM] * len(blocks) + [ANY] * len(after),
        out_specs=VMEM,
        out_shape=shape_of((part * len(blocks), depth), BF16),
        name="join",
        compiler_params=params(MAIN_MIB),
    )(*blocks, *after)


class Reduction:
    def __init__(self, blocks, order, weights):
        self.blocks, self.order, self.weights = blocks, order, weights
        self.part = blocks[0].shape[0]
        self.n = len(blocks) + 1

    def rows(self, offsets, after):
        return chained([jnp.concatenate([self.blocks[j - 1] for j in offsets], 0)], after)[0]

    def send(self, after, extra=None):
        offsets = [j for j in range(self.n) if j & self.order[0]]
        out = dot32(self.rows(offsets, after), self.weights).astype(BF16)
        self.extra = extra
        if extra is not None:
            out = jnp.concatenate([out, extra], 0)
        self.got = swapped(out, "ctx", self.order[0])
        return out

    def keep(self, own, after):
        self.blocks = [*self.blocks, own]
        kept = [j for j in range(self.n) if not j & self.order[0]]
        size = self.part
        got = [self.got[i * size : (i + 1) * size] for i in range(len(kept))]
        bit = self.order[1]
        gone = [i for i, j in enumerate(kept) if j & bit]
        stay = [i for i, j in enumerate(kept) if not j & bit]
        rows = self.rows([kept[i] for i in gone], after)
        out = (dot32(rows, self.weights) + jnp.concatenate([got[i] for i in gone], 0)).astype(BF16)
        mark = out
        if self.extra is not None:
            out = jnp.concatenate([out, self.extra, self.got[size * len(kept) :]], 0)
        arrived = swapped(out, "ctx", bit)
        rows = self.rows([kept[i] for i in stay], after)
        total = dot32(rows, self.weights) + jnp.concatenate([got[i] for i in stay], 0)
        kept = [kept[i] for i in stay]
        for bit in self.order[2:]:
            total = total + arrived.astype(F32)
            gone = [i for i, j in enumerate(kept) if j & bit]
            stay = [i for i, j in enumerate(kept) if not j & bit]
            parts = [total[i * size : (i + 1) * size] for i in range(len(kept))]
            out = jnp.concatenate([parts[i] for i in gone], 0).astype(BF16)
            total = jnp.concatenate([parts[i] for i in stay], 0)
            arrived = swapped(out, "ctx", bit)
            kept = [kept[i] for i in stay]
        self.total, self.last = total, arrived
        return mark


def finished(total, last, scale):
    return ((total + last.astype(F32)) * scale).astype(BF16)


def finish_kernel(count, *refs):
    totals, lasts, scale_ref, outs = refs[:count], refs[count : 2 * count], refs[2 * count], refs[-count:]
    for total, last, out in zip(totals, lasts, outs):
        out[...] = finished(total[...], last[: total.shape[0]], scale_ref[...])


def finish(name, totals, lasts, scale, after):
    count = len(totals)
    return pl.pallas_call(
        functools.partial(finish_kernel, count),
        in_specs=[VMEM] * (2 * count + 1) + [ANY] * len(after),
        out_specs=[VMEM] * count,
        out_shape=[shape_of(t.shape, BF16) for t in totals],
        cost_estimate=cost(4 * count * totals[0].size, 8 * count * totals[0].size),
        name=name,
        compiler_params=params(MAIN_MIB),
    )(*totals, *lasts, scale, *after)


def quarter_values(values, totals, lasts, scale):
    early = [v[...] for v in values]
    return early + [finished(t[...], l[...], scale) for t, l in zip(totals, lasts)]


def step_kernel(n, me_ref, tok_ref, *refs):
    weights, heads_ref = refs[:n], refs[n]
    shift_t_ref, cum_ref, fade_ref, log_ref, acc = refs[-5:]
    j = pl.program_id(0)

    @pl.when(j == 0)
    def _():
        acc[...] = jnp.zeros_like(acc)

    for i in range(n):

        @pl.when(j == i)
        def _():
            acc[...] += lax.dot_general(
                weights[i][...], tok_ref[...], (((1,), (1,)), ((), ())), preferred_element_type=F32
            )

    @pl.when(j == pl.num_programs(0) - 1)
    def _():
        v = acc[: heads_ref.shape[0]] + heads_ref[:, 0:1]
        step = jnp.maximum(v, 0.0) + jnp.log1p(jnp.exp(-jnp.abs(v)))
        rate = -jnp.exp(heads_ref[:, 1:2]) * step
        rows = rate.shape[1]
        up_to = lax.broadcasted_iota(jnp.int32, (rows, rows), 0) <= lax.broadcasted_iota(
            jnp.int32, (rows, rows), 1
        )
        cum = jnp.dot(
            rate, up_to.astype(F32), precision=lax.Precision.HIGHEST, preferred_element_type=F32
        )
        last = cum[:, rows - 1 : rows]
        shift_t_ref[...] = cum - jnp.log(step)
        cum_ref[...] = cum.T
        fade_ref[...] = (jnp.exp(last - cum) * step).T
        left = jnp.broadcast_to(last.T, (8, last.shape[0]))
        hits = head_spread(last.shape[0])
        index = lax.broadcasted_iota(jnp.int32, log_ref.shape, 0)
        block = jnp.zeros(log_ref.shape, F32)
        for i in range(LOG_PARTS):
            term = left.astype(BF16)
            left = left - term.astype(F32)
            block = jnp.where(index == i, dot32(term, hits)[0:1], block)
        log_ref[...] = block.astype(BF16)


def step_sizes(place, tokens, dt_t, payloads, heads, after):
    dt_rows, depth = dt_t.shape
    local_heads = heads.shape[0]
    n = len(payloads) + 1
    rows = tokens.shape[0]
    last = payloads[0].shape[0] // dt_rows - 1
    whole = lambda shape: pl.BlockSpec(shape, lambda j, place: (0, 0))
    return pl.pallas_call(
        functools.partial(step_kernel, n),
        grid_spec=pltpu.PrefetchScalarGridSpec(
            num_scalar_prefetch=1,
            grid=(n,),
            in_specs=[
                pl.BlockSpec((rows, depth), lambda j, place: (0, place[1] ^ j)),
                whole((dt_rows, depth)),
            ]
            + [pl.BlockSpec((dt_rows, depth), lambda j, place: (last, 0))] * (n - 1)
            + [whole((local_heads, 3))]
            + [ANY] * len(after),
            out_specs=[
                whole((local_heads, rows)),
                whole((rows, local_heads)),
                whole((rows, local_heads)),
                whole((EDGE, local_heads * P_SIZE)),
            ],
            scratch_shapes=[pltpu.VMEM((dt_rows, rows), F32)],
        ),
        out_shape=[
            shape_of((local_heads, rows), F32),
            shape_of((rows, local_heads), F32),
            shape_of((rows, local_heads), F32),
            shape_of((EDGE, local_heads * P_SIZE), BF16),
        ],
        cost_estimate=cost(2 * n * rows * depth * LANES, 2 * n * rows * depth),
        name="steps",
        compiler_params=params(MAIN_MIB),
    )(place, tokens, dt_t, *payloads, heads, *after)


def head_spread(local_heads):
    channels = local_heads * P_SIZE
    hit = (
        lax.broadcasted_iota(jnp.int32, (local_heads, channels), 1) // P_SIZE
        == lax.broadcasted_iota(jnp.int32, (local_heads, channels), 0)
    )
    return hit.astype(F32).astype(BF16)


def spread_heads(values, hits):
    high = values.astype(BF16)
    low = (values - high.astype(F32)).astype(BF16)
    return dot32(high, hits) + dot32(low, hits)


def conv_kernel(count, place_ref, *refs):
    values, totals, lasts = refs[:EARLY], refs[EARLY:SLOTS], refs[SLOTS : 2 * SLOTS - EARLY]
    arrived_ref, before_ref, scale_ref, taps_ref, fade_ref = refs[2 * SLOTS - EARLY : 2 * SLOTS - EARLY + 5]
    conv_ref, states, vals = refs[-2 - count], refs[-1 - count : -1], refs[-1]
    part, width = totals[0].shape
    rows = part * SLOTS
    channels = width - 2 * N
    slot = place_ref[0]
    first = place_ref[1] == 0
    vals[:EDGE] = jnp.where(first, before_ref[...].astype(F32), arrived_ref[...].astype(F32))
    for k, value in enumerate(quarter_values(values, totals, lasts, scale_ref[...])):
        start = pl.multiple_of(EDGE + (slot ^ k) * part, EDGE)
        vals[pl.ds(start, part)] = value[:part].astype(F32)
    for c in range(0, width, 2 * LANES):
        cols = slice(c, c + 2 * LANES)
        for r in range(0, rows, part):
            summed = taps_ref[K : K + 1, cols]
            for tap in range(K):
                at = r + EDGE - (K - 1) + tap
                summed = summed + taps_ref[tap : tap + 1, cols] * vals[at : at + part, cols]
            conv_ref[r : r + part, cols] = silu(summed).astype(BF16)
    hits = head_spread(channels // P_SIZE)
    faded = spread_heads(fade_ref[...], hits) * conv_ref[:, :channels].astype(F32)
    state = lax.dot_general(
        conv_ref[:, channels : channels + N],
        faded.astype(BF16),
        (((0,), (0,)), ((), ())),
        preferred_element_type=F32,
    ).astype(BF16)
    size = channels // len(states)
    for i, out in enumerate(states):
        out[...] = state[:, i * size : (i + 1) * size]


def conv_and_state(count, place, values, totals, lasts, arrived, before, scale, taps, fade, after):
    part, width = totals[0].shape
    rows = part * SLOTS
    return pl.pallas_call(
        functools.partial(conv_kernel, count),
        in_specs=[SMEM] + [VMEM] * (2 * SLOTS - EARLY + 5) + [ANY] * len(after),
        out_specs=[VMEM] * (1 + count),
        out_shape=[shape_of((rows, width), BF16)] + [shape_of((N, (width - 2 * N) // count), BF16)] * count,
        scratch_shapes=[pltpu.VMEM((rows + EDGE, width), F32)],
        cost_estimate=cost(30 * rows * width, 12 * rows * width, 2 * rows * width),
        name="conv",
        compiler_params=params(MAIN_MIB),
    )(place, *values, *totals, *lasts, arrived, before, scale, taps, fade, *after)


def inner_kernel(conv_ref, cum_ref, shift_t_ref, skip_ref, *refs):
    y_ref, scores = refs[-2:]
    rows, width = conv_ref.shape
    channels = width - 2 * N
    size = LANES
    blocks = rows // size
    nt = (((1,), (1,)), ((), ()))
    scores[...] = lax.dot_general(
        conv_ref[:, channels + N :], conv_ref[:, channels : channels + N], nt, preferred_element_type=F32
    )
    lower = lax.broadcasted_iota(jnp.int32, (size, size), 0) >= lax.broadcasted_iota(
        jnp.int32, (size, size), 1
    )
    left = lax.broadcasted_iota(jnp.int32, (size, 2 * P_SIZE), 1) < P_SIZE
    for pair in range(channels // (2 * P_SIZE)):
        cols = slice(pair * 2 * P_SIZE, (pair + 1) * 2 * P_SIZE)
        for a in range(blocks):
            t = slice(a * size, (a + 1) * size)
            products = []
            for h in (2 * pair, 2 * pair + 1):
                here = cum_ref[t, h : h + 1]
                own = jnp.where(lower, here - shift_t_ref[h : h + 1, t], -jnp.inf)
                weights = jnp.exp(own) * scores[t, t]
                if a > 0:
                    before = slice(0, a * size)
                    earlier = jnp.exp(here - shift_t_ref[h : h + 1, before]) * scores[t, before]
                    weights = jnp.concatenate([earlier, weights], 1)
                products.append(dot32(weights.astype(BF16), conv_ref[: (a + 1) * size, cols]))
            y_ref[t, cols] = jnp.where(left, products[0], products[1]) + skip_ref[:, cols] * conv_ref[
                t, cols
            ].astype(F32)


def inner_output(conved, cum, shift_t, skip, after):
    rows, width = conved.shape
    channels = width - 2 * N
    return pl.pallas_call(
        inner_kernel,
        in_specs=[VMEM] * 4 + [ANY] * len(after),
        out_specs=VMEM,
        out_shape=shape_of((rows, channels), F32),
        scratch_shapes=[pltpu.VMEM((rows, rows), F32)],
        cost_estimate=cost(2 * rows * rows * channels, 8 * rows * width, rows * rows * channels // P_SIZE),
        name="inner",
        compiler_params=params(MAIN_MIB),
    )(conved, cum, shift_t, skip, *after)


def falls_kernel(n, plan, place_ref, *refs):
    logs, out_ref = refs[:n], refs[-1]
    values = []
    for log in logs:
        block = log[...].astype(F32)
        values.append(sum(block[i : i + 1] for i in range(LOG_PARTS)))
    index = lax.broadcasted_iota(jnp.int32, out_ref.shape, 0)
    block = jnp.zeros(out_ref.shape, F32)
    for i, (counts, parts) in enumerate(plan(place_ref[1], n)):
        total = jnp.zeros_like(values[0])
        for present, offset in parts:
            total = total + jnp.where(present, values[offset], 0.0)
        block = jnp.where(index == i, jnp.where(counts, jnp.exp(total), 0.0), block)
    out_ref[...] = block


def falls(plan, place, logs, after):
    n = len(logs)
    channels = logs[0][0].shape[1]
    rows = -(-len(plan(0, n)) // 8) * 8
    return pl.pallas_call(
        functools.partial(falls_kernel, n, plan),
        grid_spec=pltpu.PrefetchScalarGridSpec(
            num_scalar_prefetch=1,
            grid=(1,),
            in_specs=[pl.BlockSpec((EDGE, channels), lambda i, place, at=at: (at, 0)) for _, at in logs]
            + [ANY] * len(after),
            out_specs=pl.BlockSpec((rows, channels), lambda i, place: (0, 0)),
        ),
        out_shape=shape_of((rows, channels), F32),
        name="falls",
        compiler_params=params(MAIN_MIB),
    )(place, *[array for array, _ in logs], *after)


def scan_plan(me, n):
    out, before = [], []
    bit = 1
    while bit < n:
        later = (me & bit) > 0
        own_span = [(True, j) for j in range(bit)]
        got_span = [(True, j) for j in range(bit, 2 * bit)]
        out.append((True, [(jnp.logical_not(later), j) for _, j in got_span]))
        out.append((True, [(later, j) for _, j in own_span]))
        out.append((later, list(before)))
        before += [(later, j) for _, j in got_span]
        bit *= 2
    return out + [(True, before)]


def swap_plan(me, n):
    low, high = (me & 1) > 0, (me & 2) > 0
    return [
        (jnp.logical_not(low), []),
        (high, [(jnp.logical_not(low), 0), (jnp.logical_not(low), 3)]),
        (high, [(low, 1), (jnp.logical_not(low), 3)]),
        (True, []),
        (True, []),
        (True, []),
    ]


def both_plans(me, n):
    return scan_plan(me, n) + (swap_plan(me, n) if n == 4 else [])


def merge_kernel(row, falls_ref, own_ref, got_ref, *refs):
    own_fall, got_fall = falls_ref[row : row + 1], falls_ref[row + 1 : row + 2]
    refs[-1][...] = (own_fall * own_ref[...].astype(F32) + got_fall * got_ref[...].astype(F32)).astype(BF16)


def merged(row, factors, own, got, after):
    return pl.pallas_call(
        functools.partial(merge_kernel, row),
        in_specs=[VMEM] * 3 + [ANY] * len(after),
        out_specs=VMEM,
        out_shape=shape_of(own.shape, BF16),
        cost_estimate=cost(4 * own.size, 6 * own.size),
        name="merge",
        compiler_params=params(MAIN_MIB),
    )(factors, own, got, *after)


def final_kernel(whole_group, plans, init_row, place_ref, *refs):
    rounds = sum(len(rows) for rows in plans)
    values, totals, lasts = refs[:EARLY], refs[EARLY:SLOTS], refs[SLOTS : 2 * SLOTS - EARLY]
    refs = refs[2 * SLOTS - EARLY :]
    gots, refs = refs[:rounds], refs[rounds:]
    y_ref, conv_ref, init_ref, cum_ref, scale_ref, gain_ref, falls_ref = refs[:7]
    outs = refs[7:]
    part, channels = totals[0].shape
    slot = place_ref[0]
    hits = head_spread(channels // P_SIZE)
    size = channels // len(plans)
    states = []
    for i, rows in enumerate(plans):
        cols = slice(i * size, (i + 1) * size)
        states.append(
            sum(
                falls_ref[row : row + 1, cols] * got[...].astype(F32)
                for row, got in zip(rows, gots[i * len(rows) : (i + 1) * len(rows)])
            )
        )
    state = jnp.concatenate(states, 1).astype(BF16)
    init = init_ref[...].astype(BF16)
    init_fall = falls_ref[init_row : init_row + 1]
    nt = (((1,), (1,)), ((), ()))
    for k, value in enumerate(quarter_values(values, totals, lasts, scale_ref[...])):
        at = pl.ds(pl.multiple_of((slot ^ k) * part, part), part)
        c_part = conv_ref[at, channels + N :]
        carried = dot32(c_part, state)
        carried = carried + init_fall * lax.dot_general(c_part, init, nt, preferred_element_type=F32)
        y = y_ref[at] + carried * spread_heads(jnp.exp(cum_ref[at]), hits)
        gated = y * silu(value.astype(F32))
        squares = jnp.sum(gated * gated, axis=1, keepdims=True)
        if whole_group:
            meansq = squares / (H // G * P_SIZE)
            outs[0][at] = (gated * lax.rsqrt(meansq + 1e-05) * gain_ref[...]).astype(BF16)
        else:
            outs[0][at] = gated
            outs[1][at] = jnp.broadcast_to(squares, (part, LANES))


def final_output(whole_group, plans, init_row, place, values, totals, lasts, gots, y, conved, init, cum, scale, gain, factors):
    rows, channels = y.shape
    if whole_group:
        outs = [shape_of((rows, channels), BF16)]
    else:
        outs = [shape_of((rows, channels), F32), shape_of((rows, LANES), F32)]
    return pl.pallas_call(
        functools.partial(final_kernel, whole_group, plans, init_row),
        in_specs=[SMEM] + [VMEM] * (2 * SLOTS - EARLY + 7 + len(gots)),
        out_specs=[VMEM] * len(outs),
        out_shape=outs,
        cost_estimate=cost(2 * rows * channels * N, 12 * rows * channels, 2 * rows * channels),
        name="final",
        compiler_params=params(MAIN_MIB),
    )(place, *values, *totals, *lasts, *gots, y, conved, init, cum, scale, gain, factors)


def body(
    tokens,
    w_zx,
    zx_scale,
    w_bc,
    bc_scale,
    w_dt,
    conv_x,
    conv_bc,
    tail_x,
    tail_bc,
    head_params,
    init_state,
    norm_gain,
):
    tok_rows = tokens.shape[0]
    depth = w_zx.shape[0]
    local_heads = head_params.shape[1]
    channels = local_heads * P_SIZE
    per_group = H // G
    n_ctx = lax.axis_size("ctx")
    me = lax.axis_index("ctx")
    head_place = lax.axis_index("head")
    group_index = head_place * local_heads // per_group
    bits = [1 << i for i in range(n_ctx.bit_length() - 1)]
    part = tok_rows // SLOTS
    slot = head_place % SLOTS
    place = jnp.stack([slot.astype(jnp.int32), me.astype(jnp.int32)])

    dt_t = w_dt.T
    if local_heads % EDGE:
        dt_t = jnp.pad(dt_t, ((0, EDGE - local_heads % EDGE), (0, 0)))
    payloads = pack(place, tokens, dt_t, n_ctx)
    payloads = [swapped(one, "ctx", j) for j, one in enumerate(payloads, 1)]
    w_all = jnp.transpose(w_zx, (1, 0, 2))
    bc_rows = pick_group(w_bc, group_index, 1)
    gate_w = w_all[0]
    first_w = jnp.concatenate([w_all[1], bc_rows], 1)

    def blocks_of(rows):
        return [rows[i * part : (i + 1) * part] for i in range(n_ctx - 1)]

    one_way, other_way = bits, bits[::-1]
    gate0 = Reduction([one[:part] for one in payloads], one_way, gate_w)
    first0 = Reduction([one[: part + EDGE] for one in payloads], other_way, first_w)
    mark = gate0.send(first_w)
    fetched = join(payloads, part, (mark,))
    from_chip = swapped(fetched, "head", 2)
    from_core = swapped(fetched, "head", 1)
    first1 = Reduction(blocks_of(from_core), one_way, first_w)
    gate1 = Reduction(blocks_of(from_core), other_way, gate_w)
    mark = first0.send(fetched)
    mark = first1.send(mark)
    shift_t, cum, fade, logs = step_sizes(place, tokens, dt_t, payloads, head_params.T, (mark, first_w))
    mark = gate1.send(cum, logs if n_ctx == 4 else None)
    own_rows = lax.dynamic_slice_in_dim(chained([tokens], mark)[0], me * depth, depth, 1)
    own = [lax.dynamic_slice_in_dim(own_rows, (slot ^ k) * part, part, 0) for k in range(SLOTS)]
    mark = gate0.keep(own[0], mark)
    mark = first0.keep(jnp.concatenate([own[0], own_rows[tok_rows - EDGE :]], 0), mark)
    mark = first1.keep(own[1], mark)
    mark = gate1.keep(own[1], mark)
    from_both = swapped(chained([from_chip], mark)[0], "head", 1)
    first2, gate2 = (Reduction(blocks_of(from_chip), other_way, w) for w in (first_w, gate_w))
    first3, gate3 = (Reduction(blocks_of(from_both), one_way, w) for w in (first_w, gate_w))
    mark = first2.send(mark)
    mark = first3.send(mark)
    scale = jnp.concatenate([zx_scale[1], pick_group(bc_scale, group_index, 0)], 0)[None]
    firsts01 = finish(
        "fin_first", (first0.total, first1.total), (first0.last, first1.last), scale, (mark,)
    )
    gates01 = finish(
        "fin_gate", (gate0.total, gate1.total), (gate0.last, gate1.last), zx_scale[0:1], (firsts01[0],)
    )
    if n_ctx == 4:
        at = part // EDGE
        by_ctx = [(logs, 0), (gate1.last, at), (gate1.got, 2 * at), (gate1.last, at + 1)]
    else:
        by_ctx = [(logs, 0)] + [(swapped(logs, "ctx", j), 0) for j in range(1, n_ctx)]
    factors = falls(both_plans, place, by_ctx, (gates01[0],))
    mark = first2.keep(own[2], factors)
    mark = first3.keep(own[3], mark)
    arrived = passed_along(chained([firsts01[0][part:]], mark)[0], "ctx", 1)
    mark = gate2.send(mark)
    mark = gate3.send(mark)

    taps = jnp.concatenate([conv_x, pick_group(conv_bc, group_index, 1)], 1)
    before = jnp.concatenate([tail_x, pick_group(tail_bc, group_index, 1)], 1)
    before = jnp.pad(before, ((EDGE - (K - 1), 0), (0, 0)))
    halves = 2 if n_ctx == 4 else 1
    conved, *local_states = conv_and_state(
        halves, place, firsts01, (first2.total, first3.total), (first2.last, first3.last), arrived, before, scale,
        taps, fade, (mark,),
    )
    mark = gate2.keep(own[2], conved)
    mark = gate3.keep(own[3], mark)
    y_local = inner_output(conved, cum, shift_t, jnp.repeat(head_params[2], P_SIZE)[None], (mark,))

    gots, plans, start = [], [], 0
    for half, run in enumerate(local_states):
        order = bits[::-1] if half else bits
        rows = []
        for i, bit in enumerate(order):
            if i < len(bits) - 1 or half:
                gots.append(swapped(run, "ctx", bit))
            else:
                gots.append(passed_along(run, "ctx", bit))
            if i < len(bits) - 1:
                size = run.shape[1]
                share = factors[:, half * size : (half + 1) * size]
                run = merged(start + 3 * i, share, run, gots[-1], (mark,))
            rows.append(start + 3 * i + 2)
        plans.append(tuple(rows))
        start += 3 * len(bits) + 1
    init_row = 3 * len(bits)

    whole_group = local_heads >= per_group
    outs = final_output(
        whole_group,
        tuple(plans),
        init_row,
        place,
        gates01,
        (gate2.total, gate3.total),
        (gate2.last, gate3.last),
        gots,
        y_local,
        conved,
        init_state.reshape(channels, N),
        cum,
        zx_scale[0:1],
        norm_gain[None],
        factors,
    )
    if whole_group:
        return outs[0]
    gated, squares = outs
    slot_hits = (jnp.arange(G) == group_index).astype(F32)
    group_sums = lax.psum(slot_hits[:, None] * squares[:, 0][None, :], "head")
    totals = lax.dynamic_index_in_dim(group_sums, group_index, 0, keepdims=False)
    meansq = totals / (per_group * P_SIZE)
    return (gated * lax.rsqrt(meansq + 1e-05)[:, None] * norm_gain).astype(BF16)


def solution(mesh):
    return jax.shard_map(
        body,
        mesh=mesh,
        in_specs=(
            P("ctx", None),
            P("ctx", None, "head"),
            P(None, "head"),
            P("ctx", None, None),
            P(),
            P("ctx", "head"),
            P(None, "head"),
            P(),
            P(None, "head"),
            P(),
            P(None, "head"),
            P("head", None, None),
            P("head"),
        ),
        out_specs=P("ctx", "head"),
        check_vma=False,
    )
```

```python
import functools
import jax
import jax.numpy as jnp
from jax import lax
from jax.experimental import pallas as pl
from jax.experimental.pallas import tpu as pltpu
from jax.sharding import PartitionSpec as P

H = 128
P_SIZE = 64
N = 256
G = 8
K = 4
SLOTS = 4
LANES = 128
EDGE = 16
EARLY = 2
LOG_PARTS = 3
MIB = 1 << 20
MAIN_MIB = 32
SCALE = 64
BF16 = jnp.bfloat16
F32 = jnp.float32
VMEM = pl.BlockSpec(memory_space=pltpu.VMEM)
SMEM = pl.BlockSpec(memory_space=pltpu.SMEM)
ANY = pl.BlockSpec(memory_space=pl.ANY)


def shape_of(shape, dtype):
    return jax.ShapeDtypeStruct(shape, dtype)


def params(mib):
    return pltpu.CompilerParams(vmem_limit_bytes=mib * MIB)


def cost(flops, moved, transcendentals=0):
    return pl.CostEstimate(
        flops=int(flops) // SCALE, bytes_accessed=int(moved) // SCALE, transcendentals=int(transcendentals) // SCALE
    )


def chained(values, after):
    return lax.optimization_barrier((*values, after))[: len(values)]


def passed_along(x, axis, by):
    length = lax.axis_size(axis)
    pairs = [(i, i + by) for i in range(length) if 0 <= i + by < length]
    return lax.ppermute(x, axis, pairs)


def swapped(x, axis, by):
    length = lax.axis_size(axis)
    return lax.ppermute(x, axis, [(i, i ^ by) for i in range(length)])


def pick_group(values, group_index, axis_index):
    return lax.dynamic_index_in_dim(values, group_index, axis_index, keepdims=False)


def dot32(a, b):
    return jnp.dot(a, b, preferred_element_type=F32)


def silu(v):
    return v / (1.0 + jnp.exp(-v))


def pack_kernel(n, place_ref, *refs):
    blocks, tails, dt_ref, outs = refs[: n - 1], refs[n - 1 : 2 * n - 2], refs[2 * n - 2], refs[2 * n - 1 :]
    part, edge = blocks[0].shape[0], tails[0].shape[0]
    for block, tail, out in zip(blocks, tails, outs):
        out[:part] = block[...]
        out[part : part + edge] = tail[...]
        out[part + edge :] = dt_ref[...]


def pack(place, tokens, dt_t, n):
    dt_rows, depth = dt_t.shape
    part = tokens.shape[0] // SLOTS
    height = part + EDGE + dt_rows
    last = tokens.shape[0] // EDGE - 1
    return pl.pallas_call(
        functools.partial(pack_kernel, n),
        grid_spec=pltpu.PrefetchScalarGridSpec(
            num_scalar_prefetch=1,
            grid=(1,),
            in_specs=[
                pl.BlockSpec((part, depth), lambda i, place, j=j: (place[0], place[1] ^ j))
                for j in range(1, n)
            ]
            + [pl.BlockSpec((EDGE, depth), lambda i, place, j=j: (last, place[1] ^ j)) for j in range(1, n)]
            + [pl.BlockSpec((dt_rows, depth), lambda i, place: (0, 0))],
            out_specs=[pl.BlockSpec((height, depth), lambda i, place: (0, 0))] * (n - 1),
        ),
        out_shape=[shape_of((height, depth), BF16)] * (n - 1),
        name="pack",
        compiler_params=params(58),
    )(place, *[tokens] * (2 * n - 2), dt_t)


def join_kernel(part, count, *refs):
    blocks, out = refs[:count], refs[-1]
    for i, block in enumerate(blocks):
        out[i * part : (i + 1) * part] = block[:part]


def join(blocks, part, after):
    depth = blocks[0].shape[1]
    return pl.pallas_call(
        functools.partial(join_kernel, part, len(blocks)),
        in_specs=[VMEM] * len(blocks) + [ANY] * len(after),
        out_specs=VMEM,
        out_shape=shape_of((part * len(blocks), depth), BF16),
        name="join",
        compiler_params=params(8),
    )(*blocks, *after)


class Reduction:
    def __init__(self, blocks, order, weights):
        self.blocks, self.order, self.weights = blocks, order, weights
        self.part = blocks[0].shape[0]
        self.n = len(blocks) + 1

    def rows(self, offsets, after):
        return jnp.concatenate(chained([self.blocks[j - 1] for j in offsets], after), 0)

    def send(self, after, extra=None):
        offsets = [j for j in range(self.n) if j & self.order[0]]
        out = dot32(self.rows(offsets, after), self.weights).astype(BF16)
        self.extra = extra
        if extra is not None:
            out = jnp.concatenate([out, extra], 0)
        self.got = swapped(out, "ctx", self.order[0])
        return out

    def keep(self, own, after):
        self.blocks = [*self.blocks, own]
        kept = [j for j in range(self.n) if not j & self.order[0]]
        size = self.part
        got = [self.got[i * size : (i + 1) * size] for i in range(len(kept))]
        bit = self.order[1]
        gone = [i for i, j in enumerate(kept) if j & bit]
        stay = [i for i, j in enumerate(kept) if not j & bit]
        rows = self.rows([kept[i] for i in gone], after)
        out = (dot32(rows, self.weights) + jnp.concatenate([got[i] for i in gone], 0)).astype(BF16)
        mark = out
        if self.extra is not None:
            out = jnp.concatenate([out, self.extra, self.got[size * len(kept) :]], 0)
        arrived = swapped(out, "ctx", bit)
        rows = self.rows([kept[i] for i in stay], after)
        total = dot32(rows, self.weights) + jnp.concatenate([got[i] for i in stay], 0)
        kept = [kept[i] for i in stay]
        for bit in self.order[2:]:
            total = total + arrived.astype(F32)
            gone = [i for i, j in enumerate(kept) if j & bit]
            stay = [i for i, j in enumerate(kept) if not j & bit]
            parts = [total[i * size : (i + 1) * size] for i in range(len(kept))]
            out = jnp.concatenate([parts[i] for i in gone], 0).astype(BF16)
            total = jnp.concatenate([parts[i] for i in stay], 0)
            arrived = swapped(out, "ctx", bit)
            kept = [kept[i] for i in stay]
        self.total, self.last = total, arrived
        return mark


def finished(total, last, scale):
    return ((total + last.astype(F32)) * scale).astype(BF16)


def finish_kernel(count, *refs):
    totals, lasts, scale_ref, outs = refs[:count], refs[count : 2 * count], refs[2 * count], refs[-count:]
    for total, last, out in zip(totals, lasts, outs):
        out[...] = finished(total[...], last[: total.shape[0]], scale_ref[...])


def finish(name, totals, lasts, scale, after):
    count = len(totals)
    lasts = chained(lasts, after[0])
    return pl.pallas_call(
        functools.partial(finish_kernel, count),
        in_specs=[VMEM] * (2 * count + 1) + [ANY] * len(after),
        out_specs=[VMEM] * count,
        out_shape=[shape_of(t.shape, BF16) for t in totals],
        cost_estimate=cost(4 * count * totals[0].size, 8 * count * totals[0].size),
        name=name,
        compiler_params=params(12),
    )(*totals, *lasts, scale, *after)


def quarter_values(values, totals, lasts, scale):
    early = [v[...] for v in values]
    return early + [finished(t[...], l[...], scale) for t, l in zip(totals, lasts)]


def step_kernel(n, me_ref, tok_ref, *refs):
    weights, heads_ref = refs[:n], refs[n]
    shift_t_ref, cum_ref, fade_ref, log_ref, acc = refs[-5:]
    j = pl.program_id(0)

    @pl.when(j == 0)
    def _():
        acc[...] = jnp.zeros_like(acc)

    for i in range(n):

        @pl.when(j == i)
        def _():
            acc[...] += lax.dot_general(
                weights[i][...], tok_ref[...], (((1,), (1,)), ((), ())), preferred_element_type=F32
            )

    @pl.when(j == pl.num_programs(0) - 1)
    def _():
        v = acc[: heads_ref.shape[0]] + heads_ref[:, 0:1]
        step = jnp.maximum(v, 0.0) + jnp.log1p(jnp.exp(-jnp.abs(v)))
        rate = -jnp.exp(heads_ref[:, 1:2]) * step
        rows = rate.shape[1]
        up_to = lax.broadcasted_iota(jnp.int32, (rows, rows), 0) <= lax.broadcasted_iota(
            jnp.int32, (rows, rows), 1
        )
        cum = jnp.dot(
            rate, up_to.astype(F32), precision=lax.Precision.HIGHEST, preferred_element_type=F32
        )
        last = cum[:, rows - 1 : rows]
        shift_t_ref[...] = cum - jnp.log(step)
        cum_ref[...] = cum.T
        fade_ref[...] = (jnp.exp(last - cum) * step).T
        left = jnp.broadcast_to(last.T, (8, last.shape[0]))
        hits = head_spread(last.shape[0])
        index = lax.broadcasted_iota(jnp.int32, log_ref.shape, 0)
        block = jnp.zeros(log_ref.shape, F32)
        for i in range(LOG_PARTS):
            term = left.astype(BF16)
            left = left - term.astype(F32)
            block = jnp.where(index == i, dot32(term, hits)[0:1], block)
        log_ref[...] = block.astype(BF16)


def step_sizes(place, tokens, dt_t, payloads, heads, after):
    dt_rows, depth = dt_t.shape
    local_heads = heads.shape[0]
    n = len(payloads) + 1
    rows = tokens.shape[0]
    last = payloads[0].shape[0] // dt_rows - 1
    whole = lambda shape: pl.BlockSpec(shape, lambda j, place: (0, 0))
    return pl.pallas_call(
        functools.partial(step_kernel, n),
        grid_spec=pltpu.PrefetchScalarGridSpec(
            num_scalar_prefetch=1,
            grid=(n,),
            in_specs=[
                pl.BlockSpec((rows, depth), lambda j, place: (0, place[1] ^ j)),
                whole((dt_rows, depth)),
            ]
            + [pl.BlockSpec((dt_rows, depth), lambda j, place: (last, 0))] * (n - 1)
            + [whole((local_heads, 3))]
            + [ANY] * len(after),
            out_specs=[
                whole((local_heads, rows)),
                whole((rows, local_heads)),
                whole((rows, local_heads)),
                whole((EDGE, local_heads * P_SIZE)),
            ],
            scratch_shapes=[pltpu.VMEM((dt_rows, rows), F32)],
        ),
        out_shape=[
            shape_of((local_heads, rows), F32),
            shape_of((rows, local_heads), F32),
            shape_of((rows, local_heads), F32),
            shape_of((EDGE, local_heads * P_SIZE), BF16),
        ],
        cost_estimate=cost(2 * n * rows * depth * LANES, 2 * n * rows * depth),
        name="steps",
        compiler_params=params(16),
    )(place, tokens, dt_t, *payloads, heads, *after)


def head_spread(local_heads):
    channels = local_heads * P_SIZE
    hit = (
        lax.broadcasted_iota(jnp.int32, (local_heads, channels), 1) // P_SIZE
        == lax.broadcasted_iota(jnp.int32, (local_heads, channels), 0)
    )
    return hit.astype(F32).astype(BF16)


def spread_heads(values, hits):
    high = values.astype(BF16)
    low = (values - high.astype(F32)).astype(BF16)
    return dot32(high, hits) + dot32(low, hits)


def conv_kernel(count, place_ref, *refs):
    values, totals, lasts = refs[:EARLY], refs[EARLY:SLOTS], refs[SLOTS : 2 * SLOTS - EARLY]
    arrived_ref, before_ref, scale_ref, taps_ref, fade_ref = refs[2 * SLOTS - EARLY : 2 * SLOTS - EARLY + 5]
    conv_ref, states, vals = refs[-2 - count], refs[-1 - count : -1], refs[-1]
    part, width = totals[0].shape
    rows = part * SLOTS
    channels = width - 2 * N
    slot = place_ref[0]
    first = place_ref[1] == 0
    vals[:EDGE] = jnp.where(first, before_ref[...].astype(F32), arrived_ref[...].astype(F32))
    for k, value in enumerate(quarter_values(values, totals, lasts, scale_ref[...])):
        start = pl.multiple_of(EDGE + (slot ^ k) * part, EDGE)
        vals[pl.ds(start, part)] = value[:part].astype(F32)
    for c in range(0, width, 2 * LANES):
        cols = slice(c, c + 2 * LANES)
        for r in range(0, rows, part):
            summed = taps_ref[K : K + 1, cols]
            for tap in range(K):
                at = r + EDGE - (K - 1) + tap
                summed = summed + taps_ref[tap : tap + 1, cols] * vals[at : at + part, cols]
            conv_ref[r : r + part, cols] = silu(summed).astype(BF16)
    hits = head_spread(channels // P_SIZE)
    faded = spread_heads(fade_ref[...], hits) * conv_ref[:, :channels].astype(F32)
    state = lax.dot_general(
        conv_ref[:, channels : channels + N],
        faded.astype(BF16),
        (((0,), (0,)), ((), ())),
        preferred_element_type=F32,
    ).astype(BF16)
    size = channels // len(states)
    for i, out in enumerate(states):
        out[...] = state[:, i * size : (i + 1) * size]


def conv_and_state(count, place, values, totals, lasts, arrived, before, scale, taps, fade, after):
    part, width = totals[0].shape
    rows = part * SLOTS
    return pl.pallas_call(
        functools.partial(conv_kernel, count),
        in_specs=[SMEM] + [VMEM] * (2 * SLOTS - EARLY + 5) + [ANY] * len(after),
        out_specs=[VMEM] * (1 + count),
        out_shape=[shape_of((rows, width), BF16)] + [shape_of((N, (width - 2 * N) // count), BF16)] * count,
        scratch_shapes=[pltpu.VMEM((rows + EDGE, width), F32)],
        cost_estimate=cost(30 * rows * width, 12 * rows * width, 2 * rows * width),
        name="conv",
        compiler_params=params(MAIN_MIB),
    )(place, *values, *totals, *lasts, arrived, before, scale, taps, fade, *after)


def inner_kernel(conv_ref, cum_ref, shift_t_ref, skip_ref, *refs):
    y_ref, scores = refs[-2:]
    rows, width = conv_ref.shape
    channels = width - 2 * N
    size = LANES
    blocks = rows // size
    nt = (((1,), (1,)), ((), ()))
    scores[...] = lax.dot_general(
        conv_ref[:, channels + N :], conv_ref[:, channels : channels + N], nt, preferred_element_type=F32
    )
    lower = lax.broadcasted_iota(jnp.int32, (size, size), 0) >= lax.broadcasted_iota(
        jnp.int32, (size, size), 1
    )
    left = lax.broadcasted_iota(jnp.int32, (size, 2 * P_SIZE), 1) < P_SIZE
    for pair in range(channels // (2 * P_SIZE)):
        cols = slice(pair * 2 * P_SIZE, (pair + 1) * 2 * P_SIZE)
        for a in range(blocks):
            t = slice(a * size, (a + 1) * size)
            products = []
            for h in (2 * pair, 2 * pair + 1):
                here = cum_ref[t, h : h + 1]
                own = jnp.where(lower, here - shift_t_ref[h : h + 1, t], -jnp.inf)
                weights = jnp.exp(own) * scores[t, t]
                if a > 0:
                    before = slice(0, a * size)
                    earlier = jnp.exp(here - shift_t_ref[h : h + 1, before]) * scores[t, before]
                    weights = jnp.concatenate([earlier, weights], 1)
                products.append(dot32(weights.astype(BF16), conv_ref[: (a + 1) * size, cols]))
            y_ref[t, cols] = jnp.where(left, products[0], products[1]) + skip_ref[:, cols] * conv_ref[
                t, cols
            ].astype(F32)


def inner_output(conved, cum, shift_t, skip, after):
    rows, width = conved.shape
    channels = width - 2 * N
    return pl.pallas_call(
        inner_kernel,
        in_specs=[VMEM] * 4 + [ANY] * len(after),
        out_specs=VMEM,
        out_shape=shape_of((rows, channels), F32),
        scratch_shapes=[pltpu.VMEM((rows, rows), F32)],
        cost_estimate=cost(2 * rows * rows * channels, 8 * rows * width, rows * rows * channels // P_SIZE),
        name="inner",
        compiler_params=params(MAIN_MIB),
    )(conved, cum, shift_t, skip, *after)


def falls_kernel(n, plan, place_ref, *refs):
    logs, out_ref = refs[:n], refs[-1]
    values = []
    for log in logs:
        block = log[...].astype(F32)
        values.append(sum(block[i : i + 1] for i in range(LOG_PARTS)))
    index = lax.broadcasted_iota(jnp.int32, out_ref.shape, 0)
    block = jnp.zeros(out_ref.shape, F32)
    for i, (counts, parts) in enumerate(plan(place_ref[1], n)):
        total = jnp.zeros_like(values[0])
        for present, offset in parts:
            total = total + jnp.where(present, values[offset], 0.0)
        block = jnp.where(index == i, jnp.where(counts, jnp.exp(total), 0.0), block)
    out_ref[...] = block


def falls(plan, place, logs, after):
    n = len(logs)
    channels = logs[0][0].shape[1]
    rows = -(-len(plan(0, n)) // 8) * 8
    return pl.pallas_call(
        functools.partial(falls_kernel, n, plan),
        grid_spec=pltpu.PrefetchScalarGridSpec(
            num_scalar_prefetch=1,
            grid=(1,),
            in_specs=[pl.BlockSpec((EDGE, channels), lambda i, place, at=at: (at, 0)) for _, at in logs]
            + [ANY] * len(after),
            out_specs=pl.BlockSpec((rows, channels), lambda i, place: (0, 0)),
        ),
        out_shape=shape_of((rows, channels), F32),
        name="falls",
        compiler_params=params(8),
    )(place, *[array for array, _ in logs], *after)


def scan_plan(me, n):
    out, before = [], []
    bit = 1
    while bit < n:
        later = (me & bit) > 0
        own_span = [(True, j) for j in range(bit)]
        got_span = [(True, j) for j in range(bit, 2 * bit)]
        out.append((True, [(jnp.logical_not(later), j) for _, j in got_span]))
        out.append((True, [(later, j) for _, j in own_span]))
        out.append((later, list(before)))
        before += [(later, j) for _, j in got_span]
        bit *= 2
    return out + [(True, before)]


def swap_plan(me, n):
    low, high = (me & 1) > 0, (me & 2) > 0
    return [
        (jnp.logical_not(low), []),
        (high, [(jnp.logical_not(low), 0), (jnp.logical_not(low), 3)]),
        (high, [(low, 1), (jnp.logical_not(low), 3)]),
        (True, []),
        (True, []),
        (True, []),
    ]


def both_plans(me, n):
    return scan_plan(me, n) + (swap_plan(me, n) if n == 4 else [])


def merge_kernel(row, falls_ref, own_ref, got_ref, *refs):
    own_fall, got_fall = falls_ref[row : row + 1], falls_ref[row + 1 : row + 2]
    refs[-1][...] = (own_fall * own_ref[...].astype(F32) + got_fall * got_ref[...].astype(F32)).astype(BF16)


def merged(row, factors, own, got, after):
    return pl.pallas_call(
        functools.partial(merge_kernel, row),
        in_specs=[VMEM] * 3 + [ANY] * len(after),
        out_specs=VMEM,
        out_shape=shape_of(own.shape, BF16),
        cost_estimate=cost(4 * own.size, 6 * own.size),
        name="merge",
        compiler_params=params(12),
    )(factors, own, got, *after)


def final_kernel(whole_group, plans, init_row, place_ref, *refs):
    rounds = sum(len(rows) for rows in plans)
    values, totals, lasts = refs[:EARLY], refs[EARLY:SLOTS], refs[SLOTS : 2 * SLOTS - EARLY]
    refs = refs[2 * SLOTS - EARLY :]
    gots, refs = refs[:rounds], refs[rounds:]
    y_ref, conv_ref, init_ref, cum_ref, scale_ref, gain_ref, falls_ref = refs[:7]
    outs = refs[7:]
    part, channels = totals[0].shape
    slot = place_ref[0]
    hits = head_spread(channels // P_SIZE)
    size = channels // len(plans)
    states = []
    for i, rows in enumerate(plans):
        cols = slice(i * size, (i + 1) * size)
        states.append(
            sum(
                falls_ref[row : row + 1, cols] * got[...].astype(F32)
                for row, got in zip(rows, gots[i * len(rows) : (i + 1) * len(rows)])
            )
        )
    state = jnp.concatenate(states, 1).astype(BF16)
    init = init_ref[...].astype(BF16)
    init_fall = falls_ref[init_row : init_row + 1]
    nt = (((1,), (1,)), ((), ()))
    for k, value in enumerate(quarter_values(values, totals, lasts, scale_ref[...])):
        at = pl.ds(pl.multiple_of((slot ^ k) * part, part), part)
        c_part = conv_ref[at, channels + N :]
        carried = dot32(c_part, state)
        carried = carried + init_fall * lax.dot_general(c_part, init, nt, preferred_element_type=F32)
        y = y_ref[at] + carried * spread_heads(jnp.exp(cum_ref[at]), hits)
        gated = y * silu(value.astype(F32))
        squares = jnp.sum(gated * gated, axis=1, keepdims=True)
        if whole_group:
            meansq = squares / (H // G * P_SIZE)
            outs[0][at] = (gated * lax.rsqrt(meansq + 1e-05) * gain_ref[...]).astype(BF16)
        else:
            outs[0][at] = gated
            outs[1][at] = jnp.broadcast_to(squares, (part, LANES))


def final_output(whole_group, plans, init_row, place, values, totals, lasts, gots, y, conved, init, cum, scale, gain, factors):
    rows, channels = y.shape
    if whole_group:
        outs = [shape_of((rows, channels), BF16)]
    else:
        outs = [shape_of((rows, channels), F32), shape_of((rows, LANES), F32)]
    return pl.pallas_call(
        functools.partial(final_kernel, whole_group, plans, init_row),
        in_specs=[SMEM] + [VMEM] * (2 * SLOTS - EARLY + 7 + len(gots)),
        out_specs=[VMEM] * len(outs),
        out_shape=outs,
        cost_estimate=cost(2 * rows * channels * N, 12 * rows * channels, 2 * rows * channels),
        name="final",
        compiler_params=params(MAIN_MIB),
    )(place, *values, *totals, *lasts, *gots, y, conved, init, cum, scale, gain, factors)


def body(
    tokens,
    w_zx,
    zx_scale,
    w_bc,
    bc_scale,
    w_dt,
    conv_x,
    conv_bc,
    tail_x,
    tail_bc,
    head_params,
    init_state,
    norm_gain,
):
    tok_rows = tokens.shape[0]
    depth = w_zx.shape[0]
    local_heads = head_params.shape[1]
    channels = local_heads * P_SIZE
    per_group = H // G
    n_ctx = lax.axis_size("ctx")
    me = lax.axis_index("ctx")
    head_place = lax.axis_index("head")
    group_index = head_place * local_heads // per_group
    bits = [1 << i for i in range(n_ctx.bit_length() - 1)]
    part = tok_rows // SLOTS
    slot = head_place % SLOTS
    place = jnp.stack([slot.astype(jnp.int32), me.astype(jnp.int32)])

    dt_t = w_dt.T
    if local_heads % EDGE:
        dt_t = jnp.pad(dt_t, ((0, EDGE - local_heads % EDGE), (0, 0)))
    payloads = pack(place, tokens, dt_t, n_ctx)
    payloads = [swapped(one, "ctx", j) for j, one in enumerate(payloads, 1)]
    w_all = jnp.transpose(w_zx, (1, 0, 2))
    bc_rows = pick_group(w_bc, group_index, 1)
    gate_w = w_all[0]
    first_w = jnp.concatenate([w_all[1], bc_rows], 1)

    def blocks_of(rows):
        return [rows[i * part : (i + 1) * part] for i in range(n_ctx - 1)]

    one_way, other_way = bits, bits[::-1]
    gate0 = Reduction([one[:part] for one in payloads], one_way, gate_w)
    first0 = Reduction([one[: part + EDGE] for one in payloads], other_way, first_w)
    mark = gate0.send(first_w)
    fetched = join(payloads, part, (mark, gate_w))
    from_chip = swapped(fetched, "head", 2)
    from_core = swapped(fetched, "head", 1)
    first1 = Reduction(blocks_of(from_core), one_way, first_w)
    gate1 = Reduction(blocks_of(from_core), other_way, gate_w)
    mark = first0.send(fetched)
    mark = first1.send(mark)
    shift_t, cum, fade, logs = step_sizes(place, tokens, dt_t, payloads, head_params.T, (mark, first_w))
    mark = gate1.send(cum, logs if n_ctx == 4 else None)
    own_rows = lax.dynamic_slice_in_dim(chained([tokens], mark)[0], me * depth, depth, 1)
    own = [lax.dynamic_slice_in_dim(own_rows, (slot ^ k) * part, part, 0) for k in range(SLOTS)]
    mark = first0.keep(jnp.concatenate([own[0], own_rows[tok_rows - EDGE :]], 0), mark)
    mark = first1.keep(own[1], mark)
    mark = gate0.keep(own[0], mark)
    mark = gate1.keep(own[1], mark)
    from_chip = chained([from_chip], mark)[0]
    from_both = swapped(from_chip, "head", 1)
    first2, gate2 = (Reduction(blocks_of(from_chip), other_way, w) for w in (first_w, gate_w))
    first3, gate3 = (Reduction(blocks_of(from_both), one_way, w) for w in (first_w, gate_w))
    mark = first2.send(mark)
    mark = first3.send(mark)
    scale = jnp.concatenate([zx_scale[1], pick_group(bc_scale, group_index, 0)], 0)[None]
    firsts01 = finish(
        "fin_first", (first0.total, first1.total), (first0.last, first1.last), scale, (mark,)
    )
    gates01 = finish(
        "fin_gate", (gate0.total, gate1.total), (gate0.last, gate1.last), zx_scale[0:1], (firsts01[0],)
    )
    if n_ctx == 4:
        at = part // EDGE
        got, last = chained([gate1.got, gate1.last], gates01[0])
        by_ctx = [(logs, 0), (last, at), (got, 2 * at), (last, at + 1)]
    else:
        by_ctx = [(logs, 0)] + [(swapped(logs, "ctx", j), 0) for j in range(1, n_ctx)]
    factors = falls(both_plans, place, by_ctx, (gates01[0],))
    arrived = passed_along(chained([firsts01[0][part:]], factors)[0], "ctx", 1)
    mark = first2.keep(own[2], factors)
    mark = first3.keep(own[3], mark)
    mark = gate2.send(mark)
    mark = gate3.send(mark)

    taps = jnp.concatenate([conv_x, pick_group(conv_bc, group_index, 1)], 1)
    before = jnp.concatenate([tail_x, pick_group(tail_bc, group_index, 1)], 1)
    before = jnp.pad(before, ((EDGE - (K - 1), 0), (0, 0)))
    halves = 2 if n_ctx == 4 else 1
    conved, *local_states = conv_and_state(
        halves, place, firsts01, (first2.total, first3.total), (first2.last, first3.last), arrived, before, scale,
        taps, fade, (mark,),
    )
    mark = gate2.keep(own[2], conved)
    mark = gate3.keep(own[3], mark)
    gots, plans, runs, start = [], [], [], 0
    for half, run in enumerate(local_states):
        order = bits[::-1] if half else bits
        rows = []
        for i, bit in enumerate(order):
            if i < len(bits) - 1 or half:
                gots.append(swapped(run, "ctx", bit))
            else:
                gots.append(passed_along(run, "ctx", bit))
            if i < len(bits) - 1:
                size = run.shape[1]
                share = factors[:, half * size : (half + 1) * size]
                run = merged(start + 3 * i, share, run, gots[-1], (mark,))
            rows.append(start + 3 * i + 2)
        runs.append(run)
        plans.append(tuple(rows))
        start += 3 * len(bits) + 1
    init_row = 3 * len(bits)
    y_local = inner_output(conved, cum, shift_t, jnp.repeat(head_params[2], P_SIZE)[None], tuple(runs))

    whole_group = local_heads >= per_group
    outs = final_output(
        whole_group,
        tuple(plans),
        init_row,
        place,
        gates01,
        (gate2.total, gate3.total),
        (gate2.last, gate3.last),
        gots,
        y_local,
        conved,
        init_state.reshape(channels, N),
        cum,
        zx_scale[0:1],
        norm_gain[None],
        factors,
    )
    if whole_group:
        return outs[0]
    gated, squares = outs
    slot_hits = (jnp.arange(G) == group_index).astype(F32)
    group_sums = lax.psum(slot_hits[:, None] * squares[:, 0][None, :], "head")
    totals = lax.dynamic_index_in_dim(group_sums, group_index, 0, keepdims=False)
    meansq = totals / (per_group * P_SIZE)
    return (gated * lax.rsqrt(meansq + 1e-05)[:, None] * norm_gain).astype(BF16)


def solution(mesh):
    return jax.shard_map(
        body,
        mesh=mesh,
        in_specs=(
            P("ctx", None),
            P("ctx", None, "head"),
            P(None, "head"),
            P("ctx", None, None),
            P(),
            P("ctx", "head"),
            P(None, "head"),
            P(),
            P(None, "head"),
            P(),
            P(None, "head"),
            P("head", None, None),
            P("head"),
        ),
        out_specs=P("ctx", "head"),
        check_vma=False,
    )
```

```python
import functools
import jax
import jax.numpy as jnp
from jax import lax
from jax.experimental import pallas as pl
from jax.experimental.pallas import tpu as pltpu
from jax.sharding import PartitionSpec as P

H = 128
P_SIZE = 64
N = 256
G = 8
K = 4
SLOTS = 4
LANES = 128
EDGE = 16
EARLY = 2
LOG_PARTS = 3
MIB = 1 << 20
MAIN_MIB = 32
SCALE = 64
BF16 = jnp.bfloat16
F32 = jnp.float32
VMEM = pl.BlockSpec(memory_space=pltpu.VMEM)
SMEM = pl.BlockSpec(memory_space=pltpu.SMEM)
ANY = pl.BlockSpec(memory_space=pl.ANY)


def shape_of(shape, dtype):
    return jax.ShapeDtypeStruct(shape, dtype)


def params(mib):
    return pltpu.CompilerParams(vmem_limit_bytes=mib * MIB)


def cost(flops, moved, transcendentals=0):
    return pl.CostEstimate(
        flops=int(flops) // SCALE, bytes_accessed=int(moved) // SCALE, transcendentals=int(transcendentals) // SCALE
    )


def chained(values, after):
    return lax.optimization_barrier((*values, after))[: len(values)]


def passed_along(x, axis, by):
    length = lax.axis_size(axis)
    pairs = [(i, i + by) for i in range(length) if 0 <= i + by < length]
    return lax.ppermute(x, axis, pairs)


def swapped(x, axis, by):
    length = lax.axis_size(axis)
    return lax.ppermute(x, axis, [(i, i ^ by) for i in range(length)])


def pick_group(values, group_index, axis_index):
    return lax.dynamic_index_in_dim(values, group_index, axis_index, keepdims=False)


def dot32(a, b):
    return jnp.dot(a, b, preferred_element_type=F32)


def silu(v):
    return v / (1.0 + jnp.exp(-v))


def pack_kernel(n, place_ref, *refs):
    blocks, tails, dt_ref, outs = refs[: n - 1], refs[n - 1 : 2 * n - 2], refs[2 * n - 2], refs[2 * n - 1 :]
    part, edge = blocks[0].shape[0], tails[0].shape[0]
    for block, tail, out in zip(blocks, tails, outs):
        out[:part] = block[...]
        out[part : part + edge] = tail[...]
        out[part + edge :] = dt_ref[...]


def pack(place, tokens, dt_t, n):
    dt_rows, depth = dt_t.shape
    part = tokens.shape[0] // SLOTS
    height = part + EDGE + dt_rows
    last = tokens.shape[0] // EDGE - 1
    return pl.pallas_call(
        functools.partial(pack_kernel, n),
        grid_spec=pltpu.PrefetchScalarGridSpec(
            num_scalar_prefetch=1,
            grid=(1,),
            in_specs=[
                pl.BlockSpec((part, depth), lambda i, place, j=j: (place[0], place[1] ^ j))
                for j in range(1, n)
            ]
            + [pl.BlockSpec((EDGE, depth), lambda i, place, j=j: (last, place[1] ^ j)) for j in range(1, n)]
            + [pl.BlockSpec((dt_rows, depth), lambda i, place: (0, 0))],
            out_specs=[pl.BlockSpec((height, depth), lambda i, place: (0, 0))] * (n - 1),
        ),
        out_shape=[shape_of((height, depth), BF16)] * (n - 1),
        name="pack",
        compiler_params=params(58),
    )(place, *[tokens] * (2 * n - 2), dt_t)


def join_kernel(part, count, *refs):
    blocks, out = refs[:count], refs[-1]
    for i, block in enumerate(blocks):
        out[i * part : (i + 1) * part] = block[:part]


def join(blocks, part, after):
    depth = blocks[0].shape[1]
    return pl.pallas_call(
        functools.partial(join_kernel, part, len(blocks)),
        in_specs=[VMEM] * len(blocks) + [ANY] * len(after),
        out_specs=VMEM,
        out_shape=shape_of((part * len(blocks), depth), BF16),
        name="join",
        compiler_params=params(8),
    )(*blocks, *after)


def weights_kernel(all_ref, side_ref, *refs):
    gate_ref, first_ref = refs[-2:]
    channels = gate_ref.shape[1]
    gate_ref[...] = all_ref[0]
    first_ref[:, :channels] = all_ref[1]
    first_ref[:, channels:] = side_ref[...]


def weights(w_all, side, after):
    _, depth, channels = w_all.shape
    width = side.shape[1]
    rows = min(depth, 256)
    return pl.pallas_call(
        weights_kernel,
        grid=(depth // rows,),
        in_specs=[
            pl.BlockSpec((2, rows, channels), lambda i: (0, i, 0)),
            pl.BlockSpec((rows, width), lambda i: (i, 0)),
        ]
        + [ANY] * len(after),
        out_specs=[
            pl.BlockSpec((rows, channels), lambda i: (i, 0)),
            pl.BlockSpec((rows, channels + width), lambda i: (i, 0)),
        ],
        out_shape=[shape_of((depth, channels), BF16), shape_of((depth, channels + width), BF16)],
        name="weights",
        compiler_params=params(58),
    )(w_all, side, *after)


class Reduction:
    def __init__(self, blocks, order, weights):
        self.blocks, self.order, self.weights = blocks, order, weights
        self.part = blocks[0].shape[0]
        self.n = len(blocks) + 1

    def rows(self, offsets, after):
        return jnp.concatenate(chained([self.blocks[j - 1] for j in offsets], after), 0)

    def send(self, after, extra=None):
        offsets = [j for j in range(self.n) if j & self.order[0]]
        out = dot32(self.rows(offsets, after), self.weights).astype(BF16)
        self.extra = extra
        if extra is not None:
            out = jnp.concatenate([out, extra], 0)
        self.got = swapped(out, "ctx", self.order[0])
        return out

    def keep(self, own, after):
        self.blocks = [*self.blocks, own]
        kept = [j for j in range(self.n) if not j & self.order[0]]
        size = self.part
        got = [self.got[i * size : (i + 1) * size] for i in range(len(kept))]
        bit = self.order[1]
        gone = [i for i, j in enumerate(kept) if j & bit]
        stay = [i for i, j in enumerate(kept) if not j & bit]
        rows = self.rows([kept[i] for i in gone], after)
        out = (dot32(rows, self.weights) + jnp.concatenate([got[i] for i in gone], 0)).astype(BF16)
        mark = out
        if self.extra is not None:
            out = jnp.concatenate([out, self.extra, self.got[size * len(kept) :]], 0)
        arrived = swapped(out, "ctx", bit)
        rows = self.rows([kept[i] for i in stay], after)
        total = dot32(rows, self.weights) + jnp.concatenate([got[i] for i in stay], 0)
        kept = [kept[i] for i in stay]
        for bit in self.order[2:]:
            total = total + arrived.astype(F32)
            gone = [i for i, j in enumerate(kept) if j & bit]
            stay = [i for i, j in enumerate(kept) if not j & bit]
            parts = [total[i * size : (i + 1) * size] for i in range(len(kept))]
            out = jnp.concatenate([parts[i] for i in gone], 0).astype(BF16)
            total = jnp.concatenate([parts[i] for i in stay], 0)
            arrived = swapped(out, "ctx", bit)
            kept = [kept[i] for i in stay]
        self.total, self.last = total, arrived
        return mark


def finished(total, last, scale):
    return ((total + last.astype(F32)) * scale).astype(BF16)


def finish_kernel(count, *refs):
    totals, lasts, scale_ref, outs = refs[:count], refs[count : 2 * count], refs[2 * count], refs[-count:]
    for total, last, out in zip(totals, lasts, outs):
        out[...] = finished(total[...], last[: total.shape[0]], scale_ref[...])


def finish(name, totals, lasts, scale, after):
    count = len(totals)
    lasts = chained(lasts, after[0])
    return pl.pallas_call(
        functools.partial(finish_kernel, count),
        in_specs=[VMEM] * (2 * count + 1) + [ANY] * len(after),
        out_specs=[VMEM] * count,
        out_shape=[shape_of(t.shape, BF16) for t in totals],
        cost_estimate=cost(4 * count * totals[0].size, 8 * count * totals[0].size),
        name=name,
        compiler_params=params(12),
    )(*totals, *lasts, scale, *after)


def quarter_values(values, totals, lasts, scale):
    early = [v[...] for v in values]
    return early + [finished(t[...], l[...], scale) for t, l in zip(totals, lasts)]


def step_kernel(n, me_ref, tok_ref, *refs):
    weights, heads_ref = refs[:n], refs[n]
    shift_t_ref, cum_ref, fade_ref, log_ref, acc = refs[-5:]
    j = pl.program_id(0)

    @pl.when(j == 0)
    def _():
        acc[...] = jnp.zeros_like(acc)

    for i in range(n):

        @pl.when(j == i)
        def _():
            acc[...] += lax.dot_general(
                weights[i][...], tok_ref[...], (((1,), (1,)), ((), ())), preferred_element_type=F32
            )

    @pl.when(j == pl.num_programs(0) - 1)
    def _():
        v = acc[: heads_ref.shape[0]] + heads_ref[:, 0:1]
        step = jnp.maximum(v, 0.0) + jnp.log1p(jnp.exp(-jnp.abs(v)))
        rate = -jnp.exp(heads_ref[:, 1:2]) * step
        rows = rate.shape[1]
        up_to = lax.broadcasted_iota(jnp.int32, (rows, rows), 0) <= lax.broadcasted_iota(
            jnp.int32, (rows, rows), 1
        )
        cum = jnp.dot(
            rate, up_to.astype(F32), precision=lax.Precision.HIGHEST, preferred_element_type=F32
        )
        last = cum[:, rows - 1 : rows]
        shift_t_ref[...] = cum - jnp.log(step)
        cum_ref[...] = cum.T
        fade_ref[...] = (jnp.exp(last - cum) * step).T
        left = jnp.broadcast_to(last.T, (8, last.shape[0]))
        hits = head_spread(last.shape[0])
        index = lax.broadcasted_iota(jnp.int32, log_ref.shape, 0)
        block = jnp.zeros(log_ref.shape, F32)
        for i in range(LOG_PARTS):
            term = left.astype(BF16)
            left = left - term.astype(F32)
            block = jnp.where(index == i, dot32(term, hits)[0:1], block)
        log_ref[...] = block.astype(BF16)


def step_sizes(place, tokens, dt_t, payloads, heads, after):
    dt_rows, depth = dt_t.shape
    local_heads = heads.shape[0]
    n = len(payloads) + 1
    rows = tokens.shape[0]
    last = payloads[0].shape[0] // dt_rows - 1
    whole = lambda shape: pl.BlockSpec(shape, lambda j, place: (0, 0))
    return pl.pallas_call(
        functools.partial(step_kernel, n),
        grid_spec=pltpu.PrefetchScalarGridSpec(
            num_scalar_prefetch=1,
            grid=(n,),
            in_specs=[
                pl.BlockSpec((rows, depth), lambda j, place: (0, place[1] ^ j)),
                whole((dt_rows, depth)),
            ]
            + [pl.BlockSpec((dt_rows, depth), lambda j, place: (last, 0))] * (n - 1)
            + [whole((local_heads, 3))]
            + [ANY] * len(after),
            out_specs=[
                whole((local_heads, rows)),
                whole((rows, local_heads)),
                whole((rows, local_heads)),
                whole((EDGE, local_heads * P_SIZE)),
            ],
            scratch_shapes=[pltpu.VMEM((dt_rows, rows), F32)],
        ),
        out_shape=[
            shape_of((local_heads, rows), F32),
            shape_of((rows, local_heads), F32),
            shape_of((rows, local_heads), F32),
            shape_of((EDGE, local_heads * P_SIZE), BF16),
        ],
        cost_estimate=cost(2 * n * rows * depth * LANES, 2 * n * rows * depth),
        name="steps",
        compiler_params=params(16),
    )(place, tokens, dt_t, *payloads, heads, *after)


def head_spread(local_heads):
    channels = local_heads * P_SIZE
    hit = (
        lax.broadcasted_iota(jnp.int32, (local_heads, channels), 1) // P_SIZE
        == lax.broadcasted_iota(jnp.int32, (local_heads, channels), 0)
    )
    return hit.astype(F32).astype(BF16)


def spread_heads(values, hits):
    high = values.astype(BF16)
    low = (values - high.astype(F32)).astype(BF16)
    return dot32(high, hits) + dot32(low, hits)


def conv_kernel(count, place_ref, *refs):
    values, totals, lasts = refs[:EARLY], refs[EARLY:SLOTS], refs[SLOTS : 2 * SLOTS - EARLY]
    arrived_ref, before_ref, scale_ref, taps_ref, fade_ref = refs[2 * SLOTS - EARLY : 2 * SLOTS - EARLY + 5]
    conv_ref, states, vals = refs[-2 - count], refs[-1 - count : -1], refs[-1]
    part, width = totals[0].shape
    rows = part * SLOTS
    channels = width - 2 * N
    slot = place_ref[0]
    first = place_ref[1] == 0
    vals[:EDGE] = jnp.where(first, before_ref[...].astype(F32), arrived_ref[...].astype(F32))
    for k, value in enumerate(quarter_values(values, totals, lasts, scale_ref[...])):
        start = pl.multiple_of(EDGE + (slot ^ k) * part, EDGE)
        vals[pl.ds(start, part)] = value[:part].astype(F32)
    for c in range(0, width, 2 * LANES):
        cols = slice(c, c + 2 * LANES)
        for r in range(0, rows, part):
            summed = taps_ref[K : K + 1, cols]
            for tap in range(K):
                at = r + EDGE - (K - 1) + tap
                summed = summed + taps_ref[tap : tap + 1, cols] * vals[at : at + part, cols]
            conv_ref[r : r + part, cols] = silu(summed).astype(BF16)
    hits = head_spread(channels // P_SIZE)
    faded = spread_heads(fade_ref[...], hits) * conv_ref[:, :channels].astype(F32)
    state = lax.dot_general(
        conv_ref[:, channels : channels + N],
        faded.astype(BF16),
        (((0,), (0,)), ((), ())),
        preferred_element_type=F32,
    ).astype(BF16)
    size = channels // len(states)
    for i, out in enumerate(states):
        out[...] = state[:, i * size : (i + 1) * size]


def conv_and_state(count, place, values, totals, lasts, arrived, before, scale, taps, fade, after):
    part, width = totals[0].shape
    rows = part * SLOTS
    return pl.pallas_call(
        functools.partial(conv_kernel, count),
        in_specs=[SMEM] + [VMEM] * (2 * SLOTS - EARLY + 5) + [ANY] * len(after),
        out_specs=[VMEM] * (1 + count),
        out_shape=[shape_of((rows, width), BF16)] + [shape_of((N, (width - 2 * N) // count), BF16)] * count,
        scratch_shapes=[pltpu.VMEM((rows + EDGE, width), F32)],
        cost_estimate=cost(30 * rows * width, 12 * rows * width, 2 * rows * width),
        name="conv",
        compiler_params=params(MAIN_MIB),
    )(place, *values, *totals, *lasts, arrived, before, scale, taps, fade, *after)


def inner_kernel(conv_ref, cum_ref, shift_t_ref, skip_ref, *refs):
    y_ref, scores = refs[-2:]
    rows, width = conv_ref.shape
    channels = width - 2 * N
    size = LANES
    blocks = rows // size
    nt = (((1,), (1,)), ((), ()))
    scores[...] = lax.dot_general(
        conv_ref[:, channels + N :], conv_ref[:, channels : channels + N], nt, preferred_element_type=F32
    )
    lower = lax.broadcasted_iota(jnp.int32, (size, size), 0) >= lax.broadcasted_iota(
        jnp.int32, (size, size), 1
    )
    left = lax.broadcasted_iota(jnp.int32, (size, 2 * P_SIZE), 1) < P_SIZE
    for pair in range(channels // (2 * P_SIZE)):
        cols = slice(pair * 2 * P_SIZE, (pair + 1) * 2 * P_SIZE)
        for a in range(blocks):
            t = slice(a * size, (a + 1) * size)
            products = []
            for h in (2 * pair, 2 * pair + 1):
                here = cum_ref[t, h : h + 1]
                own = jnp.where(lower, here - shift_t_ref[h : h + 1, t], -jnp.inf)
                weights = jnp.exp(own) * scores[t, t]
                if a > 0:
                    before = slice(0, a * size)
                    earlier = jnp.exp(here - shift_t_ref[h : h + 1, before]) * scores[t, before]
                    weights = jnp.concatenate([earlier, weights], 1)
                products.append(dot32(weights.astype(BF16), conv_ref[: (a + 1) * size, cols]))
            y_ref[t, cols] = jnp.where(left, products[0], products[1]) + skip_ref[:, cols] * conv_ref[
                t, cols
            ].astype(F32)


def inner_output(conved, cum, shift_t, skip, after):
    rows, width = conved.shape
    channels = width - 2 * N
    return pl.pallas_call(
        inner_kernel,
        in_specs=[VMEM] * 4 + [ANY] * len(after),
        out_specs=VMEM,
        out_shape=shape_of((rows, channels), F32),
        scratch_shapes=[pltpu.VMEM((rows, rows), F32)],
        cost_estimate=cost(2 * rows * rows * channels, 8 * rows * width, rows * rows * channels // P_SIZE),
        name="inner",
        compiler_params=params(MAIN_MIB),
    )(conved, cum, shift_t, skip, *after)


def falls_kernel(n, plan, place_ref, *refs):
    logs, out_ref = refs[:n], refs[-1]
    values = []
    for log in logs:
        block = log[...].astype(F32)
        values.append(sum(block[i : i + 1] for i in range(LOG_PARTS)))
    index = lax.broadcasted_iota(jnp.int32, out_ref.shape, 0)
    block = jnp.zeros(out_ref.shape, F32)
    for i, (counts, parts) in enumerate(plan(place_ref[1], n)):
        total = jnp.zeros_like(values[0])
        for present, offset in parts:
            total = total + jnp.where(present, values[offset], 0.0)
        block = jnp.where(index == i, jnp.where(counts, jnp.exp(total), 0.0), block)
    out_ref[...] = block


def falls(plan, place, logs, after):
    n = len(logs)
    channels = logs[0][0].shape[1]
    rows = -(-len(plan(0, n)) // 8) * 8
    return pl.pallas_call(
        functools.partial(falls_kernel, n, plan),
        grid_spec=pltpu.PrefetchScalarGridSpec(
            num_scalar_prefetch=1,
            grid=(1,),
            in_specs=[pl.BlockSpec((EDGE, channels), lambda i, place, at=at: (at, 0)) for _, at in logs]
            + [ANY] * len(after),
            out_specs=pl.BlockSpec((rows, channels), lambda i, place: (0, 0)),
        ),
        out_shape=shape_of((rows, channels), F32),
        name="falls",
        compiler_params=params(8),
    )(place, *[array for array, _ in logs], *after)


def scan_plan(me, n):
    out, before = [], []
    bit = 1
    while bit < n:
        later = (me & bit) > 0
        own_span = [(True, j) for j in range(bit)]
        got_span = [(True, j) for j in range(bit, 2 * bit)]
        out.append((True, [(jnp.logical_not(later), j) for _, j in got_span]))
        out.append((True, [(later, j) for _, j in own_span]))
        out.append((later, list(before)))
        before += [(later, j) for _, j in got_span]
        bit *= 2
    return out + [(True, before)]


def swap_plan(me, n):
    low, high = (me & 1) > 0, (me & 2) > 0
    return [
        (jnp.logical_not(low), []),
        (high, [(jnp.logical_not(low), 0), (jnp.logical_not(low), 3)]),
        (high, [(low, 1), (jnp.logical_not(low), 3)]),
        (True, []),
        (True, []),
        (True, []),
    ]


def both_plans(me, n):
    return scan_plan(me, n) + (swap_plan(me, n) if n == 4 else [])


def merge_kernel(row, falls_ref, own_ref, got_ref, *refs):
    own_fall, got_fall = falls_ref[row : row + 1], falls_ref[row + 1 : row + 2]
    refs[-1][...] = (own_fall * own_ref[...].astype(F32) + got_fall * got_ref[...].astype(F32)).astype(BF16)


def merged(row, factors, own, got, after):
    return pl.pallas_call(
        functools.partial(merge_kernel, row),
        in_specs=[VMEM] * 3 + [ANY] * len(after),
        out_specs=VMEM,
        out_shape=shape_of(own.shape, BF16),
        cost_estimate=cost(4 * own.size, 6 * own.size),
        name="merge",
        compiler_params=params(12),
    )(factors, own, got, *after)


def final_kernel(whole_group, plans, init_row, place_ref, *refs):
    rounds = sum(len(rows) for rows in plans)
    values, totals, lasts = refs[:EARLY], refs[EARLY:SLOTS], refs[SLOTS : 2 * SLOTS - EARLY]
    refs = refs[2 * SLOTS - EARLY :]
    gots, refs = refs[:rounds], refs[rounds:]
    y_ref, conv_ref, init_ref, cum_ref, scale_ref, gain_ref, falls_ref = refs[:7]
    outs = refs[7:]
    part, channels = totals[0].shape
    slot = place_ref[0]
    hits = head_spread(channels // P_SIZE)
    size = channels // len(plans)
    states = []
    for i, rows in enumerate(plans):
        cols = slice(i * size, (i + 1) * size)
        states.append(
            sum(
                falls_ref[row : row + 1, cols] * got[...].astype(F32)
                for row, got in zip(rows, gots[i * len(rows) : (i + 1) * len(rows)])
            )
        )
    state = jnp.concatenate(states, 1).astype(BF16)
    init = init_ref[...].astype(BF16)
    init_fall = falls_ref[init_row : init_row + 1]
    nt = (((1,), (1,)), ((), ()))
    for k, value in enumerate(quarter_values(values, totals, lasts, scale_ref[...])):
        at = pl.ds(pl.multiple_of((slot ^ k) * part, part), part)
        c_part = conv_ref[at, channels + N :]
        carried = dot32(c_part, state)
        carried = carried + init_fall * lax.dot_general(c_part, init, nt, preferred_element_type=F32)
        y = y_ref[at] + carried * spread_heads(jnp.exp(cum_ref[at]), hits)
        gated = y * silu(value.astype(F32))
        squares = jnp.sum(gated * gated, axis=1, keepdims=True)
        if whole_group:
            meansq = squares / (H // G * P_SIZE)
            outs[0][at] = (gated * lax.rsqrt(meansq + 1e-05) * gain_ref[...]).astype(BF16)
        else:
            outs[0][at] = gated
            outs[1][at] = jnp.broadcast_to(squares, (part, LANES))


def final_output(whole_group, plans, init_row, place, values, totals, lasts, gots, y, conved, init, cum, scale, gain, factors):
    rows, channels = y.shape
    if whole_group:
        outs = [shape_of((rows, channels), BF16)]
    else:
        outs = [shape_of((rows, channels), F32), shape_of((rows, LANES), F32)]
    return pl.pallas_call(
        functools.partial(final_kernel, whole_group, plans, init_row),
        in_specs=[SMEM] + [VMEM] * (2 * SLOTS - EARLY + 7 + len(gots)),
        out_specs=[VMEM] * len(outs),
        out_shape=outs,
        cost_estimate=cost(2 * rows * channels * N, 12 * rows * channels, 2 * rows * channels),
        name="final",
        compiler_params=params(MAIN_MIB),
    )(place, *values, *totals, *lasts, *gots, y, conved, init, cum, scale, gain, factors)


def body(
    tokens,
    w_zx,
    zx_scale,
    w_bc,
    bc_scale,
    w_dt,
    conv_x,
    conv_bc,
    tail_x,
    tail_bc,
    head_params,
    init_state,
    norm_gain,
):
    tok_rows = tokens.shape[0]
    depth = w_zx.shape[0]
    local_heads = head_params.shape[1]
    channels = local_heads * P_SIZE
    per_group = H // G
    n_ctx = lax.axis_size("ctx")
    me = lax.axis_index("ctx")
    head_place = lax.axis_index("head")
    group_index = head_place * local_heads // per_group
    bits = [1 << i for i in range(n_ctx.bit_length() - 1)]
    part = tok_rows // SLOTS
    slot = head_place % SLOTS
    place = jnp.stack([slot.astype(jnp.int32), me.astype(jnp.int32)])

    dt_t = w_dt.T
    if local_heads % EDGE:
        dt_t = jnp.pad(dt_t, ((0, EDGE - local_heads % EDGE), (0, 0)))
    payloads = pack(place, tokens, dt_t, n_ctx)
    payloads = [swapped(one, "ctx", j) for j, one in enumerate(payloads, 1)]
    w_all = jnp.transpose(w_zx, (1, 0, 2))
    bc_rows = pick_group(w_bc, group_index, 1)
    scale = jnp.concatenate([zx_scale[1], pick_group(bc_scale, group_index, 0)], 0)[None]
    taps = jnp.concatenate([conv_x, pick_group(conv_bc, group_index, 1)], 1)
    before = jnp.concatenate([tail_x, pick_group(tail_bc, group_index, 1)], 1)
    before = jnp.pad(before, ((EDGE - (K - 1), 0), (0, 0)))
    skip = jnp.repeat(head_params[2], P_SIZE)[None]
    gate_w, first_w = weights(w_all, bc_rows, (scale, taps, before, skip))

    def blocks_of(rows):
        return [rows[i * part : (i + 1) * part] for i in range(n_ctx - 1)]

    one_way, other_way = bits, bits[::-1]
    gate0 = Reduction([one[:part] for one in payloads], one_way, gate_w)
    first0 = Reduction([one[: part + EDGE] for one in payloads], other_way, first_w)
    mark = gate0.send(first_w)
    mark = first0.send(mark)
    fetched = join(payloads, part, (mark,))
    from_chip = swapped(fetched, "head", 2)
    from_core = swapped(fetched, "head", 1)
    first1 = Reduction(blocks_of(from_core), one_way, first_w)
    gate1 = Reduction(blocks_of(from_core), other_way, gate_w)
    mark = first1.send(fetched)
    shift_t, cum, fade, logs = step_sizes(place, tokens, dt_t, payloads, head_params.T, (mark,))
    mark = gate1.send(cum, logs if n_ctx == 4 else None)
    own_rows = lax.dynamic_slice_in_dim(chained([tokens], mark)[0], me * depth, depth, 1)
    own = [lax.dynamic_slice_in_dim(own_rows, (slot ^ k) * part, part, 0) for k in range(SLOTS)]
    mark = first0.keep(jnp.concatenate([own[0], own_rows[tok_rows - EDGE :]], 0), mark)
    mark = first1.keep(own[1], mark)
    mark = gate0.keep(own[0], mark)
    from_chip = chained([from_chip], mark)[0]
    from_both = swapped(from_chip, "head", 1)
    first2, gate2 = (Reduction(blocks_of(from_chip), other_way, w) for w in (first_w, gate_w))
    first3, gate3 = (Reduction(blocks_of(from_both), one_way, w) for w in (first_w, gate_w))
    mark = first2.send(mark)
    mark = first3.send(mark)
    mark = gate1.keep(own[1], mark)
    firsts01 = finish(
        "fin_first", (first0.total, first1.total), (first0.last, first1.last), scale, (mark,)
    )
    gates01 = finish(
        "fin_gate", (gate0.total, gate1.total), (gate0.last, gate1.last), zx_scale[0:1], (firsts01[0],)
    )
    if n_ctx == 4:
        at = part // EDGE
        got, last = chained([gate1.got, gate1.last], gates01[0])
        by_ctx = [(logs, 0), (last, at), (got, 2 * at), (last, at + 1)]
    else:
        by_ctx = [(logs, 0)] + [(swapped(logs, "ctx", j), 0) for j in range(1, n_ctx)]
    factors = falls(both_plans, place, by_ctx, (gates01[0],))
    arrived = passed_along(chained([firsts01[0][part:]], factors)[0], "ctx", 1)
    mark = first2.keep(own[2], arrived)
    mark = first3.keep(own[3], mark)
    mark = gate2.send(mark)
    mark = gate3.send(mark)

    halves = 2 if n_ctx == 4 else 1
    conved, *local_states = conv_and_state(
        halves, place, firsts01, (first2.total, first3.total), (first2.last, first3.last), arrived, before, scale,
        taps, fade, (mark,),
    )
    mark = gate2.keep(own[2], conved)
    mark = gate3.keep(own[3], mark)
    gots, plans, runs, start = [], [], [], 0
    for half, run in enumerate(local_states):
        order = bits[::-1] if half else bits
        rows = []
        for i, bit in enumerate(order):
            if i < len(bits) - 1 or half:
                gots.append(swapped(run, "ctx", bit))
            else:
                gots.append(passed_along(run, "ctx", bit))
            if i < len(bits) - 1:
                size = run.shape[1]
                share = factors[:, half * size : (half + 1) * size]
                run = merged(start + 3 * i, share, run, gots[-1], (mark,))
            rows.append(start + 3 * i + 2)
        runs.append(run)
        plans.append(tuple(rows))
        start += 3 * len(bits) + 1
    init_row = 3 * len(bits)
    y_local = inner_output(conved, cum, shift_t, skip, tuple(runs))

    whole_group = local_heads >= per_group
    outs = final_output(
        whole_group,
        tuple(plans),
        init_row,
        place,
        gates01,
        (gate2.total, gate3.total),
        (gate2.last, gate3.last),
        gots,
        y_local,
        conved,
        init_state.reshape(channels, N),
        cum,
        zx_scale[0:1],
        norm_gain[None],
        factors,
    )
    if whole_group:
        return outs[0]
    gated, squares = outs
    slot_hits = (jnp.arange(G) == group_index).astype(F32)
    group_sums = lax.psum(slot_hits[:, None] * squares[:, 0][None, :], "head")
    totals = lax.dynamic_index_in_dim(group_sums, group_index, 0, keepdims=False)
    meansq = totals / (per_group * P_SIZE)
    return (gated * lax.rsqrt(meansq + 1e-05)[:, None] * norm_gain).astype(BF16)


def solution(mesh):
    return jax.shard_map(
        body,
        mesh=mesh,
        in_specs=(
            P("ctx", None),
            P("ctx", None, "head"),
            P(None, "head"),
            P("ctx", None, None),
            P(),
            P("ctx", "head"),
            P(None, "head"),
            P(),
            P(None, "head"),
            P(),
            P(None, "head"),
            P("head", None, None),
            P("head"),
        ),
        out_specs=P("ctx", "head"),
        check_vma=False,
    )
```

```python
import functools
import jax
import jax.numpy as jnp
from jax import lax
from jax.experimental import pallas as pl
from jax.experimental.pallas import tpu as pltpu
from jax.sharding import PartitionSpec as P

H = 128
P_SIZE = 64
N = 256
G = 8
K = 4
SLOTS = 4
LANES = 128
EDGE = 16
EARLY = 2
LOG_PARTS = 3
MIB = 1 << 20
MAIN_MIB = 32
SCALE = 64
BF16 = jnp.bfloat16
F32 = jnp.float32
VMEM = pl.BlockSpec(memory_space=pltpu.VMEM)
SMEM = pl.BlockSpec(memory_space=pltpu.SMEM)
ANY = pl.BlockSpec(memory_space=pl.ANY)


def shape_of(shape, dtype):
    return jax.ShapeDtypeStruct(shape, dtype)


def params(mib):
    return pltpu.CompilerParams(vmem_limit_bytes=mib * MIB)


def cost(flops, moved, transcendentals=0):
    return pl.CostEstimate(
        flops=int(flops) // SCALE, bytes_accessed=int(moved) // SCALE, transcendentals=int(transcendentals) // SCALE
    )


def chained(values, after):
    return lax.optimization_barrier((*values, after))[: len(values)]


def passed_along(x, axis, by):
    length = lax.axis_size(axis)
    pairs = [(i, i + by) for i in range(length) if 0 <= i + by < length]
    return lax.ppermute(x, axis, pairs)


def swapped(x, axis, by):
    length = lax.axis_size(axis)
    return lax.ppermute(x, axis, [(i, i ^ by) for i in range(length)])


def pick_group(values, group_index, axis_index):
    return lax.dynamic_index_in_dim(values, group_index, axis_index, keepdims=False)


def dot32(a, b):
    return jnp.dot(a, b, preferred_element_type=F32)


def silu(v):
    return v / (1.0 + jnp.exp(-v))


def pack_kernel(n, place_ref, *refs):
    blocks, tails, dt_ref, outs = refs[: n - 1], refs[n - 1 : 2 * n - 2], refs[2 * n - 2], refs[2 * n - 1 :]
    part, edge = blocks[0].shape[0], tails[0].shape[0]
    for block, tail, out in zip(blocks, tails, outs):
        out[:part] = block[...]
        out[part : part + edge] = tail[...]
        out[part + edge :] = dt_ref[...]


def pack(place, tokens, dt_t, n):
    dt_rows, depth = dt_t.shape
    part = tokens.shape[0] // SLOTS
    height = part + EDGE + dt_rows
    last = tokens.shape[0] // EDGE - 1
    return pl.pallas_call(
        functools.partial(pack_kernel, n),
        grid_spec=pltpu.PrefetchScalarGridSpec(
            num_scalar_prefetch=1,
            grid=(1,),
            in_specs=[
                pl.BlockSpec((part, depth), lambda i, place, j=j: (place[0], place[1] ^ j))
                for j in range(1, n)
            ]
            + [pl.BlockSpec((EDGE, depth), lambda i, place, j=j: (last, place[1] ^ j)) for j in range(1, n)]
            + [pl.BlockSpec((dt_rows, depth), lambda i, place: (0, 0))],
            out_specs=[pl.BlockSpec((height, depth), lambda i, place: (0, 0))] * (n - 1),
        ),
        out_shape=[shape_of((height, depth), BF16)] * (n - 1),
        name="pack",
        compiler_params=params(58),
    )(place, *[tokens] * (2 * n - 2), dt_t)


def join_kernel(part, count, *refs):
    blocks, out = refs[:count], refs[-1]
    for i, block in enumerate(blocks):
        out[i * part : (i + 1) * part] = block[:part]


def join(blocks, part, after):
    depth = blocks[0].shape[1]
    return pl.pallas_call(
        functools.partial(join_kernel, part, len(blocks)),
        in_specs=[VMEM] * len(blocks) + [ANY] * len(after),
        out_specs=VMEM,
        out_shape=shape_of((part * len(blocks), depth), BF16),
        name="join",
        compiler_params=params(MAIN_MIB),
    )(*blocks, *after)


class Reduction:
    def __init__(self, blocks, order, weights):
        self.blocks, self.order, self.weights = blocks, order, weights
        self.part = blocks[0].shape[0]
        self.n = len(blocks) + 1

    def rows(self, offsets, after):
        return jnp.concatenate(chained([self.blocks[j - 1] for j in offsets], after), 0)

    def send(self, after, extra=None):
        offsets = [j for j in range(self.n) if j & self.order[0]]
        out = dot32(self.rows(offsets, after), self.weights).astype(BF16)
        self.extra = extra
        if extra is not None:
            out = jnp.concatenate([out, extra], 0)
        self.got = swapped(out, "ctx", self.order[0])
        return out

    def keep(self, own, after):
        self.blocks = [*self.blocks, own]
        kept = [j for j in range(self.n) if not j & self.order[0]]
        size = self.part
        got = [self.got[i * size : (i + 1) * size] for i in range(len(kept))]
        bit = self.order[1]
        gone = [i for i, j in enumerate(kept) if j & bit]
        stay = [i for i, j in enumerate(kept) if not j & bit]
        rows = self.rows([kept[i] for i in gone], after)
        out = (dot32(rows, self.weights) + jnp.concatenate([got[i] for i in gone], 0)).astype(BF16)
        mark = out
        if self.extra is not None:
            out = jnp.concatenate([out, self.extra, self.got[size * len(kept) :]], 0)
        arrived = swapped(out, "ctx", bit)
        rows = self.rows([kept[i] for i in stay], after)
        total = dot32(rows, self.weights) + jnp.concatenate([got[i] for i in stay], 0)
        kept = [kept[i] for i in stay]
        for bit in self.order[2:]:
            total = total + arrived.astype(F32)
            gone = [i for i, j in enumerate(kept) if j & bit]
            stay = [i for i, j in enumerate(kept) if not j & bit]
            parts = [total[i * size : (i + 1) * size] for i in range(len(kept))]
            out = jnp.concatenate([parts[i] for i in gone], 0).astype(BF16)
            total = jnp.concatenate([parts[i] for i in stay], 0)
            arrived = swapped(out, "ctx", bit)
            kept = [kept[i] for i in stay]
        self.total, self.last = total, arrived
        return mark


def finished(total, last, scale):
    return ((total + last.astype(F32)) * scale).astype(BF16)


def finish_kernel(count, *refs):
    totals, lasts, scale_ref, outs = refs[:count], refs[count : 2 * count], refs[2 * count], refs[-count:]
    for total, last, out in zip(totals, lasts, outs):
        out[...] = finished(total[...], last[: total.shape[0]], scale_ref[...])


def finish(name, totals, lasts, scale, after):
    count = len(totals)
    lasts = chained(lasts, after[0])
    return pl.pallas_call(
        functools.partial(finish_kernel, count),
        in_specs=[VMEM] * (2 * count + 1) + [ANY] * len(after),
        out_specs=[VMEM] * count,
        out_shape=[shape_of(t.shape, BF16) for t in totals],
        cost_estimate=cost(4 * count * totals[0].size, 8 * count * totals[0].size),
        name=name,
        compiler_params=params(12),
    )(*totals, *lasts, scale, *after)


def quarter_values(values, totals, lasts, scale):
    early = [v[...] for v in values]
    return early + [finished(t[...], l[...], scale) for t, l in zip(totals, lasts)]


def step_kernel(n, me_ref, tok_ref, *refs):
    weights, heads_ref = refs[:n], refs[n]
    shift_t_ref, cum_ref, fade_ref, log_ref, acc = refs[-5:]
    j = pl.program_id(0)

    @pl.when(j == 0)
    def _():
        acc[...] = jnp.zeros_like(acc)

    for i in range(n):

        @pl.when(j == i)
        def _():
            acc[...] += lax.dot_general(
                weights[i][...], tok_ref[...], (((1,), (1,)), ((), ())), preferred_element_type=F32
            )

    @pl.when(j == pl.num_programs(0) - 1)
    def _():
        v = acc[: heads_ref.shape[0]] + heads_ref[:, 0:1]
        step = jnp.maximum(v, 0.0) + jnp.log1p(jnp.exp(-jnp.abs(v)))
        rate = -jnp.exp(heads_ref[:, 1:2]) * step
        rows = rate.shape[1]
        up_to = lax.broadcasted_iota(jnp.int32, (rows, rows), 0) <= lax.broadcasted_iota(
            jnp.int32, (rows, rows), 1
        )
        cum = jnp.dot(
            rate, up_to.astype(F32), precision=lax.Precision.HIGHEST, preferred_element_type=F32
        )
        last = cum[:, rows - 1 : rows]
        shift_t_ref[...] = cum - jnp.log(step)
        cum_ref[...] = cum.T
        fade_ref[...] = (jnp.exp(last - cum) * step).T
        left = jnp.broadcast_to(last.T, (8, last.shape[0]))
        hits = head_spread(last.shape[0])
        index = lax.broadcasted_iota(jnp.int32, log_ref.shape, 0)
        block = jnp.zeros(log_ref.shape, F32)
        for i in range(LOG_PARTS):
            term = left.astype(BF16)
            left = left - term.astype(F32)
            block = jnp.where(index == i, dot32(term, hits)[0:1], block)
        log_ref[...] = block.astype(BF16)


def step_sizes(place, tokens, dt_t, payloads, heads, after):
    dt_rows, depth = dt_t.shape
    local_heads = heads.shape[0]
    n = len(payloads) + 1
    rows = tokens.shape[0]
    last = payloads[0].shape[0] // dt_rows - 1
    whole = lambda shape: pl.BlockSpec(shape, lambda j, place: (0, 0))
    return pl.pallas_call(
        functools.partial(step_kernel, n),
        grid_spec=pltpu.PrefetchScalarGridSpec(
            num_scalar_prefetch=1,
            grid=(n,),
            in_specs=[
                pl.BlockSpec((rows, depth), lambda j, place: (0, place[1] ^ j)),
                whole((dt_rows, depth)),
            ]
            + [pl.BlockSpec((dt_rows, depth), lambda j, place: (last, 0))] * (n - 1)
            + [whole((local_heads, 3))]
            + [ANY] * len(after),
            out_specs=[
                whole((local_heads, rows)),
                whole((rows, local_heads)),
                whole((rows, local_heads)),
                whole((EDGE, local_heads * P_SIZE)),
            ],
            scratch_shapes=[pltpu.VMEM((dt_rows, rows), F32)],
        ),
        out_shape=[
            shape_of((local_heads, rows), F32),
            shape_of((rows, local_heads), F32),
            shape_of((rows, local_heads), F32),
            shape_of((EDGE, local_heads * P_SIZE), BF16),
        ],
        cost_estimate=cost(2 * n * rows * depth * LANES, 2 * n * rows * depth),
        name="steps",
        compiler_params=params(MAIN_MIB),
    )(place, tokens, dt_t, *payloads, heads, *after)


def head_spread(local_heads):
    channels = local_heads * P_SIZE
    hit = (
        lax.broadcasted_iota(jnp.int32, (local_heads, channels), 1) // P_SIZE
        == lax.broadcasted_iota(jnp.int32, (local_heads, channels), 0)
    )
    return hit.astype(F32).astype(BF16)


def spread_heads(values, hits):
    high = values.astype(BF16)
    low = (values - high.astype(F32)).astype(BF16)
    return dot32(high, hits) + dot32(low, hits)


def conv_kernel(count, place_ref, *refs):
    values, totals, lasts = refs[:EARLY], refs[EARLY:SLOTS], refs[SLOTS : 2 * SLOTS - EARLY]
    arrived_ref, before_ref, scale_ref, taps_ref, fade_ref = refs[2 * SLOTS - EARLY : 2 * SLOTS - EARLY + 5]
    conv_ref, states, vals = refs[-2 - count], refs[-1 - count : -1], refs[-1]
    part, width = totals[0].shape
    rows = part * SLOTS
    channels = width - 2 * N
    slot = place_ref[0]
    first = place_ref[1] == 0
    vals[:EDGE] = jnp.where(first, before_ref[...].astype(F32), arrived_ref[...].astype(F32))
    for k, value in enumerate(quarter_values(values, totals, lasts, scale_ref[...])):
        start = pl.multiple_of(EDGE + (slot ^ k) * part, EDGE)
        vals[pl.ds(start, part)] = value[:part].astype(F32)
    for c in range(0, width, 2 * LANES):
        cols = slice(c, c + 2 * LANES)
        for r in range(0, rows, part):
            summed = taps_ref[K : K + 1, cols]
            for tap in range(K):
                at = r + EDGE - (K - 1) + tap
                summed = summed + taps_ref[tap : tap + 1, cols] * vals[at : at + part, cols]
            conv_ref[r : r + part, cols] = silu(summed).astype(BF16)
    hits = head_spread(channels // P_SIZE)
    faded = spread_heads(fade_ref[...], hits) * conv_ref[:, :channels].astype(F32)
    state = lax.dot_general(
        conv_ref[:, channels : channels + N],
        faded.astype(BF16),
        (((0,), (0,)), ((), ())),
        preferred_element_type=F32,
    ).astype(BF16)
    size = channels // len(states)
    for i, out in enumerate(states):
        out[...] = state[:, i * size : (i + 1) * size]


def conv_and_state(count, place, values, totals, lasts, arrived, before, scale, taps, fade, after):
    part, width = totals[0].shape
    rows = part * SLOTS
    return pl.pallas_call(
        functools.partial(conv_kernel, count),
        in_specs=[SMEM] + [VMEM] * (2 * SLOTS - EARLY + 5) + [ANY] * len(after),
        out_specs=[VMEM] * (1 + count),
        out_shape=[shape_of((rows, width), BF16)] + [shape_of((N, (width - 2 * N) // count), BF16)] * count,
        scratch_shapes=[pltpu.VMEM((rows + EDGE, width), F32)],
        cost_estimate=cost(30 * rows * width, 12 * rows * width, 2 * rows * width),
        name="conv",
        compiler_params=params(MAIN_MIB),
    )(place, *values, *totals, *lasts, arrived, before, scale, taps, fade, *after)


def inner_kernel(conv_ref, cum_ref, shift_t_ref, skip_ref, *refs):
    y_ref, scores = refs[-2:]
    rows, width = conv_ref.shape
    channels = width - 2 * N
    size = LANES
    blocks = rows // size
    nt = (((1,), (1,)), ((), ()))
    scores[...] = lax.dot_general(
        conv_ref[:, channels + N :], conv_ref[:, channels : channels + N], nt, preferred_element_type=F32
    )
    lower = lax.broadcasted_iota(jnp.int32, (size, size), 0) >= lax.broadcasted_iota(
        jnp.int32, (size, size), 1
    )
    left = lax.broadcasted_iota(jnp.int32, (size, 2 * P_SIZE), 1) < P_SIZE
    for pair in range(channels // (2 * P_SIZE)):
        cols = slice(pair * 2 * P_SIZE, (pair + 1) * 2 * P_SIZE)
        for a in range(blocks):
            t = slice(a * size, (a + 1) * size)
            products = []
            for h in (2 * pair, 2 * pair + 1):
                here = cum_ref[t, h : h + 1]
                own = jnp.where(lower, here - shift_t_ref[h : h + 1, t], -jnp.inf)
                weights = jnp.exp(own) * scores[t, t]
                if a > 0:
                    before = slice(0, a * size)
                    earlier = jnp.exp(here - shift_t_ref[h : h + 1, before]) * scores[t, before]
                    weights = jnp.concatenate([earlier, weights], 1)
                products.append(dot32(weights.astype(BF16), conv_ref[: (a + 1) * size, cols]))
            y_ref[t, cols] = jnp.where(left, products[0], products[1]) + skip_ref[:, cols] * conv_ref[
                t, cols
            ].astype(F32)


def inner_output(conved, cum, shift_t, skip, after):
    rows, width = conved.shape
    channels = width - 2 * N
    return pl.pallas_call(
        inner_kernel,
        in_specs=[VMEM] * 4 + [ANY] * len(after),
        out_specs=VMEM,
        out_shape=shape_of((rows, channels), F32),
        scratch_shapes=[pltpu.VMEM((rows, rows), F32)],
        cost_estimate=cost(2 * rows * rows * channels, 8 * rows * width, rows * rows * channels // P_SIZE),
        name="inner",
        compiler_params=params(MAIN_MIB),
    )(conved, cum, shift_t, skip, *after)


def falls_kernel(n, plan, place_ref, *refs):
    logs, out_ref = refs[:n], refs[-1]
    values = []
    for log in logs:
        block = log[...].astype(F32)
        values.append(sum(block[i : i + 1] for i in range(LOG_PARTS)))
    index = lax.broadcasted_iota(jnp.int32, out_ref.shape, 0)
    block = jnp.zeros(out_ref.shape, F32)
    for i, (counts, parts) in enumerate(plan(place_ref[1], n)):
        total = jnp.zeros_like(values[0])
        for present, offset in parts:
            total = total + jnp.where(present, values[offset], 0.0)
        block = jnp.where(index == i, jnp.where(counts, jnp.exp(total), 0.0), block)
    out_ref[...] = block


def falls(plan, place, logs, after):
    n = len(logs)
    channels = logs[0][0].shape[1]
    rows = -(-len(plan(0, n)) // 8) * 8
    return pl.pallas_call(
        functools.partial(falls_kernel, n, plan),
        grid_spec=pltpu.PrefetchScalarGridSpec(
            num_scalar_prefetch=1,
            grid=(1,),
            in_specs=[pl.BlockSpec((EDGE, channels), lambda i, place, at=at: (at, 0)) for _, at in logs]
            + [ANY] * len(after),
            out_specs=pl.BlockSpec((rows, channels), lambda i, place: (0, 0)),
        ),
        out_shape=shape_of((rows, channels), F32),
        name="falls",
        compiler_params=params(8),
    )(place, *[array for array, _ in logs], *after)


def scan_plan(me, n):
    out, before = [], []
    bit = 1
    while bit < n:
        later = (me & bit) > 0
        own_span = [(True, j) for j in range(bit)]
        got_span = [(True, j) for j in range(bit, 2 * bit)]
        out.append((True, [(jnp.logical_not(later), j) for _, j in got_span]))
        out.append((True, [(later, j) for _, j in own_span]))
        out.append((later, list(before)))
        before += [(later, j) for _, j in got_span]
        bit *= 2
    return out + [(True, before)]


def swap_plan(me, n):
    low, high = (me & 1) > 0, (me & 2) > 0
    return [
        (jnp.logical_not(low), []),
        (high, [(jnp.logical_not(low), 0), (jnp.logical_not(low), 3)]),
        (high, [(low, 1), (jnp.logical_not(low), 3)]),
        (True, []),
        (True, []),
        (True, []),
    ]


def both_plans(me, n):
    return scan_plan(me, n) + (swap_plan(me, n) if n == 4 else [])


def merge_kernel(row, falls_ref, own_ref, got_ref, *refs):
    own_fall, got_fall = falls_ref[row : row + 1], falls_ref[row + 1 : row + 2]
    refs[-1][...] = (own_fall * own_ref[...].astype(F32) + got_fall * got_ref[...].astype(F32)).astype(BF16)


def merged(row, factors, own, got, after):
    return pl.pallas_call(
        functools.partial(merge_kernel, row),
        in_specs=[VMEM] * 3 + [ANY] * len(after),
        out_specs=VMEM,
        out_shape=shape_of(own.shape, BF16),
        cost_estimate=cost(4 * own.size, 6 * own.size),
        name="merge",
        compiler_params=params(12),
    )(factors, own, got, *after)


def final_kernel(whole_group, plans, init_row, place_ref, *refs):
    rounds = sum(len(rows) for rows in plans)
    values, totals, lasts = refs[:EARLY], refs[EARLY:SLOTS], refs[SLOTS : 2 * SLOTS - EARLY]
    refs = refs[2 * SLOTS - EARLY :]
    gots, refs = refs[:rounds], refs[rounds:]
    y_ref, conv_ref, init_ref, cum_ref, scale_ref, gain_ref, falls_ref = refs[:7]
    outs = refs[7:]
    part, channels = totals[0].shape
    slot = place_ref[0]
    hits = head_spread(channels // P_SIZE)
    size = channels // len(plans)
    states = []
    for i, rows in enumerate(plans):
        cols = slice(i * size, (i + 1) * size)
        states.append(
            sum(
                falls_ref[row : row + 1, cols] * got[...].astype(F32)
                for row, got in zip(rows, gots[i * len(rows) : (i + 1) * len(rows)])
            )
        )
    state = jnp.concatenate(states, 1).astype(BF16)
    init = init_ref[...].astype(BF16)
    init_fall = falls_ref[init_row : init_row + 1]
    nt = (((1,), (1,)), ((), ()))
    for k, value in enumerate(quarter_values(values, totals, lasts, scale_ref[...])):
        at = pl.ds(pl.multiple_of((slot ^ k) * part, part), part)
        c_part = conv_ref[at, channels + N :]
        carried = dot32(c_part, state)
        carried = carried + init_fall * lax.dot_general(c_part, init, nt, preferred_element_type=F32)
        y = y_ref[at] + carried * spread_heads(jnp.exp(cum_ref[at]), hits)
        gated = y * silu(value.astype(F32))
        squares = jnp.sum(gated * gated, axis=1, keepdims=True)
        if whole_group:
            meansq = squares / (H // G * P_SIZE)
            outs[0][at] = (gated * lax.rsqrt(meansq + 1e-05) * gain_ref[...]).astype(BF16)
        else:
            outs[0][at] = gated
            outs[1][at] = jnp.broadcast_to(squares, (part, LANES))


def final_output(whole_group, plans, init_row, place, values, totals, lasts, gots, y, conved, init, cum, scale, gain, factors):
    rows, channels = y.shape
    if whole_group:
        outs = [shape_of((rows, channels), BF16)]
    else:
        outs = [shape_of((rows, channels), F32), shape_of((rows, LANES), F32)]
    return pl.pallas_call(
        functools.partial(final_kernel, whole_group, plans, init_row),
        in_specs=[SMEM] + [VMEM] * (2 * SLOTS - EARLY + 7 + len(gots)),
        out_specs=[VMEM] * len(outs),
        out_shape=outs,
        cost_estimate=cost(2 * rows * channels * N, 12 * rows * channels, 2 * rows * channels),
        name="final",
        compiler_params=params(MAIN_MIB),
    )(place, *values, *totals, *lasts, *gots, y, conved, init, cum, scale, gain, factors)


def body(
    tokens,
    w_zx,
    zx_scale,
    w_bc,
    bc_scale,
    w_dt,
    conv_x,
    conv_bc,
    tail_x,
    tail_bc,
    head_params,
    init_state,
    norm_gain,
):
    tok_rows = tokens.shape[0]
    depth = w_zx.shape[0]
    local_heads = head_params.shape[1]
    channels = local_heads * P_SIZE
    per_group = H // G
    n_ctx = lax.axis_size("ctx")
    me = lax.axis_index("ctx")
    head_place = lax.axis_index("head")
    group_index = head_place * local_heads // per_group
    bits = [1 << i for i in range(n_ctx.bit_length() - 1)]
    part = tok_rows // SLOTS
    slot = head_place % SLOTS
    place = jnp.stack([slot.astype(jnp.int32), me.astype(jnp.int32)])

    dt_t = w_dt.T
    if local_heads % EDGE:
        dt_t = jnp.pad(dt_t, ((0, EDGE - local_heads % EDGE), (0, 0)))
    payloads = pack(place, tokens, dt_t, n_ctx)
    payloads = [swapped(one, "ctx", j) for j, one in enumerate(payloads, 1)]
    w_all = jnp.transpose(w_zx, (1, 0, 2))
    bc_rows = pick_group(w_bc, group_index, 1)
    scale = jnp.concatenate([zx_scale[1], pick_group(bc_scale, group_index, 0)], 0)[None]
    taps = jnp.concatenate([conv_x, pick_group(conv_bc, group_index, 1)], 1)
    before = jnp.concatenate([tail_x, pick_group(tail_bc, group_index, 1)], 1)
    before = jnp.pad(before, ((EDGE - (K - 1), 0), (0, 0)))
    skip = jnp.repeat(head_params[2], P_SIZE)[None]
    gate_w = w_all[0]
    first_w = jnp.concatenate([w_all[1], bc_rows], 1)

    def blocks_of(rows):
        return [rows[i * part : (i + 1) * part] for i in range(n_ctx - 1)]

    one_way, other_way = bits, bits[::-1]
    gate0 = Reduction([one[:part] for one in payloads], one_way, gate_w)
    first0 = Reduction([one[: part + EDGE] for one in payloads], other_way, first_w)
    mark = gate0.send((first_w, scale, taps, before, skip))
    mark = first0.send(mark)
    fetched = join(payloads, part, (mark,))
    from_chip = swapped(fetched, "head", 2)
    from_core = swapped(fetched, "head", 1)
    first1 = Reduction(blocks_of(from_core), one_way, first_w)
    gate1 = Reduction(blocks_of(from_core), other_way, gate_w)
    mark = first1.send(fetched)
    shift_t, cum, fade, logs = step_sizes(place, tokens, dt_t, payloads, head_params.T, (mark,))
    mark = gate1.send(cum, logs if n_ctx == 4 else None)
    own_rows = lax.dynamic_slice_in_dim(chained([tokens], mark)[0], me * depth, depth, 1)
    own = [lax.dynamic_slice_in_dim(own_rows, (slot ^ k) * part, part, 0) for k in range(SLOTS)]
    mark = first0.keep(jnp.concatenate([own[0], own_rows[tok_rows - EDGE :]], 0), mark)
    mark = first1.keep(own[1], mark)
    mark = gate0.keep(own[0], mark)
    mark = gate1.keep(own[1], mark)
    firsts01 = finish(
        "fin_first", (first0.total, first1.total), (first0.last, first1.last), scale, (mark,)
    )
    mark = firsts01[0]
    from_chip = chained([from_chip], mark)[0]
    from_both = swapped(from_chip, "head", 1)
    first2, gate2 = (Reduction(blocks_of(from_chip), other_way, w) for w in (first_w, gate_w))
    first3, gate3 = (Reduction(blocks_of(from_both), one_way, w) for w in (first_w, gate_w))
    mark = first2.send(mark)
    mark = first3.send(mark)
    arrived = passed_along(chained([firsts01[0][part:]], mark)[0], "ctx", 1)
    gates01 = finish(
        "fin_gate", (gate0.total, gate1.total), (gate0.last, gate1.last), zx_scale[0:1], (mark,)
    )
    if n_ctx == 4:
        at = part // EDGE
        got, last = chained([gate1.got, gate1.last], gates01[0])
        by_ctx = [(logs, 0), (last, at), (got, 2 * at), (last, at + 1)]
    else:
        by_ctx = [(logs, 0)] + [(swapped(logs, "ctx", j), 0) for j in range(1, n_ctx)]
    factors = falls(both_plans, place, by_ctx, (gates01[0],))
    mark = first2.keep(own[2], (gates01[0], arrived))
    mark = first3.keep(own[3], mark)
    mark = gate2.send(mark)
    mark = gate3.send(mark)

    halves = 2 if n_ctx == 4 else 1
    conved, *local_states = conv_and_state(
        halves, place, firsts01, (first2.total, first3.total), (first2.last, first3.last), arrived, before, scale,
        taps, fade, (mark,),
    )
    mark = gate2.keep(own[2], conved)
    mark = gate3.keep(own[3], mark)
    gots, plans, runs, start = [], [], [], 0
    for half, run in enumerate(local_states):
        order = bits[::-1] if half else bits
        rows = []
        for i, bit in enumerate(order):
            if i < len(bits) - 1 or half:
                gots.append(swapped(run, "ctx", bit))
            else:
                gots.append(passed_along(run, "ctx", bit))
            if i < len(bits) - 1:
                size = run.shape[1]
                share = factors[:, half * size : (half + 1) * size]
                run = merged(start + 3 * i, share, run, gots[-1], (mark,))
            rows.append(start + 3 * i + 2)
        runs.append(run)
        plans.append(tuple(rows))
        start += 3 * len(bits) + 1
    init_row = 3 * len(bits)
    y_local = inner_output(conved, cum, shift_t, skip, tuple(runs))

    whole_group = local_heads >= per_group
    outs = final_output(
        whole_group,
        tuple(plans),
        init_row,
        place,
        gates01,
        (gate2.total, gate3.total),
        (gate2.last, gate3.last),
        gots,
        y_local,
        conved,
        init_state.reshape(channels, N),
        cum,
        zx_scale[0:1],
        norm_gain[None],
        factors,
    )
    if whole_group:
        return outs[0]
    gated, squares = outs
    slot_hits = (jnp.arange(G) == group_index).astype(F32)
    group_sums = lax.psum(slot_hits[:, None] * squares[:, 0][None, :], "head")
    totals = lax.dynamic_index_in_dim(group_sums, group_index, 0, keepdims=False)
    meansq = totals / (per_group * P_SIZE)
    return (gated * lax.rsqrt(meansq + 1e-05)[:, None] * norm_gain).astype(BF16)


def solution(mesh):
    return jax.shard_map(
        body,
        mesh=mesh,
        in_specs=(
            P("ctx", None),
            P("ctx", None, "head"),
            P(None, "head"),
            P("ctx", None, None),
            P(),
            P("ctx", "head"),
            P(None, "head"),
            P(),
            P(None, "head"),
            P(),
            P(None, "head"),
            P("head", None, None),
            P("head"),
        ),
        out_specs=P("ctx", "head"),
        check_vma=False,
    )
```

```python
import functools
import jax
import jax.numpy as jnp
from jax import lax
from jax.experimental import pallas as pl
from jax.experimental.pallas import tpu as pltpu
from jax.sharding import PartitionSpec as P

H = 128
P_SIZE = 64
N = 256
G = 8
K = 4
SLOTS = 4
LANES = 128
EDGE = 16
EARLY = 2
LOG_PARTS = 3
MIB = 1 << 20
MAIN_MIB = 32
SCALE = 64
BF16 = jnp.bfloat16
F32 = jnp.float32
VMEM = pl.BlockSpec(memory_space=pltpu.VMEM)
SMEM = pl.BlockSpec(memory_space=pltpu.SMEM)
ANY = pl.BlockSpec(memory_space=pl.ANY)


def shape_of(shape, dtype):
    return jax.ShapeDtypeStruct(shape, dtype)


def params(mib):
    return pltpu.CompilerParams(vmem_limit_bytes=mib * MIB)


def cost(flops, moved, transcendentals=0):
    return pl.CostEstimate(
        flops=int(flops) // SCALE, bytes_accessed=int(moved) // SCALE, transcendentals=int(transcendentals) // SCALE
    )


def chained(values, after):
    return lax.optimization_barrier((*values, after))[: len(values)]


def passed_along(x, axis, by):
    length = lax.axis_size(axis)
    pairs = [(i, i + by) for i in range(length) if 0 <= i + by < length]
    return lax.ppermute(x, axis, pairs)


def swapped(x, axis, by):
    length = lax.axis_size(axis)
    return lax.ppermute(x, axis, [(i, i ^ by) for i in range(length)])


def pick_group(values, group_index, axis_index):
    return lax.dynamic_index_in_dim(values, group_index, axis_index, keepdims=False)


def dot32(a, b):
    return jnp.dot(a, b, preferred_element_type=F32)


def silu(v):
    return v / (1.0 + jnp.exp(-v))


def pack_kernel(n, place_ref, *refs):
    blocks, tails, dt_ref, outs = refs[: n - 1], refs[n - 1 : 2 * n - 2], refs[2 * n - 2], refs[2 * n - 1 :]
    part, edge = blocks[0].shape[0], tails[0].shape[0]
    for block, tail, out in zip(blocks, tails, outs):
        out[:part] = block[...]
        out[part : part + edge] = tail[...]
        out[part + edge :] = dt_ref[...]


def pack(place, tokens, dt_t, n):
    dt_rows, depth = dt_t.shape
    part = tokens.shape[0] // SLOTS
    height = part + EDGE + dt_rows
    last = tokens.shape[0] // EDGE - 1
    return pl.pallas_call(
        functools.partial(pack_kernel, n),
        grid_spec=pltpu.PrefetchScalarGridSpec(
            num_scalar_prefetch=1,
            grid=(1,),
            in_specs=[
                pl.BlockSpec((part, depth), lambda i, place, j=j: (place[0], place[1] ^ j))
                for j in range(1, n)
            ]
            + [pl.BlockSpec((EDGE, depth), lambda i, place, j=j: (last, place[1] ^ j)) for j in range(1, n)]
            + [pl.BlockSpec((dt_rows, depth), lambda i, place: (0, 0))],
            out_specs=[pl.BlockSpec((height, depth), lambda i, place: (0, 0))] * (n - 1),
        ),
        out_shape=[shape_of((height, depth), BF16)] * (n - 1),
        name="pack",
        compiler_params=params(58),
    )(place, *[tokens] * (2 * n - 2), dt_t)


def join_kernel(part, count, *refs):
    blocks, out = refs[:count], refs[-1]
    for i, block in enumerate(blocks):
        out[i * part : (i + 1) * part] = block[:part]


def join(blocks, part, after):
    depth = blocks[0].shape[1]
    return pl.pallas_call(
        functools.partial(join_kernel, part, len(blocks)),
        in_specs=[VMEM] * len(blocks) + [ANY] * len(after),
        out_specs=VMEM,
        out_shape=shape_of((part * len(blocks), depth), BF16),
        name="join",
        compiler_params=params(MAIN_MIB),
    )(*blocks, *after)


class Reduction:
    def __init__(self, blocks, order, weights):
        self.blocks, self.order, self.weights = blocks, order, weights
        self.part = blocks[0].shape[0]
        self.n = len(blocks) + 1

    def rows(self, offsets, after):
        return jnp.concatenate(chained([self.blocks[j - 1] for j in offsets], after), 0)

    def send(self, after, extra=None):
        offsets = [j for j in range(self.n) if j & self.order[0]]
        out = dot32(self.rows(offsets, after), self.weights).astype(BF16)
        self.extra = extra
        if extra is not None:
            out = jnp.concatenate([out, extra], 0)
        self.got = swapped(out, "ctx", self.order[0])
        return out

    def keep(self, own, after):
        self.blocks = [*self.blocks, own]
        kept = [j for j in range(self.n) if not j & self.order[0]]
        size = self.part
        got = [self.got[i * size : (i + 1) * size] for i in range(len(kept))]
        bit = self.order[1]
        gone = [i for i, j in enumerate(kept) if j & bit]
        stay = [i for i, j in enumerate(kept) if not j & bit]
        rows = self.rows([kept[i] for i in gone], after)
        out = (dot32(rows, self.weights) + jnp.concatenate([got[i] for i in gone], 0)).astype(BF16)
        mark = out
        if self.extra is not None:
            out = jnp.concatenate([out, self.extra, self.got[size * len(kept) :]], 0)
        arrived = swapped(out, "ctx", bit)
        rows = self.rows([kept[i] for i in stay], after)
        total = dot32(rows, self.weights) + jnp.concatenate([got[i] for i in stay], 0)
        kept = [kept[i] for i in stay]
        for bit in self.order[2:]:
            total = total + arrived.astype(F32)
            gone = [i for i, j in enumerate(kept) if j & bit]
            stay = [i for i, j in enumerate(kept) if not j & bit]
            parts = [total[i * size : (i + 1) * size] for i in range(len(kept))]
            out = jnp.concatenate([parts[i] for i in gone], 0).astype(BF16)
            total = jnp.concatenate([parts[i] for i in stay], 0)
            arrived = swapped(out, "ctx", bit)
            kept = [kept[i] for i in stay]
        self.total, self.last = total, arrived
        return mark


def finished(total, last, scale):
    return ((total + last.astype(F32)) * scale).astype(BF16)


def finish_kernel(count, *refs):
    totals, lasts, scale_ref, outs = refs[:count], refs[count : 2 * count], refs[2 * count], refs[-count:]
    for total, last, out in zip(totals, lasts, outs):
        out[...] = finished(total[...], last[: total.shape[0]], scale_ref[...])


def finish(name, totals, lasts, scale, after):
    count = len(totals)
    lasts = chained(lasts, after[0])
    return pl.pallas_call(
        functools.partial(finish_kernel, count),
        in_specs=[VMEM] * (2 * count + 1) + [ANY] * len(after),
        out_specs=[VMEM] * count,
        out_shape=[shape_of(t.shape, BF16) for t in totals],
        cost_estimate=cost(4 * count * totals[0].size, 8 * count * totals[0].size),
        name=name,
        compiler_params=params(12),
    )(*totals, *lasts, scale, *after)


def quarter_values(values, totals, lasts, scale):
    early = [v[...] for v in values]
    return early + [finished(t[...], l[...], scale) for t, l in zip(totals, lasts)]


def step_kernel(n, me_ref, tok_ref, *refs):
    weights, heads_ref = refs[:n], refs[n]
    shift_t_ref, cum_ref, fade_ref, log_ref, acc = refs[-5:]
    j = pl.program_id(0)

    @pl.when(j == 0)
    def _():
        acc[...] = jnp.zeros_like(acc)

    for i in range(n):

        @pl.when(j == i)
        def _():
            acc[...] += lax.dot_general(
                weights[i][...], tok_ref[...], (((1,), (1,)), ((), ())), preferred_element_type=F32
            )

    @pl.when(j == pl.num_programs(0) - 1)
    def _():
        v = acc[: heads_ref.shape[0]] + heads_ref[:, 0:1]
        step = jnp.maximum(v, 0.0) + jnp.log1p(jnp.exp(-jnp.abs(v)))
        rate = -jnp.exp(heads_ref[:, 1:2]) * step
        rows = rate.shape[1]
        up_to = lax.broadcasted_iota(jnp.int32, (rows, rows), 0) <= lax.broadcasted_iota(
            jnp.int32, (rows, rows), 1
        )
        cum = jnp.dot(
            rate, up_to.astype(F32), precision=lax.Precision.HIGHEST, preferred_element_type=F32
        )
        last = cum[:, rows - 1 : rows]
        shift_t_ref[...] = cum - jnp.log(step)
        cum_ref[...] = cum.T
        fade_ref[...] = (jnp.exp(last - cum) * step).T
        left = jnp.broadcast_to(last.T, (8, last.shape[0]))
        hits = head_spread(last.shape[0])
        index = lax.broadcasted_iota(jnp.int32, log_ref.shape, 0)
        block = jnp.zeros(log_ref.shape, F32)
        for i in range(LOG_PARTS):
            term = left.astype(BF16)
            left = left - term.astype(F32)
            block = jnp.where(index == i, dot32(term, hits)[0:1], block)
        log_ref[...] = block.astype(BF16)


def step_sizes(place, tokens, dt_t, payloads, heads, after):
    dt_rows, depth = dt_t.shape
    local_heads = heads.shape[0]
    n = len(payloads) + 1
    rows = tokens.shape[0]
    last = payloads[0].shape[0] // dt_rows - 1
    whole = lambda shape: pl.BlockSpec(shape, lambda j, place: (0, 0))
    return pl.pallas_call(
        functools.partial(step_kernel, n),
        grid_spec=pltpu.PrefetchScalarGridSpec(
            num_scalar_prefetch=1,
            grid=(n,),
            in_specs=[
                pl.BlockSpec((rows, depth), lambda j, place: (0, place[1] ^ j)),
                whole((dt_rows, depth)),
            ]
            + [pl.BlockSpec((dt_rows, depth), lambda j, place: (last, 0))] * (n - 1)
            + [whole((local_heads, 3))]
            + [ANY] * len(after),
            out_specs=[
                whole((local_heads, rows)),
                whole((rows, local_heads)),
                whole((rows, local_heads)),
                whole((EDGE, local_heads * P_SIZE)),
            ],
            scratch_shapes=[pltpu.VMEM((dt_rows, rows), F32)],
        ),
        out_shape=[
            shape_of((local_heads, rows), F32),
            shape_of((rows, local_heads), F32),
            shape_of((rows, local_heads), F32),
            shape_of((EDGE, local_heads * P_SIZE), BF16),
        ],
        cost_estimate=cost(2 * n * rows * depth * LANES, 2 * n * rows * depth),
        name="steps",
        compiler_params=params(MAIN_MIB),
    )(place, tokens, dt_t, *payloads, heads, *after)


def head_spread(local_heads):
    channels = local_heads * P_SIZE
    hit = (
        lax.broadcasted_iota(jnp.int32, (local_heads, channels), 1) // P_SIZE
        == lax.broadcasted_iota(jnp.int32, (local_heads, channels), 0)
    )
    return hit.astype(F32).astype(BF16)


def spread_heads(values, hits):
    high = values.astype(BF16)
    low = (values - high.astype(F32)).astype(BF16)
    return dot32(high, hits) + dot32(low, hits)


def conv_kernel(count, place_ref, *refs):
    values, totals, lasts = refs[:EARLY], refs[EARLY:SLOTS], refs[SLOTS : 2 * SLOTS - EARLY]
    arrived_ref, before_ref, scale_ref, taps_ref, fade_ref = refs[2 * SLOTS - EARLY : 2 * SLOTS - EARLY + 5]
    conv_ref, states, vals = refs[-2 - count], refs[-1 - count : -1], refs[-1]
    part, width = totals[0].shape
    rows = part * SLOTS
    channels = width - 2 * N
    slot = place_ref[0]
    first = place_ref[1] == 0
    vals[:EDGE] = jnp.where(first, before_ref[...].astype(F32), arrived_ref[...].astype(F32))
    for k, value in enumerate(quarter_values(values, totals, lasts, scale_ref[...])):
        start = pl.multiple_of(EDGE + (slot ^ k) * part, EDGE)
        vals[pl.ds(start, part)] = value[:part].astype(F32)
    for c in range(0, width, 2 * LANES):
        cols = slice(c, c + 2 * LANES)
        for r in range(0, rows, part):
            summed = taps_ref[K : K + 1, cols]
            for tap in range(K):
                at = r + EDGE - (K - 1) + tap
                summed = summed + taps_ref[tap : tap + 1, cols] * vals[at : at + part, cols]
            conv_ref[r : r + part, cols] = silu(summed).astype(BF16)
    hits = head_spread(channels // P_SIZE)
    faded = spread_heads(fade_ref[...], hits) * conv_ref[:, :channels].astype(F32)
    state = lax.dot_general(
        conv_ref[:, channels : channels + N],
        faded.astype(BF16),
        (((0,), (0,)), ((), ())),
        preferred_element_type=F32,
    ).astype(BF16)
    size = channels // len(states)
    for i, out in enumerate(states):
        out[...] = state[:, i * size : (i + 1) * size]


def conv_and_state(count, place, values, totals, lasts, arrived, before, scale, taps, fade, after):
    part, width = totals[0].shape
    rows = part * SLOTS
    lasts = chained(lasts, after[0])
    return pl.pallas_call(
        functools.partial(conv_kernel, count),
        in_specs=[SMEM] + [VMEM] * (2 * SLOTS - EARLY + 5) + [ANY] * len(after),
        out_specs=[VMEM] * (1 + count),
        out_shape=[shape_of((rows, width), BF16)] + [shape_of((N, (width - 2 * N) // count), BF16)] * count,
        scratch_shapes=[pltpu.VMEM((rows + EDGE, width), F32)],
        cost_estimate=cost(30 * rows * width, 12 * rows * width, 2 * rows * width),
        name="conv",
        compiler_params=params(MAIN_MIB),
    )(place, *values, *totals, *lasts, arrived, before, scale, taps, fade, *after)


def inner_kernel(conv_ref, cum_ref, shift_t_ref, skip_ref, *refs):
    y_ref, scores = refs[-2:]
    rows, width = conv_ref.shape
    channels = width - 2 * N
    size = LANES
    blocks = rows // size
    nt = (((1,), (1,)), ((), ()))
    scores[...] = lax.dot_general(
        conv_ref[:, channels + N :], conv_ref[:, channels : channels + N], nt, preferred_element_type=F32
    )
    lower = lax.broadcasted_iota(jnp.int32, (size, size), 0) >= lax.broadcasted_iota(
        jnp.int32, (size, size), 1
    )
    left = lax.broadcasted_iota(jnp.int32, (size, 2 * P_SIZE), 1) < P_SIZE
    for pair in range(channels // (2 * P_SIZE)):
        cols = slice(pair * 2 * P_SIZE, (pair + 1) * 2 * P_SIZE)
        for a in range(blocks):
            t = slice(a * size, (a + 1) * size)
            products = []
            for h in (2 * pair, 2 * pair + 1):
                here = cum_ref[t, h : h + 1]
                own = jnp.where(lower, here - shift_t_ref[h : h + 1, t], -jnp.inf)
                weights = jnp.exp(own) * scores[t, t]
                if a > 0:
                    before = slice(0, a * size)
                    earlier = jnp.exp(here - shift_t_ref[h : h + 1, before]) * scores[t, before]
                    weights = jnp.concatenate([earlier, weights], 1)
                products.append(dot32(weights.astype(BF16), conv_ref[: (a + 1) * size, cols]))
            y_ref[t, cols] = jnp.where(left, products[0], products[1]) + skip_ref[:, cols] * conv_ref[
                t, cols
            ].astype(F32)


def inner_output(conved, cum, shift_t, skip, after):
    rows, width = conved.shape
    channels = width - 2 * N
    return pl.pallas_call(
        inner_kernel,
        in_specs=[VMEM] * 4 + [ANY] * len(after),
        out_specs=VMEM,
        out_shape=shape_of((rows, channels), F32),
        scratch_shapes=[pltpu.VMEM((rows, rows), F32)],
        cost_estimate=cost(2 * rows * rows * channels, 8 * rows * width, rows * rows * channels // P_SIZE),
        name="inner",
        compiler_params=params(MAIN_MIB),
    )(conved, cum, shift_t, skip, *after)


def falls_kernel(n, plan, place_ref, *refs):
    logs, out_ref = refs[:n], refs[-1]
    values = []
    for log in logs:
        block = log[...].astype(F32)
        values.append(sum(block[i : i + 1] for i in range(LOG_PARTS)))
    index = lax.broadcasted_iota(jnp.int32, out_ref.shape, 0)
    block = jnp.zeros(out_ref.shape, F32)
    for i, (counts, parts) in enumerate(plan(place_ref[1], n)):
        total = jnp.zeros_like(values[0])
        for present, offset in parts:
            total = total + jnp.where(present, values[offset], 0.0)
        block = jnp.where(index == i, jnp.where(counts, jnp.exp(total), 0.0), block)
    out_ref[...] = block


def falls(plan, place, logs, after):
    n = len(logs)
    channels = logs[0][0].shape[1]
    rows = -(-len(plan(0, n)) // 8) * 8
    return pl.pallas_call(
        functools.partial(falls_kernel, n, plan),
        grid_spec=pltpu.PrefetchScalarGridSpec(
            num_scalar_prefetch=1,
            grid=(1,),
            in_specs=[pl.BlockSpec((EDGE, channels), lambda i, place, at=at: (at, 0)) for _, at in logs]
            + [ANY] * len(after),
            out_specs=pl.BlockSpec((rows, channels), lambda i, place: (0, 0)),
        ),
        out_shape=shape_of((rows, channels), F32),
        name="falls",
        compiler_params=params(8),
    )(place, *[array for array, _ in logs], *after)


def scan_plan(me, n):
    out, before = [], []
    bit = 1
    while bit < n:
        later = (me & bit) > 0
        own_span = [(True, j) for j in range(bit)]
        got_span = [(True, j) for j in range(bit, 2 * bit)]
        out.append((True, [(jnp.logical_not(later), j) for _, j in got_span]))
        out.append((True, [(later, j) for _, j in own_span]))
        out.append((later, list(before)))
        before += [(later, j) for _, j in got_span]
        bit *= 2
    return out + [(True, before)]


def swap_plan(me, n):
    low, high = (me & 1) > 0, (me & 2) > 0
    return [
        (jnp.logical_not(low), []),
        (high, [(jnp.logical_not(low), 0), (jnp.logical_not(low), 3)]),
        (high, [(low, 1), (jnp.logical_not(low), 3)]),
        (True, []),
        (True, []),
        (True, []),
    ]


def both_plans(me, n):
    return scan_plan(me, n) + (swap_plan(me, n) if n == 4 else [])


def merge_kernel(row, falls_ref, own_ref, got_ref, *refs):
    own_fall, got_fall = falls_ref[row : row + 1], falls_ref[row + 1 : row + 2]
    refs[-1][...] = (own_fall * own_ref[...].astype(F32) + got_fall * got_ref[...].astype(F32)).astype(BF16)


def merged(row, factors, own, got, after):
    return pl.pallas_call(
        functools.partial(merge_kernel, row),
        in_specs=[VMEM] * 3 + [ANY] * len(after),
        out_specs=VMEM,
        out_shape=shape_of(own.shape, BF16),
        cost_estimate=cost(4 * own.size, 6 * own.size),
        name="merge",
        compiler_params=params(12),
    )(factors, own, got, *after)


def final_kernel(whole_group, plans, init_row, place_ref, *refs):
    rounds = sum(len(rows) for rows in plans)
    values, totals, lasts = refs[:EARLY], refs[EARLY:SLOTS], refs[SLOTS : 2 * SLOTS - EARLY]
    refs = refs[2 * SLOTS - EARLY :]
    gots, refs = refs[:rounds], refs[rounds:]
    y_ref, conv_ref, init_ref, cum_ref, scale_ref, gain_ref, falls_ref = refs[:7]
    outs = refs[7:]
    part, channels = totals[0].shape
    slot = place_ref[0]
    hits = head_spread(channels // P_SIZE)
    size = channels // len(plans)
    states = []
    for i, rows in enumerate(plans):
        cols = slice(i * size, (i + 1) * size)
        states.append(
            sum(
                falls_ref[row : row + 1, cols] * got[...].astype(F32)
                for row, got in zip(rows, gots[i * len(rows) : (i + 1) * len(rows)])
            )
        )
    state = jnp.concatenate(states, 1).astype(BF16)
    init = init_ref[...].astype(BF16)
    init_fall = falls_ref[init_row : init_row + 1]
    nt = (((1,), (1,)), ((), ()))
    for k, value in enumerate(quarter_values(values, totals, lasts, scale_ref[...])):
        at = pl.ds(pl.multiple_of((slot ^ k) * part, part), part)
        c_part = conv_ref[at, channels + N :]
        carried = dot32(c_part, state)
        carried = carried + init_fall * lax.dot_general(c_part, init, nt, preferred_element_type=F32)
        y = y_ref[at] + carried * spread_heads(jnp.exp(cum_ref[at]), hits)
        gated = y * silu(value.astype(F32))
        squares = jnp.sum(gated * gated, axis=1, keepdims=True)
        if whole_group:
            meansq = squares / (H // G * P_SIZE)
            outs[0][at] = (gated * lax.rsqrt(meansq + 1e-05) * gain_ref[...]).astype(BF16)
        else:
            outs[0][at] = gated
            outs[1][at] = jnp.broadcast_to(squares, (part, LANES))


def final_output(whole_group, plans, init_row, place, values, totals, lasts, gots, y, conved, init, cum, scale, gain, factors):
    rows, channels = y.shape
    if whole_group:
        outs = [shape_of((rows, channels), BF16)]
    else:
        outs = [shape_of((rows, channels), F32), shape_of((rows, LANES), F32)]
    return pl.pallas_call(
        functools.partial(final_kernel, whole_group, plans, init_row),
        in_specs=[SMEM] + [VMEM] * (2 * SLOTS - EARLY + 7 + len(gots)),
        out_specs=[VMEM] * len(outs),
        out_shape=outs,
        cost_estimate=cost(2 * rows * channels * N, 12 * rows * channels, 2 * rows * channels),
        name="final",
        compiler_params=params(MAIN_MIB),
    )(place, *values, *totals, *lasts, *gots, y, conved, init, cum, scale, gain, factors)


def body(
    tokens,
    w_zx,
    zx_scale,
    w_bc,
    bc_scale,
    w_dt,
    conv_x,
    conv_bc,
    tail_x,
    tail_bc,
    head_params,
    init_state,
    norm_gain,
):
    tok_rows = tokens.shape[0]
    depth = w_zx.shape[0]
    local_heads = head_params.shape[1]
    channels = local_heads * P_SIZE
    per_group = H // G
    n_ctx = lax.axis_size("ctx")
    me = lax.axis_index("ctx")
    head_place = lax.axis_index("head")
    group_index = head_place * local_heads // per_group
    bits = [1 << i for i in range(n_ctx.bit_length() - 1)]
    part = tok_rows // SLOTS
    slot = head_place % SLOTS
    place = jnp.stack([slot.astype(jnp.int32), me.astype(jnp.int32)])

    dt_t = w_dt.T
    if local_heads % EDGE:
        dt_t = jnp.pad(dt_t, ((0, EDGE - local_heads % EDGE), (0, 0)))
    payloads = pack(place, tokens, dt_t, n_ctx)
    payloads = [swapped(one, "ctx", j) for j, one in enumerate(payloads, 1)]
    w_all = jnp.transpose(w_zx, (1, 0, 2))
    bc_rows = pick_group(w_bc, group_index, 1)
    scale = jnp.concatenate([zx_scale[1], pick_group(bc_scale, group_index, 0)], 0)[None]
    taps = jnp.concatenate([conv_x, pick_group(conv_bc, group_index, 1)], 1)
    before = jnp.concatenate([tail_x, pick_group(tail_bc, group_index, 1)], 1)
    before = jnp.pad(before, ((EDGE - (K - 1), 0), (0, 0)))
    skip = jnp.repeat(head_params[2], P_SIZE)[None]
    gate_w = w_all[0]
    first_w = jnp.concatenate([w_all[1], bc_rows], 1)

    def blocks_of(rows):
        return [rows[i * part : (i + 1) * part] for i in range(n_ctx - 1)]

    one_way, other_way = bits, bits[::-1]
    gate0 = Reduction([one[:part] for one in payloads], one_way, gate_w)
    first0 = Reduction([one[: part + EDGE] for one in payloads], other_way, first_w)
    mark = gate0.send((first_w, scale, taps, before, skip))
    mark = first0.send(mark)
    fetched = join(payloads, part, (mark,))
    from_chip = swapped(fetched, "head", 2)
    from_core = swapped(fetched, "head", 1)
    first1 = Reduction(blocks_of(from_core), one_way, first_w)
    gate1 = Reduction(blocks_of(from_core), other_way, gate_w)
    mark = first1.send(fetched)
    shift_t, cum, fade, logs = step_sizes(place, tokens, dt_t, payloads, head_params.T, (mark,))
    mark = gate1.send(cum, logs if n_ctx == 4 else None)
    own_rows = lax.dynamic_slice_in_dim(chained([tokens], mark)[0], me * depth, depth, 1)
    own = [lax.dynamic_slice_in_dim(own_rows, (slot ^ k) * part, part, 0) for k in range(SLOTS)]
    mark = first0.keep(jnp.concatenate([own[0], own_rows[tok_rows - EDGE :]], 0), mark)
    mark = first1.keep(own[1], mark)
    mark = gate0.keep(own[0], mark)
    mark = gate1.keep(own[1], mark)
    firsts01 = finish(
        "fin_first", (first0.total, first1.total), (first0.last, first1.last), scale, (mark,)
    )
    mark = firsts01[0]
    from_chip = chained([from_chip], mark)[0]
    from_both = swapped(from_chip, "head", 1)
    first2, gate2 = (Reduction(blocks_of(from_chip), other_way, w) for w in (first_w, gate_w))
    first3, gate3 = (Reduction(blocks_of(from_both), one_way, w) for w in (first_w, gate_w))
    mark = first2.send(mark)
    mark = first3.send(mark)
    gates01 = finish(
        "fin_gate", (gate0.total, gate1.total), (gate0.last, gate1.last), zx_scale[0:1], (mark,)
    )
    if n_ctx == 4:
        at = part // EDGE
        got, last = chained([gate1.got, gate1.last], gates01[0])
        by_ctx = [(logs, 0), (last, at), (got, 2 * at), (last, at + 1)]
    else:
        by_ctx = [(logs, 0)] + [(swapped(logs, "ctx", j), 0) for j in range(1, n_ctx)]
    factors = falls(both_plans, place, by_ctx, (gates01[0],))
    mark = first2.keep(own[2], gates01[0])
    mark = first3.keep(own[3], mark)
    arrived = passed_along(chained([firsts01[0][part:]], mark)[0], "ctx", 1)
    mark = gate2.send(mark)
    mark = gate3.send(mark)

    halves = 2 if n_ctx == 4 else 1
    conved, *local_states = conv_and_state(
        halves, place, firsts01, (first2.total, first3.total), (first2.last, first3.last), arrived, before, scale,
        taps, fade, (mark,),
    )
    mark = gate2.keep(own[2], conved)
    mark = gate3.keep(own[3], mark)
    gots, plans, runs, start = [], [], [], 0
    for half, run in enumerate(local_states):
        order = bits[::-1] if half else bits
        rows = []
        for i, bit in enumerate(order):
            if i < len(bits) - 1 or half:
                gots.append(swapped(run, "ctx", bit))
            else:
                gots.append(passed_along(run, "ctx", bit))
            if i < len(bits) - 1:
                size = run.shape[1]
                share = factors[:, half * size : (half + 1) * size]
                run = merged(start + 3 * i, share, run, gots[-1], (mark,))
            rows.append(start + 3 * i + 2)
        runs.append(run)
        plans.append(tuple(rows))
        start += 3 * len(bits) + 1
    init_row = 3 * len(bits)
    y_local = inner_output(conved, cum, shift_t, skip, tuple(runs))

    whole_group = local_heads >= per_group
    outs = final_output(
        whole_group,
        tuple(plans),
        init_row,
        place,
        gates01,
        (gate2.total, gate3.total),
        (gate2.last, gate3.last),
        gots,
        y_local,
        conved,
        init_state.reshape(channels, N),
        cum,
        zx_scale[0:1],
        norm_gain[None],
        factors,
    )
    if whole_group:
        return outs[0]
    gated, squares = outs
    slot_hits = (jnp.arange(G) == group_index).astype(F32)
    group_sums = lax.psum(slot_hits[:, None] * squares[:, 0][None, :], "head")
    totals = lax.dynamic_index_in_dim(group_sums, group_index, 0, keepdims=False)
    meansq = totals / (per_group * P_SIZE)
    return (gated * lax.rsqrt(meansq + 1e-05)[:, None] * norm_gain).astype(BF16)


def solution(mesh):
    return jax.shard_map(
        body,
        mesh=mesh,
        in_specs=(
            P("ctx", None),
            P("ctx", None, "head"),
            P(None, "head"),
            P("ctx", None, None),
            P(),
            P("ctx", "head"),
            P(None, "head"),
            P(),
            P(None, "head"),
            P(),
            P(None, "head"),
            P("head", None, None),
            P("head"),
        ),
        out_specs=P("ctx", "head"),
        check_vma=False,
    )
```

```python
import functools
import jax
import jax.numpy as jnp
from jax import lax
from jax.experimental import pallas as pl
from jax.experimental.pallas import tpu as pltpu
from jax.sharding import PartitionSpec as P

H = 128
P_SIZE = 64
N = 256
G = 8
K = 4
SLOTS = 4
LANES = 128
EDGE = 16
EARLY = 2
LOG_PARTS = 3
MIB = 1 << 20
MAIN_MIB = 32
SCALE = 64
BF16 = jnp.bfloat16
F32 = jnp.float32
VMEM = pl.BlockSpec(memory_space=pltpu.VMEM)
SMEM = pl.BlockSpec(memory_space=pltpu.SMEM)
ANY = pl.BlockSpec(memory_space=pl.ANY)


def shape_of(shape, dtype):
    return jax.ShapeDtypeStruct(shape, dtype)


def params(mib):
    return pltpu.CompilerParams(vmem_limit_bytes=mib * MIB)


def cost(flops, moved, transcendentals=0):
    return pl.CostEstimate(
        flops=int(flops) // SCALE, bytes_accessed=int(moved) // SCALE, transcendentals=int(transcendentals) // SCALE
    )


def chained(values, after):
    return lax.optimization_barrier((*values, after))[: len(values)]


def passed_along(x, axis, by):
    length = lax.axis_size(axis)
    pairs = [(i, i + by) for i in range(length) if 0 <= i + by < length]
    return lax.ppermute(x, axis, pairs)


def swapped(x, axis, by):
    length = lax.axis_size(axis)
    return lax.ppermute(x, axis, [(i, i ^ by) for i in range(length)])


def pick_group(values, group_index, axis_index):
    return lax.dynamic_index_in_dim(values, group_index, axis_index, keepdims=False)


def dot32(a, b):
    return jnp.dot(a, b, preferred_element_type=F32)


def silu(v):
    return v / (1.0 + jnp.exp(-v))


def pack_kernel(n, place_ref, *refs):
    blocks, tails, dt_ref, outs = refs[: n - 1], refs[n - 1 : 2 * n - 2], refs[2 * n - 2], refs[2 * n - 1 :]
    part, edge = blocks[0].shape[0], tails[0].shape[0]
    for block, tail, out in zip(blocks, tails, outs):
        out[:part] = block[...]
        out[part : part + edge] = tail[...]
        out[part + edge :] = dt_ref[...]


def pack(place, tokens, dt_t, n):
    dt_rows, depth = dt_t.shape
    part = tokens.shape[0] // SLOTS
    height = part + EDGE + dt_rows
    last = tokens.shape[0] // EDGE - 1
    return pl.pallas_call(
        functools.partial(pack_kernel, n),
        grid_spec=pltpu.PrefetchScalarGridSpec(
            num_scalar_prefetch=1,
            grid=(1,),
            in_specs=[
                pl.BlockSpec((part, depth), lambda i, place, j=j: (place[0], place[1] ^ j))
                for j in range(1, n)
            ]
            + [pl.BlockSpec((EDGE, depth), lambda i, place, j=j: (last, place[1] ^ j)) for j in range(1, n)]
            + [pl.BlockSpec((dt_rows, depth), lambda i, place: (0, 0))],
            out_specs=[pl.BlockSpec((height, depth), lambda i, place: (0, 0))] * (n - 1),
        ),
        out_shape=[shape_of((height, depth), BF16)] * (n - 1),
        name="pack",
        compiler_params=params(58),
    )(place, *[tokens] * (2 * n - 2), dt_t)


def join_kernel(part, count, *refs):
    blocks, out = refs[:count], refs[-1]
    for i, block in enumerate(blocks):
        out[i * part : (i + 1) * part] = block[:part]


def join(blocks, part, after):
    depth = blocks[0].shape[1]
    return pl.pallas_call(
        functools.partial(join_kernel, part, len(blocks)),
        in_specs=[VMEM] * len(blocks) + [ANY] * len(after),
        out_specs=VMEM,
        out_shape=shape_of((part * len(blocks), depth), BF16),
        name="join",
        compiler_params=params(MAIN_MIB),
    )(*blocks, *after)


class Reduction:
    def __init__(self, blocks, order, weights):
        self.blocks, self.order, self.weights = blocks, order, weights
        self.part = blocks[0].shape[0]
        self.n = len(blocks) + 1

    def rows(self, offsets, after):
        return jnp.concatenate(chained([self.blocks[j - 1] for j in offsets], after), 0)

    def send(self, after, extra=None):
        offsets = [j for j in range(self.n) if j & self.order[0]]
        out = dot32(self.rows(offsets, after), self.weights).astype(BF16)
        self.extra = extra
        if extra is not None:
            out = jnp.concatenate([out, extra], 0)
        self.got = swapped(out, "ctx", self.order[0])
        return out

    def keep(self, own, after):
        self.blocks = [*self.blocks, own]
        kept = [j for j in range(self.n) if not j & self.order[0]]
        size = self.part
        got = [self.got[i * size : (i + 1) * size] for i in range(len(kept))]
        bit = self.order[1]
        gone = [i for i, j in enumerate(kept) if j & bit]
        stay = [i for i, j in enumerate(kept) if not j & bit]
        rows = self.rows([kept[i] for i in gone], after)
        out = (dot32(rows, self.weights) + jnp.concatenate([got[i] for i in gone], 0)).astype(BF16)
        mark = out
        if self.extra is not None:
            out = jnp.concatenate([out, self.extra, self.got[size * len(kept) :]], 0)
        arrived = swapped(out, "ctx", bit)
        rows = self.rows([kept[i] for i in stay], after)
        total = dot32(rows, self.weights) + jnp.concatenate([got[i] for i in stay], 0)
        kept = [kept[i] for i in stay]
        for bit in self.order[2:]:
            total = total + arrived.astype(F32)
            gone = [i for i, j in enumerate(kept) if j & bit]
            stay = [i for i, j in enumerate(kept) if not j & bit]
            parts = [total[i * size : (i + 1) * size] for i in range(len(kept))]
            out = jnp.concatenate([parts[i] for i in gone], 0).astype(BF16)
            total = jnp.concatenate([parts[i] for i in stay], 0)
            arrived = swapped(out, "ctx", bit)
            kept = [kept[i] for i in stay]
        self.total, self.last = total, arrived
        return mark


def finished(total, last, scale):
    return ((total + last.astype(F32)) * scale).astype(BF16)


def finish_kernel(count, *refs):
    totals, lasts, scale_ref, outs = refs[:count], refs[count : 2 * count], refs[2 * count], refs[-count:]
    for total, last, out in zip(totals, lasts, outs):
        out[...] = finished(total[...], last[: total.shape[0]], scale_ref[...])


def finish(name, totals, lasts, scale, after):
    count = len(totals)
    lasts = chained(lasts, after[0])
    return pl.pallas_call(
        functools.partial(finish_kernel, count),
        in_specs=[VMEM] * (2 * count + 1) + [ANY] * len(after),
        out_specs=[VMEM] * count,
        out_shape=[shape_of(t.shape, BF16) for t in totals],
        cost_estimate=cost(4 * count * totals[0].size, 8 * count * totals[0].size),
        name=name,
        compiler_params=params(12),
    )(*totals, *lasts, scale, *after)


def quarter_values(values, totals, lasts, scale):
    early = [v[...] for v in values]
    return early + [finished(t[...], l[...], scale) for t, l in zip(totals, lasts)]


def step_kernel(n, me_ref, tok_ref, *refs):
    weights, heads_ref = refs[:n], refs[n]
    shift_t_ref, cum_ref, fade_ref, log_ref, acc = refs[-5:]
    j = pl.program_id(0)

    @pl.when(j == 0)
    def _():
        acc[...] = jnp.zeros_like(acc)

    for i in range(n):

        @pl.when(j == i)
        def _():
            acc[...] += lax.dot_general(
                weights[i][...], tok_ref[...], (((1,), (1,)), ((), ())), preferred_element_type=F32
            )

    @pl.when(j == pl.num_programs(0) - 1)
    def _():
        v = acc[: heads_ref.shape[0]] + heads_ref[:, 0:1]
        step = jnp.maximum(v, 0.0) + jnp.log1p(jnp.exp(-jnp.abs(v)))
        rate = -jnp.exp(heads_ref[:, 1:2]) * step
        rows = rate.shape[1]
        up_to = lax.broadcasted_iota(jnp.int32, (rows, rows), 0) <= lax.broadcasted_iota(
            jnp.int32, (rows, rows), 1
        )
        cum = jnp.dot(
            rate, up_to.astype(F32), precision=lax.Precision.HIGHEST, preferred_element_type=F32
        )
        last = cum[:, rows - 1 : rows]
        shift_t_ref[...] = cum - jnp.log(step)
        cum_ref[...] = cum.T
        fade_ref[...] = (jnp.exp(last - cum) * step).T
        left = jnp.broadcast_to(last.T, (8, last.shape[0]))
        hits = head_spread(last.shape[0])
        index = lax.broadcasted_iota(jnp.int32, log_ref.shape, 0)
        block = jnp.zeros(log_ref.shape, F32)
        for i in range(LOG_PARTS):
            term = left.astype(BF16)
            left = left - term.astype(F32)
            block = jnp.where(index == i, dot32(term, hits)[0:1], block)
        log_ref[...] = block.astype(BF16)


def step_sizes(place, tokens, dt_t, payloads, heads, after):
    dt_rows, depth = dt_t.shape
    local_heads = heads.shape[0]
    n = len(payloads) + 1
    rows = tokens.shape[0]
    last = payloads[0].shape[0] // dt_rows - 1
    whole = lambda shape: pl.BlockSpec(shape, lambda j, place: (0, 0))
    return pl.pallas_call(
        functools.partial(step_kernel, n),
        grid_spec=pltpu.PrefetchScalarGridSpec(
            num_scalar_prefetch=1,
            grid=(n,),
            in_specs=[
                pl.BlockSpec((rows, depth), lambda j, place: (0, place[1] ^ j)),
                whole((dt_rows, depth)),
            ]
            + [pl.BlockSpec((dt_rows, depth), lambda j, place: (last, 0))] * (n - 1)
            + [whole((local_heads, 3))]
            + [ANY] * len(after),
            out_specs=[
                whole((local_heads, rows)),
                whole((rows, local_heads)),
                whole((rows, local_heads)),
                whole((EDGE, local_heads * P_SIZE)),
            ],
            scratch_shapes=[pltpu.VMEM((dt_rows, rows), F32)],
        ),
        out_shape=[
            shape_of((local_heads, rows), F32),
            shape_of((rows, local_heads), F32),
            shape_of((rows, local_heads), F32),
            shape_of((EDGE, local_heads * P_SIZE), BF16),
        ],
        cost_estimate=cost(2 * n * rows * depth * LANES, 2 * n * rows * depth),
        name="steps",
        compiler_params=params(MAIN_MIB),
    )(place, tokens, dt_t, *payloads, heads, *after)


def head_spread(local_heads):
    channels = local_heads * P_SIZE
    hit = (
        lax.broadcasted_iota(jnp.int32, (local_heads, channels), 1) // P_SIZE
        == lax.broadcasted_iota(jnp.int32, (local_heads, channels), 0)
    )
    return hit.astype(F32).astype(BF16)


def spread_heads(values, hits):
    high = values.astype(BF16)
    low = (values - high.astype(F32)).astype(BF16)
    return dot32(high, hits) + dot32(low, hits)


def conv_kernel(count, place_ref, *refs):
    values, totals, lasts = refs[:EARLY], refs[EARLY:SLOTS], refs[SLOTS : 2 * SLOTS - EARLY]
    arrived_ref, before_ref, scale_ref, taps_ref, fade_ref = refs[2 * SLOTS - EARLY : 2 * SLOTS - EARLY + 5]
    conv_ref, states, vals = refs[-2 - count], refs[-1 - count : -1], refs[-1]
    part, width = totals[0].shape
    rows = part * SLOTS
    channels = width - 2 * N
    slot = place_ref[0]
    first = place_ref[1] == 0
    vals[:EDGE] = jnp.where(first, before_ref[...].astype(F32), arrived_ref[...].astype(F32))
    for k, value in enumerate(quarter_values(values, totals, lasts, scale_ref[...])):
        start = pl.multiple_of(EDGE + (slot ^ k) * part, EDGE)
        vals[pl.ds(start, part)] = value[:part].astype(F32)
    for c in range(0, width, 2 * LANES):
        cols = slice(c, c + 2 * LANES)
        for r in range(0, rows, part):
            summed = taps_ref[K : K + 1, cols]
            for tap in range(K):
                at = r + EDGE - (K - 1) + tap
                summed = summed + taps_ref[tap : tap + 1, cols] * vals[at : at + part, cols]
            conv_ref[r : r + part, cols] = silu(summed).astype(BF16)
    hits = head_spread(channels // P_SIZE)
    faded = spread_heads(fade_ref[...], hits) * conv_ref[:, :channels].astype(F32)
    state = lax.dot_general(
        conv_ref[:, channels : channels + N],
        faded.astype(BF16),
        (((0,), (0,)), ((), ())),
        preferred_element_type=F32,
    ).astype(BF16)
    size = channels // len(states)
    for i, out in enumerate(states):
        out[...] = state[:, i * size : (i + 1) * size]


def conv_and_state(count, place, values, totals, lasts, arrived, before, scale, taps, fade, after):
    part, width = totals[0].shape
    rows = part * SLOTS
    lasts = chained(lasts, after[0])
    return pl.pallas_call(
        functools.partial(conv_kernel, count),
        in_specs=[SMEM] + [VMEM] * (2 * SLOTS - EARLY + 5) + [ANY] * len(after),
        out_specs=[VMEM] * (1 + count),
        out_shape=[shape_of((rows, width), BF16)] + [shape_of((N, (width - 2 * N) // count), BF16)] * count,
        scratch_shapes=[pltpu.VMEM((rows + EDGE, width), F32)],
        cost_estimate=cost(30 * rows * width, 12 * rows * width, 2 * rows * width),
        name="conv",
        compiler_params=params(MAIN_MIB),
    )(place, *values, *totals, *lasts, arrived, before, scale, taps, fade, *after)


def inner_kernel(conv_ref, cum_ref, shift_t_ref, skip_ref, *refs):
    y_ref, scores = refs[-2:]
    rows, width = conv_ref.shape
    channels = width - 2 * N
    size = LANES
    blocks = rows // size
    nt = (((1,), (1,)), ((), ()))
    scores[...] = lax.dot_general(
        conv_ref[:, channels + N :], conv_ref[:, channels : channels + N], nt, preferred_element_type=F32
    )
    lower = lax.broadcasted_iota(jnp.int32, (size, size), 0) >= lax.broadcasted_iota(
        jnp.int32, (size, size), 1
    )
    left = lax.broadcasted_iota(jnp.int32, (size, 2 * P_SIZE), 1) < P_SIZE
    for pair in range(channels // (2 * P_SIZE)):
        cols = slice(pair * 2 * P_SIZE, (pair + 1) * 2 * P_SIZE)
        for a in range(blocks):
            t = slice(a * size, (a + 1) * size)
            products = []
            for h in (2 * pair, 2 * pair + 1):
                here = cum_ref[t, h : h + 1]
                own = jnp.where(lower, here - shift_t_ref[h : h + 1, t], -jnp.inf)
                weights = jnp.exp(own) * scores[t, t]
                if a > 0:
                    before = slice(0, a * size)
                    earlier = jnp.exp(here - shift_t_ref[h : h + 1, before]) * scores[t, before]
                    weights = jnp.concatenate([earlier, weights], 1)
                products.append(dot32(weights.astype(BF16), conv_ref[: (a + 1) * size, cols]))
            y_ref[t, cols] = jnp.where(left, products[0], products[1]) + skip_ref[:, cols] * conv_ref[
                t, cols
            ].astype(F32)


def inner_output(conved, cum, shift_t, skip, after):
    rows, width = conved.shape
    channels = width - 2 * N
    return pl.pallas_call(
        inner_kernel,
        in_specs=[VMEM] * 4 + [ANY] * len(after),
        out_specs=VMEM,
        out_shape=shape_of((rows, channels), F32),
        scratch_shapes=[pltpu.VMEM((rows, rows), F32)],
        cost_estimate=cost(2 * rows * rows * channels, 8 * rows * width, rows * rows * channels // P_SIZE),
        name="inner",
        compiler_params=params(MAIN_MIB),
    )(conved, cum, shift_t, skip, *after)


def falls_kernel(n, plan, place_ref, *refs):
    logs, out_ref = refs[:n], refs[-1]
    values = []
    for log in logs:
        block = log[...].astype(F32)
        values.append(sum(block[i : i + 1] for i in range(LOG_PARTS)))
    index = lax.broadcasted_iota(jnp.int32, out_ref.shape, 0)
    block = jnp.zeros(out_ref.shape, F32)
    for i, (counts, parts) in enumerate(plan(place_ref[1], n)):
        total = jnp.zeros_like(values[0])
        for present, offset in parts:
            total = total + jnp.where(present, values[offset], 0.0)
        block = jnp.where(index == i, jnp.where(counts, jnp.exp(total), 0.0), block)
    out_ref[...] = block


def falls(plan, place, logs, after):
    n = len(logs)
    channels = logs[0][0].shape[1]
    rows = -(-len(plan(0, n)) // 8) * 8
    return pl.pallas_call(
        functools.partial(falls_kernel, n, plan),
        grid_spec=pltpu.PrefetchScalarGridSpec(
            num_scalar_prefetch=1,
            grid=(1,),
            in_specs=[pl.BlockSpec((EDGE, channels), lambda i, place, at=at: (at, 0)) for _, at in logs]
            + [ANY] * len(after),
            out_specs=pl.BlockSpec((rows, channels), lambda i, place: (0, 0)),
        ),
        out_shape=shape_of((rows, channels), F32),
        name="falls",
        compiler_params=params(8),
    )(place, *[array for array, _ in logs], *after)


def scan_plan(me, n):
    out, before = [], []
    bit = 1
    while bit < n:
        later = (me & bit) > 0
        own_span = [(True, j) for j in range(bit)]
        got_span = [(True, j) for j in range(bit, 2 * bit)]
        out.append((True, [(jnp.logical_not(later), j) for _, j in got_span]))
        out.append((True, [(later, j) for _, j in own_span]))
        out.append((later, list(before)))
        before += [(later, j) for _, j in got_span]
        bit *= 2
    return out + [(True, before)]


def swap_plan(me, n):
    low, high = (me & 1) > 0, (me & 2) > 0
    return [
        (jnp.logical_not(low), []),
        (high, [(jnp.logical_not(low), 0), (jnp.logical_not(low), 3)]),
        (high, [(low, 1), (jnp.logical_not(low), 3)]),
        (True, []),
        (True, []),
        (True, []),
    ]


def both_plans(me, n):
    return scan_plan(me, n) + (swap_plan(me, n) if n == 4 else [])


def merge_kernel(row, falls_ref, own_ref, got_ref, *refs):
    own_fall, got_fall = falls_ref[row : row + 1], falls_ref[row + 1 : row + 2]
    refs[-1][...] = (own_fall * own_ref[...].astype(F32) + got_fall * got_ref[...].astype(F32)).astype(BF16)


def merged(row, factors, own, got, after):
    return pl.pallas_call(
        functools.partial(merge_kernel, row),
        in_specs=[VMEM] * 3 + [ANY] * len(after),
        out_specs=VMEM,
        out_shape=shape_of(own.shape, BF16),
        cost_estimate=cost(4 * own.size, 6 * own.size),
        name="merge",
        compiler_params=params(12),
    )(factors, own, got, *after)


def final_kernel(whole_group, plans, init_row, place_ref, *refs):
    rounds = sum(len(rows) for rows in plans)
    values, totals, lasts = refs[:EARLY], refs[EARLY:SLOTS], refs[SLOTS : 2 * SLOTS - EARLY]
    refs = refs[2 * SLOTS - EARLY :]
    gots, refs = refs[:rounds], refs[rounds:]
    y_ref, conv_ref, init_ref, cum_ref, scale_ref, gain_ref, falls_ref = refs[:7]
    outs = refs[7:]
    part, channels = totals[0].shape
    slot = place_ref[0]
    hits = head_spread(channels // P_SIZE)
    size = channels // len(plans)
    states = []
    for i, rows in enumerate(plans):
        cols = slice(i * size, (i + 1) * size)
        states.append(
            sum(
                falls_ref[row : row + 1, cols] * got[...].astype(F32)
                for row, got in zip(rows, gots[i * len(rows) : (i + 1) * len(rows)])
            )
        )
    state = jnp.concatenate(states, 1).astype(BF16)
    init = init_ref[...].astype(BF16)
    init_fall = falls_ref[init_row : init_row + 1]
    nt = (((1,), (1,)), ((), ()))
    for k, value in enumerate(quarter_values(values, totals, lasts, scale_ref[...])):
        at = pl.ds(pl.multiple_of((slot ^ k) * part, part), part)
        c_part = conv_ref[at, channels + N :]
        carried = dot32(c_part, state)
        carried = carried + init_fall * lax.dot_general(c_part, init, nt, preferred_element_type=F32)
        y = y_ref[at] + carried * spread_heads(jnp.exp(cum_ref[at]), hits)
        gated = y * silu(value.astype(F32))
        squares = jnp.sum(gated * gated, axis=1, keepdims=True)
        if whole_group:
            meansq = squares / (H // G * P_SIZE)
            outs[0][at] = (gated * lax.rsqrt(meansq + 1e-05) * gain_ref[...]).astype(BF16)
        else:
            outs[0][at] = gated
            outs[1][at] = jnp.broadcast_to(squares, (part, LANES))


def final_output(whole_group, plans, init_row, place, values, totals, lasts, gots, y, conved, init, cum, scale, gain, factors):
    rows, channels = y.shape
    if whole_group:
        outs = [shape_of((rows, channels), BF16)]
    else:
        outs = [shape_of((rows, channels), F32), shape_of((rows, LANES), F32)]
    return pl.pallas_call(
        functools.partial(final_kernel, whole_group, plans, init_row),
        in_specs=[SMEM] + [VMEM] * (2 * SLOTS - EARLY + 7 + len(gots)),
        out_specs=[VMEM] * len(outs),
        out_shape=outs,
        cost_estimate=cost(2 * rows * channels * N, 12 * rows * channels, 2 * rows * channels),
        name="final",
        compiler_params=params(MAIN_MIB),
    )(place, *values, *totals, *lasts, *gots, y, conved, init, cum, scale, gain, factors)


def body(
    tokens,
    w_zx,
    zx_scale,
    w_bc,
    bc_scale,
    w_dt,
    conv_x,
    conv_bc,
    tail_x,
    tail_bc,
    head_params,
    init_state,
    norm_gain,
):
    tok_rows = tokens.shape[0]
    depth = w_zx.shape[0]
    local_heads = head_params.shape[1]
    channels = local_heads * P_SIZE
    per_group = H // G
    n_ctx = lax.axis_size("ctx")
    me = lax.axis_index("ctx")
    head_place = lax.axis_index("head")
    group_index = head_place * local_heads // per_group
    bits = [1 << i for i in range(n_ctx.bit_length() - 1)]
    part = tok_rows // SLOTS
    slot = head_place % SLOTS
    place = jnp.stack([slot.astype(jnp.int32), me.astype(jnp.int32)])

    dt_t = w_dt.T
    if local_heads % EDGE:
        dt_t = jnp.pad(dt_t, ((0, EDGE - local_heads % EDGE), (0, 0)))
    payloads = pack(place, tokens, dt_t, n_ctx)
    payloads = [swapped(one, "ctx", j) for j, one in enumerate(payloads, 1)]
    w_all = jnp.transpose(w_zx, (1, 0, 2))
    bc_rows = pick_group(w_bc, group_index, 1)
    scale = jnp.concatenate([zx_scale[1], pick_group(bc_scale, group_index, 0)], 0)[None]
    taps = jnp.concatenate([conv_x, pick_group(conv_bc, group_index, 1)], 1)
    before = jnp.concatenate([tail_x, pick_group(tail_bc, group_index, 1)], 1)
    before = jnp.pad(before, ((EDGE - (K - 1), 0), (0, 0)))
    skip = jnp.repeat(head_params[2], P_SIZE)[None]
    gate_w = chained([w_all[0]], bc_rows)[0]
    first_w = jnp.concatenate([w_all[1], bc_rows], 1)

    def blocks_of(rows):
        return [rows[i * part : (i + 1) * part] for i in range(n_ctx - 1)]

    one_way, other_way = bits, bits[::-1]
    gate0 = Reduction([one[:part] for one in payloads], one_way, gate_w)
    first0 = Reduction([one[: part + EDGE] for one in payloads], other_way, first_w)
    mark = gate0.send((first_w, scale, taps, before, skip))
    mark = first0.send(mark)
    fetched = join(payloads, part, (mark,))
    from_chip = swapped(fetched, "head", 2)
    from_core = swapped(fetched, "head", 1)
    first1 = Reduction(blocks_of(from_core), one_way, first_w)
    gate1 = Reduction(blocks_of(from_core), other_way, gate_w)
    mark = first1.send(fetched)
    shift_t, cum, fade, logs = step_sizes(place, tokens, dt_t, payloads, head_params.T, (mark,))
    mark = gate1.send(cum, logs if n_ctx == 4 else None)
    own_rows = lax.dynamic_slice_in_dim(chained([tokens], mark)[0], me * depth, depth, 1)
    own = [lax.dynamic_slice_in_dim(own_rows, (slot ^ k) * part, part, 0) for k in range(SLOTS)]
    mark = first0.keep(jnp.concatenate([own[0], own_rows[tok_rows - EDGE :]], 0), mark)
    mark = first1.keep(own[1], mark)
    mark = gate0.keep(own[0], mark)
    mark = gate1.keep(own[1], mark)
    from_chip = chained([from_chip], mark)[0]
    from_both = swapped(from_chip, "head", 1)
    firsts01 = finish(
        "fin_first", (first0.total, first1.total), (first0.last, first1.last), scale, (mark,)
    )
    mark = firsts01[0]
    first2, gate2 = (Reduction(blocks_of(from_chip), other_way, w) for w in (first_w, gate_w))
    first3, gate3 = (Reduction(blocks_of(from_both), one_way, w) for w in (first_w, gate_w))
    mark = first3.send(mark)
    mark = first2.send(mark)
    gates01 = finish(
        "fin_gate", (gate0.total, gate1.total), (gate0.last, gate1.last), zx_scale[0:1], (mark,)
    )
    if n_ctx == 4:
        at = part // EDGE
        got, last = chained([gate1.got, gate1.last], gates01[0])
        by_ctx = [(logs, 0), (last, at), (got, 2 * at), (last, at + 1)]
    else:
        by_ctx = [(logs, 0)] + [(swapped(logs, "ctx", j), 0) for j in range(1, n_ctx)]
    factors = falls(both_plans, place, by_ctx, (gates01[0],))
    mark = first3.keep(own[3], gates01[0])
    mark = first2.keep(own[2], mark)
    arrived = passed_along(chained([firsts01[0][part:]], mark)[0], "ctx", 1)
    mark = gate2.send(mark)
    mark = gate3.send(mark)

    halves = 2 if n_ctx == 4 else 1
    conved, *local_states = conv_and_state(
        halves, place, firsts01, (first2.total, first3.total), (first2.last, first3.last), arrived, before, scale,
        taps, fade, (mark,),
    )
    mark = gate2.keep(own[2], conved)
    mark = gate3.keep(own[3], mark)
    gots, plans, runs, start = [], [], [], 0
    for half, run in enumerate(local_states):
        order = bits[::-1] if half else bits
        rows = []
        for i, bit in enumerate(order):
            if i < len(bits) - 1 or half:
                gots.append(swapped(run, "ctx", bit))
            else:
                gots.append(passed_along(run, "ctx", bit))
            if i < len(bits) - 1:
                size = run.shape[1]
                share = factors[:, half * size : (half + 1) * size]
                run = merged(start + 3 * i, share, run, gots[-1], (mark,))
            rows.append(start + 3 * i + 2)
        runs.append(run)
        plans.append(tuple(rows))
        start += 3 * len(bits) + 1
    init_row = 3 * len(bits)
    y_local = inner_output(conved, cum, shift_t, skip, tuple(runs))

    whole_group = local_heads >= per_group
    outs = final_output(
        whole_group,
        tuple(plans),
        init_row,
        place,
        gates01,
        (gate2.total, gate3.total),
        (gate2.last, gate3.last),
        gots,
        y_local,
        conved,
        init_state.reshape(channels, N),
        cum,
        zx_scale[0:1],
        norm_gain[None],
        factors,
    )
    if whole_group:
        return outs[0]
    gated, squares = outs
    slot_hits = (jnp.arange(G) == group_index).astype(F32)
    group_sums = lax.psum(slot_hits[:, None] * squares[:, 0][None, :], "head")
    totals = lax.dynamic_index_in_dim(group_sums, group_index, 0, keepdims=False)
    meansq = totals / (per_group * P_SIZE)
    return (gated * lax.rsqrt(meansq + 1e-05)[:, None] * norm_gain).astype(BF16)


def solution(mesh):
    return jax.shard_map(
        body,
        mesh=mesh,
        in_specs=(
            P("ctx", None),
            P("ctx", None, "head"),
            P(None, "head"),
            P("ctx", None, None),
            P(),
            P("ctx", "head"),
            P(None, "head"),
            P(),
            P(None, "head"),
            P(),
            P(None, "head"),
            P("head", None, None),
            P("head"),
        ),
        out_specs=P("ctx", "head"),
        check_vma=False,
    )
```

```python
import functools
import jax
import jax.numpy as jnp
from jax import lax
from jax.experimental import pallas as pl
from jax.experimental.pallas import tpu as pltpu
from jax.sharding import PartitionSpec as P

H = 128
P_SIZE = 64
N = 256
G = 8
K = 4
SLOTS = 4
LANES = 128
EDGE = 16
EARLY = 2
LOG_PARTS = 3
MIB = 1 << 20
MAIN_MIB = 32
SCALE = 64
BF16 = jnp.bfloat16
F32 = jnp.float32
VMEM = pl.BlockSpec(memory_space=pltpu.VMEM)
SMEM = pl.BlockSpec(memory_space=pltpu.SMEM)
ANY = pl.BlockSpec(memory_space=pl.ANY)


def shape_of(shape, dtype):
    return jax.ShapeDtypeStruct(shape, dtype)


def params(mib):
    return pltpu.CompilerParams(vmem_limit_bytes=mib * MIB)


def cost(flops, moved, transcendentals=0):
    return pl.CostEstimate(
        flops=int(flops) // SCALE, bytes_accessed=int(moved) // SCALE, transcendentals=int(transcendentals) // SCALE
    )


def chained(values, after):
    return lax.optimization_barrier((*values, after))[: len(values)]


def passed_along(x, axis, by):
    length = lax.axis_size(axis)
    pairs = [(i, i + by) for i in range(length) if 0 <= i + by < length]
    return lax.ppermute(x, axis, pairs)


def swapped(x, axis, by):
    length = lax.axis_size(axis)
    return lax.ppermute(x, axis, [(i, i ^ by) for i in range(length)])


def pick_group(values, group_index, axis_index):
    return lax.dynamic_index_in_dim(values, group_index, axis_index, keepdims=False)


def dot32(a, b):
    return jnp.dot(a, b, preferred_element_type=F32)


def silu(v):
    return v / (1.0 + jnp.exp(-v))


def pack_kernel(n, place_ref, *refs):
    blocks, tails, dt_ref, outs = refs[: n - 1], refs[n - 1 : 2 * n - 2], refs[2 * n - 2], refs[2 * n - 1 :]
    part, edge = blocks[0].shape[0], tails[0].shape[0]
    for block, tail, out in zip(blocks, tails, outs):
        out[:part] = block[...]
        out[part : part + edge] = tail[...]
        out[part + edge :] = dt_ref[...]


def pack(place, tokens, dt_t, n):
    dt_rows, depth = dt_t.shape
    part = tokens.shape[0] // SLOTS
    height = part + EDGE + dt_rows
    last = tokens.shape[0] // EDGE - 1
    return pl.pallas_call(
        functools.partial(pack_kernel, n),
        grid_spec=pltpu.PrefetchScalarGridSpec(
            num_scalar_prefetch=1,
            grid=(1,),
            in_specs=[
                pl.BlockSpec((part, depth), lambda i, place, j=j: (place[0], place[1] ^ j))
                for j in range(1, n)
            ]
            + [pl.BlockSpec((EDGE, depth), lambda i, place, j=j: (last, place[1] ^ j)) for j in range(1, n)]
            + [pl.BlockSpec((dt_rows, depth), lambda i, place: (0, 0))],
            out_specs=[pl.BlockSpec((height, depth), lambda i, place: (0, 0))] * (n - 1),
        ),
        out_shape=[shape_of((height, depth), BF16)] * (n - 1),
        name="pack",
        compiler_params=params(58),
    )(place, *[tokens] * (2 * n - 2), dt_t)


def join_kernel(part, count, *refs):
    blocks, out = refs[:count], refs[-1]
    for i, block in enumerate(blocks):
        out[i * part : (i + 1) * part] = block[:part]


def join(blocks, part, after):
    depth = blocks[0].shape[1]
    return pl.pallas_call(
        functools.partial(join_kernel, part, len(blocks)),
        in_specs=[VMEM] * len(blocks) + [ANY] * len(after),
        out_specs=VMEM,
        out_shape=shape_of((part * len(blocks), depth), BF16),
        name="join",
        compiler_params=params(MAIN_MIB),
    )(*blocks, *after)


class Reduction:
    def __init__(self, blocks, order, weights):
        self.blocks, self.order, self.weights = blocks, order, weights
        self.part = blocks[0].shape[0]
        self.n = len(blocks) + 1

    def rows(self, offsets, after):
        return jnp.concatenate(chained([self.blocks[j - 1] for j in offsets], after), 0)

    def send(self, after, extra=None):
        offsets = [j for j in range(self.n) if j & self.order[0]]
        out = dot32(self.rows(offsets, after), self.weights).astype(BF16)
        self.extra = extra
        if extra is not None:
            out = jnp.concatenate([out, extra], 0)
        self.got = swapped(out, "ctx", self.order[0])
        return out

    def keep(self, own, after):
        self.blocks = [*self.blocks, own]
        kept = [j for j in range(self.n) if not j & self.order[0]]
        size = self.part
        got = [self.got[i * size : (i + 1) * size] for i in range(len(kept))]
        bit = self.order[1]
        gone = [i for i, j in enumerate(kept) if j & bit]
        stay = [i for i, j in enumerate(kept) if not j & bit]
        rows = self.rows([kept[i] for i in gone], after)
        out = (dot32(rows, self.weights) + jnp.concatenate([got[i] for i in gone], 0)).astype(BF16)
        mark = out
        if self.extra is not None:
            out = jnp.concatenate([out, self.extra, self.got[size * len(kept) :]], 0)
        arrived = swapped(out, "ctx", bit)
        rows = self.rows([kept[i] for i in stay], after)
        total = dot32(rows, self.weights) + jnp.concatenate([got[i] for i in stay], 0)
        kept = [kept[i] for i in stay]
        for bit in self.order[2:]:
            total = total + arrived.astype(F32)
            gone = [i for i, j in enumerate(kept) if j & bit]
            stay = [i for i, j in enumerate(kept) if not j & bit]
            parts = [total[i * size : (i + 1) * size] for i in range(len(kept))]
            out = jnp.concatenate([parts[i] for i in gone], 0).astype(BF16)
            total = jnp.concatenate([parts[i] for i in stay], 0)
            arrived = swapped(out, "ctx", bit)
            kept = [kept[i] for i in stay]
        self.total, self.last = total, arrived
        return mark


def finished(total, last, scale):
    return ((total + last.astype(F32)) * scale).astype(BF16)


def finish_kernel(count, *refs):
    totals, lasts, scale_ref, outs = refs[:count], refs[count : 2 * count], refs[2 * count], refs[-count:]
    for total, last, out in zip(totals, lasts, outs):
        out[...] = finished(total[...], last[: total.shape[0]], scale_ref[...])


def finish(name, totals, lasts, scale, after):
    count = len(totals)
    lasts = chained(lasts, after[0])
    return pl.pallas_call(
        functools.partial(finish_kernel, count),
        in_specs=[VMEM] * (2 * count + 1) + [ANY] * len(after),
        out_specs=[VMEM] * count,
        out_shape=[shape_of(t.shape, BF16) for t in totals],
        cost_estimate=cost(4 * count * totals[0].size, 8 * count * totals[0].size),
        name=name,
        compiler_params=params(12),
    )(*totals, *lasts, scale, *after)


def quarter_values(values, totals, lasts, scale):
    early = [v[...] for v in values]
    return early + [finished(t[...], l[...], scale) for t, l in zip(totals, lasts)]


def step_kernel(n, me_ref, tok_ref, *refs):
    weights, heads_ref = refs[:n], refs[n]
    shift_t_ref, cum_ref, fade_ref, log_ref, acc = refs[-5:]
    j = pl.program_id(0)

    @pl.when(j == 0)
    def _():
        acc[...] = jnp.zeros_like(acc)

    for i in range(n):

        @pl.when(j == i)
        def _():
            acc[...] += lax.dot_general(
                weights[i][...], tok_ref[...], (((1,), (1,)), ((), ())), preferred_element_type=F32
            )

    @pl.when(j == pl.num_programs(0) - 1)
    def _():
        v = acc[: heads_ref.shape[0]] + heads_ref[:, 0:1]
        step = jnp.maximum(v, 0.0) + jnp.log1p(jnp.exp(-jnp.abs(v)))
        rate = -jnp.exp(heads_ref[:, 1:2]) * step
        rows = rate.shape[1]
        up_to = lax.broadcasted_iota(jnp.int32, (rows, rows), 0) <= lax.broadcasted_iota(
            jnp.int32, (rows, rows), 1
        )
        cum = jnp.dot(
            rate, up_to.astype(F32), precision=lax.Precision.HIGHEST, preferred_element_type=F32
        )
        last = cum[:, rows - 1 : rows]
        shift_t_ref[...] = cum - jnp.log(step)
        cum_ref[...] = cum.T
        fade_ref[...] = (jnp.exp(last - cum) * step).T
        left = jnp.broadcast_to(last.T, (8, last.shape[0]))
        hits = head_spread(last.shape[0])
        index = lax.broadcasted_iota(jnp.int32, log_ref.shape, 0)
        block = jnp.zeros(log_ref.shape, F32)
        for i in range(LOG_PARTS):
            term = left.astype(BF16)
            left = left - term.astype(F32)
            block = jnp.where(index == i, dot32(term, hits)[0:1], block)
        log_ref[...] = block.astype(BF16)


def step_sizes(place, tokens, dt_t, payloads, heads, after):
    dt_rows, depth = dt_t.shape
    local_heads = heads.shape[0]
    n = len(payloads) + 1
    rows = tokens.shape[0]
    last = payloads[0].shape[0] // dt_rows - 1
    whole = lambda shape: pl.BlockSpec(shape, lambda j, place: (0, 0))
    return pl.pallas_call(
        functools.partial(step_kernel, n),
        grid_spec=pltpu.PrefetchScalarGridSpec(
            num_scalar_prefetch=1,
            grid=(n,),
            in_specs=[
                pl.BlockSpec((rows, depth), lambda j, place: (0, place[1] ^ j)),
                whole((dt_rows, depth)),
            ]
            + [pl.BlockSpec((dt_rows, depth), lambda j, place: (last, 0))] * (n - 1)
            + [whole((local_heads, 3))]
            + [ANY] * len(after),
            out_specs=[
                whole((local_heads, rows)),
                whole((rows, local_heads)),
                whole((rows, local_heads)),
                whole((EDGE, local_heads * P_SIZE)),
            ],
            scratch_shapes=[pltpu.VMEM((dt_rows, rows), F32)],
        ),
        out_shape=[
            shape_of((local_heads, rows), F32),
            shape_of((rows, local_heads), F32),
            shape_of((rows, local_heads), F32),
            shape_of((EDGE, local_heads * P_SIZE), BF16),
        ],
        cost_estimate=cost(2 * n * rows * depth * LANES, 2 * n * rows * depth),
        name="steps",
        compiler_params=params(MAIN_MIB),
    )(place, tokens, dt_t, *payloads, heads, *after)


def head_spread(local_heads):
    channels = local_heads * P_SIZE
    hit = (
        lax.broadcasted_iota(jnp.int32, (local_heads, channels), 1) // P_SIZE
        == lax.broadcasted_iota(jnp.int32, (local_heads, channels), 0)
    )
    return hit.astype(F32).astype(BF16)


def spread_heads(values, hits):
    high = values.astype(BF16)
    low = (values - high.astype(F32)).astype(BF16)
    return dot32(high, hits) + dot32(low, hits)


def conv_kernel(count, place_ref, *refs):
    values, totals, lasts = refs[:EARLY], refs[EARLY:SLOTS], refs[SLOTS : 2 * SLOTS - EARLY]
    arrived_ref, before_ref, scale_ref, taps_ref, fade_ref = refs[2 * SLOTS - EARLY : 2 * SLOTS - EARLY + 5]
    conv_ref, states, vals = refs[-2 - count], refs[-1 - count : -1], refs[-1]
    part, width = totals[0].shape
    rows = part * SLOTS
    channels = width - 2 * N
    slot = place_ref[0]
    first = place_ref[1] == 0
    vals[:EDGE] = jnp.where(first, before_ref[...].astype(F32), arrived_ref[...].astype(F32))
    for k, value in enumerate(quarter_values(values, totals, lasts, scale_ref[...])):
        start = pl.multiple_of(EDGE + (slot ^ k) * part, EDGE)
        vals[pl.ds(start, part)] = value[:part].astype(F32)
    for c in range(0, width, 2 * LANES):
        cols = slice(c, c + 2 * LANES)
        for r in range(0, rows, part):
            summed = taps_ref[K : K + 1, cols]
            for tap in range(K):
                at = r + EDGE - (K - 1) + tap
                summed = summed + taps_ref[tap : tap + 1, cols] * vals[at : at + part, cols]
            conv_ref[r : r + part, cols] = silu(summed).astype(BF16)
    hits = head_spread(channels // P_SIZE)
    faded = spread_heads(fade_ref[...], hits) * conv_ref[:, :channels].astype(F32)
    state = lax.dot_general(
        conv_ref[:, channels : channels + N],
        faded.astype(BF16),
        (((0,), (0,)), ((), ())),
        preferred_element_type=F32,
    ).astype(BF16)
    size = channels // len(states)
    for i, out in enumerate(states):
        out[...] = state[:, i * size : (i + 1) * size]


def conv_and_state(count, place, values, totals, lasts, arrived, before, scale, taps, fade, after):
    part, width = totals[0].shape
    rows = part * SLOTS
    lasts = chained(lasts, after[0])
    return pl.pallas_call(
        functools.partial(conv_kernel, count),
        in_specs=[SMEM] + [VMEM] * (2 * SLOTS - EARLY + 5) + [ANY] * len(after),
        out_specs=[VMEM] * (1 + count),
        out_shape=[shape_of((rows, width), BF16)] + [shape_of((N, (width - 2 * N) // count), BF16)] * count,
        scratch_shapes=[pltpu.VMEM((rows + EDGE, width), F32)],
        cost_estimate=cost(30 * rows * width, 12 * rows * width, 2 * rows * width),
        name="conv",
        compiler_params=params(MAIN_MIB),
    )(place, *values, *totals, *lasts, arrived, before, scale, taps, fade, *after)


def inner_kernel(conv_ref, cum_ref, shift_t_ref, skip_ref, *refs):
    y_ref, scores = refs[-2:]
    rows, width = conv_ref.shape
    channels = width - 2 * N
    size = LANES
    blocks = rows // size
    nt = (((1,), (1,)), ((), ()))
    scores[...] = lax.dot_general(
        conv_ref[:, channels + N :], conv_ref[:, channels : channels + N], nt, preferred_element_type=F32
    )
    lower = lax.broadcasted_iota(jnp.int32, (size, size), 0) >= lax.broadcasted_iota(
        jnp.int32, (size, size), 1
    )
    left = lax.broadcasted_iota(jnp.int32, (size, 2 * P_SIZE), 1) < P_SIZE
    for pair in range(channels // (2 * P_SIZE)):
        cols = slice(pair * 2 * P_SIZE, (pair + 1) * 2 * P_SIZE)
        for a in range(blocks):
            t = slice(a * size, (a + 1) * size)
            products = []
            for h in (2 * pair, 2 * pair + 1):
                here = cum_ref[t, h : h + 1]
                own = jnp.where(lower, here - shift_t_ref[h : h + 1, t], -jnp.inf)
                weights = jnp.exp(own) * scores[t, t]
                if a > 0:
                    before = slice(0, a * size)
                    earlier = jnp.exp(here - shift_t_ref[h : h + 1, before]) * scores[t, before]
                    weights = jnp.concatenate([earlier, weights], 1)
                products.append(dot32(weights.astype(BF16), conv_ref[: (a + 1) * size, cols]))
            y_ref[t, cols] = jnp.where(left, products[0], products[1]) + skip_ref[:, cols] * conv_ref[
                t, cols
            ].astype(F32)


def inner_output(conved, cum, shift_t, skip, after):
    rows, width = conved.shape
    channels = width - 2 * N
    return pl.pallas_call(
        inner_kernel,
        in_specs=[VMEM] * 4 + [ANY] * len(after),
        out_specs=VMEM,
        out_shape=shape_of((rows, channels), F32),
        scratch_shapes=[pltpu.VMEM((rows, rows), F32)],
        cost_estimate=cost(2 * rows * rows * channels, 8 * rows * width, rows * rows * channels // P_SIZE),
        name="inner",
        compiler_params=params(MAIN_MIB),
    )(conved, cum, shift_t, skip, *after)


def falls_kernel(n, plan, place_ref, *refs):
    logs, out_ref = refs[:n], refs[-1]
    values = []
    for log in logs:
        block = log[...].astype(F32)
        values.append(sum(block[i : i + 1] for i in range(LOG_PARTS)))
    index = lax.broadcasted_iota(jnp.int32, out_ref.shape, 0)
    block = jnp.zeros(out_ref.shape, F32)
    for i, (counts, parts) in enumerate(plan(place_ref[1], n)):
        total = jnp.zeros_like(values[0])
        for present, offset in parts:
            total = total + jnp.where(present, values[offset], 0.0)
        block = jnp.where(index == i, jnp.where(counts, jnp.exp(total), 0.0), block)
    out_ref[...] = block


def falls(plan, place, logs, after):
    n = len(logs)
    channels = logs[0][0].shape[1]
    rows = -(-len(plan(0, n)) // 8) * 8
    return pl.pallas_call(
        functools.partial(falls_kernel, n, plan),
        grid_spec=pltpu.PrefetchScalarGridSpec(
            num_scalar_prefetch=1,
            grid=(1,),
            in_specs=[pl.BlockSpec((EDGE, channels), lambda i, place, at=at: (at, 0)) for _, at in logs]
            + [ANY] * len(after),
            out_specs=pl.BlockSpec((rows, channels), lambda i, place: (0, 0)),
        ),
        out_shape=shape_of((rows, channels), F32),
        name="falls",
        compiler_params=params(8),
    )(place, *[array for array, _ in logs], *after)


def scan_plan(me, n):
    out, before = [], []
    bit = 1
    while bit < n:
        later = (me & bit) > 0
        own_span = [(True, j) for j in range(bit)]
        got_span = [(True, j) for j in range(bit, 2 * bit)]
        out.append((True, [(jnp.logical_not(later), j) for _, j in got_span]))
        out.append((True, [(later, j) for _, j in own_span]))
        out.append((later, list(before)))
        before += [(later, j) for _, j in got_span]
        bit *= 2
    return out + [(True, before)]


def swap_plan(me, n):
    low, high = (me & 1) > 0, (me & 2) > 0
    return [
        (jnp.logical_not(low), []),
        (high, [(jnp.logical_not(low), 0), (jnp.logical_not(low), 3)]),
        (high, [(low, 1), (jnp.logical_not(low), 3)]),
        (True, []),
        (True, []),
        (True, []),
    ]


def both_plans(me, n):
    return scan_plan(me, n) + (swap_plan(me, n) if n == 4 else [])


def merge_kernel(row, falls_ref, own_ref, got_ref, *refs):
    own_fall, got_fall = falls_ref[row : row + 1], falls_ref[row + 1 : row + 2]
    refs[-1][...] = (own_fall * own_ref[...].astype(F32) + got_fall * got_ref[...].astype(F32)).astype(BF16)


def merged(row, factors, own, got, after):
    return pl.pallas_call(
        functools.partial(merge_kernel, row),
        in_specs=[VMEM] * 3 + [ANY] * len(after),
        out_specs=VMEM,
        out_shape=shape_of(own.shape, BF16),
        cost_estimate=cost(4 * own.size, 6 * own.size),
        name="merge",
        compiler_params=params(12),
    )(factors, own, got, *after)


def final_kernel(whole_group, plans, init_row, place_ref, *refs):
    rounds = sum(len(rows) for rows in plans)
    values, totals, lasts = refs[:EARLY], refs[EARLY:SLOTS], refs[SLOTS : 2 * SLOTS - EARLY]
    refs = refs[2 * SLOTS - EARLY :]
    gots, refs = refs[:rounds], refs[rounds:]
    y_ref, conv_ref, init_ref, cum_ref, scale_ref, gain_ref, falls_ref = refs[:7]
    outs = refs[7:]
    part, channels = totals[0].shape
    slot = place_ref[0]
    hits = head_spread(channels // P_SIZE)
    size = channels // len(plans)
    states = []
    for i, rows in enumerate(plans):
        cols = slice(i * size, (i + 1) * size)
        states.append(
            sum(
                falls_ref[row : row + 1, cols] * got[...].astype(F32)
                for row, got in zip(rows, gots[i * len(rows) : (i + 1) * len(rows)])
            )
        )
    state = jnp.concatenate(states, 1).astype(BF16)
    init = init_ref[...].astype(BF16)
    init_fall = falls_ref[init_row : init_row + 1]
    nt = (((1,), (1,)), ((), ()))
    for k, value in enumerate(quarter_values(values, totals, lasts, scale_ref[...])):
        at = pl.ds(pl.multiple_of((slot ^ k) * part, part), part)
        c_part = conv_ref[at, channels + N :]
        carried = dot32(c_part, state)
        carried = carried + init_fall * lax.dot_general(c_part, init, nt, preferred_element_type=F32)
        y = y_ref[at] + carried * spread_heads(jnp.exp(cum_ref[at]), hits)
        gated = y * silu(value.astype(F32))
        squares = jnp.sum(gated * gated, axis=1, keepdims=True)
        if whole_group:
            meansq = squares / (H // G * P_SIZE)
            outs[0][at] = (gated * lax.rsqrt(meansq + 1e-05) * gain_ref[...]).astype(BF16)
        else:
            outs[0][at] = gated
            outs[1][at] = jnp.broadcast_to(squares, (part, LANES))


def final_output(whole_group, plans, init_row, place, values, totals, lasts, gots, y, conved, init, cum, scale, gain, factors):
    rows, channels = y.shape
    if whole_group:
        outs = [shape_of((rows, channels), BF16)]
    else:
        outs = [shape_of((rows, channels), F32), shape_of((rows, LANES), F32)]
    return pl.pallas_call(
        functools.partial(final_kernel, whole_group, plans, init_row),
        in_specs=[SMEM] + [VMEM] * (2 * SLOTS - EARLY + 7 + len(gots)),
        out_specs=[VMEM] * len(outs),
        out_shape=outs,
        cost_estimate=cost(2 * rows * channels * N, 12 * rows * channels, 2 * rows * channels),
        name="final",
        compiler_params=params(MAIN_MIB),
    )(place, *values, *totals, *lasts, *gots, y, conved, init, cum, scale, gain, factors)


def body(
    tokens,
    w_zx,
    zx_scale,
    w_bc,
    bc_scale,
    w_dt,
    conv_x,
    conv_bc,
    tail_x,
    tail_bc,
    head_params,
    init_state,
    norm_gain,
):
    tok_rows = tokens.shape[0]
    depth = w_zx.shape[0]
    local_heads = head_params.shape[1]
    channels = local_heads * P_SIZE
    per_group = H // G
    n_ctx = lax.axis_size("ctx")
    me = lax.axis_index("ctx")
    head_place = lax.axis_index("head")
    group_index = head_place * local_heads // per_group
    bits = [1 << i for i in range(n_ctx.bit_length() - 1)]
    part = tok_rows // SLOTS
    slot = head_place % SLOTS
    place = jnp.stack([slot.astype(jnp.int32), me.astype(jnp.int32)])

    dt_t = w_dt.T
    if local_heads % EDGE:
        dt_t = jnp.pad(dt_t, ((0, EDGE - local_heads % EDGE), (0, 0)))
    payloads = pack(place, tokens, dt_t, n_ctx)
    payloads = [swapped(one, "ctx", j) for j, one in enumerate(payloads, 1)]
    w_all = jnp.transpose(w_zx, (1, 0, 2))
    bc_rows = pick_group(w_bc, group_index, 1)
    scale = jnp.concatenate([zx_scale[1], pick_group(bc_scale, group_index, 0)], 0)[None]
    taps = jnp.concatenate([conv_x, pick_group(conv_bc, group_index, 1)], 1)
    before = jnp.concatenate([tail_x, pick_group(tail_bc, group_index, 1)], 1)
    before = jnp.pad(before, ((EDGE - (K - 1), 0), (0, 0)))
    skip = jnp.repeat(head_params[2], P_SIZE)[None]
    gate_w = chained([w_all[0]], bc_rows)[0]
    first_w = jnp.concatenate([w_all[1], bc_rows], 1)

    def blocks_of(rows):
        return [rows[i * part : (i + 1) * part] for i in range(n_ctx - 1)]

    one_way, other_way = bits, bits[::-1]
    gate0 = Reduction([one[:part] for one in payloads], one_way, gate_w)
    first0 = Reduction([one[: part + EDGE] for one in payloads], other_way, first_w)
    mark = gate0.send((first_w, scale, taps, before, skip))
    mark = first0.send(mark)
    fetched = join(payloads, part, (mark,))
    from_chip = swapped(fetched, "head", 2)
    from_core = swapped(fetched, "head", 1)
    first1 = Reduction(blocks_of(from_core), one_way, first_w)
    gate1 = Reduction(blocks_of(from_core), other_way, gate_w)
    mark = first1.send(fetched)
    shift_t, cum, fade, logs = step_sizes(place, tokens, dt_t, payloads, head_params.T, (mark,))
    mark = gate1.send(cum, logs if n_ctx == 4 else None)
    own_rows = lax.dynamic_slice_in_dim(chained([tokens], mark)[0], me * depth, depth, 1)
    own = [lax.dynamic_slice_in_dim(own_rows, (slot ^ k) * part, part, 0) for k in range(SLOTS)]
    mark = first0.keep(jnp.concatenate([own[0], own_rows[tok_rows - EDGE :]], 0), mark)
    mark = first1.keep(own[1], mark)
    mark = gate0.keep(own[0], mark)
    mark = gate1.keep(own[1], mark)
    firsts01 = finish(
        "fin_first", (first0.total, first1.total), (first0.last, first1.last), scale, (mark,)
    )
    mark = firsts01[0]
    from_chip = chained([from_chip], mark)[0]
    from_both = swapped(from_chip, "head", 1)
    first2, gate2 = (Reduction(blocks_of(from_chip), other_way, w) for w in (first_w, gate_w))
    first3, gate3 = (Reduction(blocks_of(from_both), one_way, w) for w in (first_w, gate_w))
    mark = first2.send(mark)
    mark = first3.send(mark)
    gates01 = finish(
        "fin_gate", (gate0.total, gate1.total), (gate0.last, gate1.last), zx_scale[0:1], (mark,)
    )
    if n_ctx == 4:
        at = part // EDGE
        got, last = chained([gate1.got, gate1.last], gates01[0])
        by_ctx = [(logs, 0), (last, at), (got, 2 * at), (last, at + 1)]
    else:
        by_ctx = [(logs, 0)] + [(swapped(logs, "ctx", j), 0) for j in range(1, n_ctx)]
    factors = falls(both_plans, place, by_ctx, (gates01[0],))
    mark = first2.keep(own[2], gates01[0])
    mark = first3.keep(own[3], mark)
    arrived = passed_along(chained([firsts01[0][part:]], mark)[0], "ctx", 1)
    mark = gate2.send(mark)
    mark = gate3.send(mark)

    halves = 2 if n_ctx == 4 else 1
    conved, *local_states = conv_and_state(
        halves, place, firsts01, (first2.total, first3.total), (first2.last, first3.last), arrived, before, scale,
        taps, fade, (mark,),
    )
    mark = gate2.keep(own[2], conved)
    mark = gate3.keep(own[3], mark)
    gots, plans, runs, start = [], [], [], 0
    for half, run in enumerate(local_states):
        order = bits[::-1] if half else bits
        rows = []
        for i, bit in enumerate(order):
            if i < len(bits) - 1 or half:
                gots.append(swapped(run, "ctx", bit))
            else:
                gots.append(passed_along(run, "ctx", bit))
            if i < len(bits) - 1:
                size = run.shape[1]
                share = factors[:, half * size : (half + 1) * size]
                run = merged(start + 3 * i, share, run, gots[-1], (mark,))
            rows.append(start + 3 * i + 2)
        runs.append(run)
        plans.append(tuple(rows))
        start += 3 * len(bits) + 1
    init_row = 3 * len(bits)
    y_local = inner_output(conved, cum, shift_t, skip, tuple(runs))

    whole_group = local_heads >= per_group
    outs = final_output(
        whole_group,
        tuple(plans),
        init_row,
        place,
        gates01,
        (gate2.total, gate3.total),
        (gate2.last, gate3.last),
        gots,
        y_local,
        conved,
        init_state.reshape(channels, N),
        cum,
        zx_scale[0:1],
        norm_gain[None],
        factors,
    )
    if whole_group:
        return outs[0]
    gated, squares = outs
    slot_hits = (jnp.arange(G) == group_index).astype(F32)
    group_sums = lax.psum(slot_hits[:, None] * squares[:, 0][None, :], "head")
    totals = lax.dynamic_index_in_dim(group_sums, group_index, 0, keepdims=False)
    meansq = totals / (per_group * P_SIZE)
    return (gated * lax.rsqrt(meansq + 1e-05)[:, None] * norm_gain).astype(BF16)


def solution(mesh):
    return jax.shard_map(
        body,
        mesh=mesh,
        in_specs=(
            P("ctx", None),
            P("ctx", None, "head"),
            P(None, "head"),
            P("ctx", None, None),
            P(),
            P("ctx", "head"),
            P(None, "head"),
            P(),
            P(None, "head"),
            P(),
            P(None, "head"),
            P("head", None, None),
            P("head"),
        ),
        out_specs=P("ctx", "head"),
        check_vma=False,
    )
```

```python
import functools
import jax
import jax.numpy as jnp
from jax import lax
from jax.experimental import pallas as pl
from jax.experimental.pallas import tpu as pltpu
from jax.sharding import PartitionSpec as P

H = 128
P_SIZE = 64
N = 256
G = 8
K = 4
SLOTS = 4
LANES = 128
EDGE = 16
EARLY = 2
LOG_PARTS = 3
MIB = 1 << 20
MAIN_MIB = 32
SCALE = 64
BF16 = jnp.bfloat16
F32 = jnp.float32
VMEM = pl.BlockSpec(memory_space=pltpu.VMEM)
SMEM = pl.BlockSpec(memory_space=pltpu.SMEM)
ANY = pl.BlockSpec(memory_space=pl.ANY)


def shape_of(shape, dtype):
    return jax.ShapeDtypeStruct(shape, dtype)


def params(mib):
    return pltpu.CompilerParams(vmem_limit_bytes=mib * MIB)


def cost(flops, moved, transcendentals=0):
    return pl.CostEstimate(
        flops=int(flops) // SCALE, bytes_accessed=int(moved) // SCALE, transcendentals=int(transcendentals) // SCALE
    )


def chained(values, after):
    return lax.optimization_barrier((*values, after))[: len(values)]


def passed_along(x, axis, by):
    length = lax.axis_size(axis)
    pairs = [(i, i + by) for i in range(length) if 0 <= i + by < length]
    return lax.ppermute(x, axis, pairs)


def swapped(x, axis, by):
    length = lax.axis_size(axis)
    return lax.ppermute(x, axis, [(i, i ^ by) for i in range(length)])


def pick_group(values, group_index, axis_index):
    return lax.dynamic_index_in_dim(values, group_index, axis_index, keepdims=False)


def dot32(a, b):
    return jnp.dot(a, b, preferred_element_type=F32)


def silu(v):
    return v / (1.0 + jnp.exp(-v))


def pack_kernel(n, place_ref, *refs):
    blocks, tails, dt_ref, outs = refs[: n - 1], refs[n - 1 : 2 * n - 2], refs[2 * n - 2], refs[2 * n - 1 :]
    part, edge = blocks[0].shape[0], tails[0].shape[0]
    for block, tail, out in zip(blocks, tails, outs):
        out[:part] = block[...]
        out[part : part + edge] = tail[...]
        out[part + edge :] = dt_ref[...]


def pack(place, tokens, dt_t, n):
    dt_rows, depth = dt_t.shape
    part = tokens.shape[0] // SLOTS
    height = part + EDGE + dt_rows
    last = tokens.shape[0] // EDGE - 1
    return pl.pallas_call(
        functools.partial(pack_kernel, n),
        grid_spec=pltpu.PrefetchScalarGridSpec(
            num_scalar_prefetch=1,
            grid=(1,),
            in_specs=[
                pl.BlockSpec((part, depth), lambda i, place, j=j: (place[0], place[1] ^ j))
                for j in range(1, n)
            ]
            + [pl.BlockSpec((EDGE, depth), lambda i, place, j=j: (last, place[1] ^ j)) for j in range(1, n)]
            + [pl.BlockSpec((dt_rows, depth), lambda i, place: (0, 0))],
            out_specs=[pl.BlockSpec((height, depth), lambda i, place: (0, 0))] * (n - 1),
        ),
        out_shape=[shape_of((height, depth), BF16)] * (n - 1),
        name="pack",
        compiler_params=params(58),
    )(place, *[tokens] * (2 * n - 2), dt_t)


def join_kernel(part, count, *refs):
    blocks, out = refs[:count], refs[-1]
    for i, block in enumerate(blocks):
        out[i * part : (i + 1) * part] = block[:part]


def join(blocks, part, after):
    depth = blocks[0].shape[1]
    return pl.pallas_call(
        functools.partial(join_kernel, part, len(blocks)),
        in_specs=[VMEM] * len(blocks) + [ANY] * len(after),
        out_specs=VMEM,
        out_shape=shape_of((part * len(blocks), depth), BF16),
        name="join",
        compiler_params=params(MAIN_MIB),
    )(*blocks, *after)


class Reduction:
    def __init__(self, blocks, order, weights):
        self.blocks, self.order, self.weights = blocks, order, weights
        self.part = blocks[0].shape[0]
        self.n = len(blocks) + 1

    def rows(self, offsets, after):
        return jnp.concatenate(chained([self.blocks[j - 1] for j in offsets], after), 0)

    def send(self, after, extra=None):
        offsets = [j for j in range(self.n) if j & self.order[0]]
        out = dot32(self.rows(offsets, after), self.weights).astype(BF16)
        self.extra = extra
        if extra is not None:
            out = jnp.concatenate([out, extra], 0)
        self.got = swapped(out, "ctx", self.order[0])
        return out

    def keep(self, own, after):
        self.blocks = [*self.blocks, own]
        kept = [j for j in range(self.n) if not j & self.order[0]]
        size = self.part
        got = [self.got[i * size : (i + 1) * size] for i in range(len(kept))]
        bit = self.order[1]
        gone = [i for i, j in enumerate(kept) if j & bit]
        stay = [i for i, j in enumerate(kept) if not j & bit]
        rows = self.rows([kept[i] for i in gone], after)
        out = (dot32(rows, self.weights) + jnp.concatenate([got[i] for i in gone], 0)).astype(BF16)
        mark = out
        if self.extra is not None:
            out = jnp.concatenate([out, self.extra, self.got[size * len(kept) :]], 0)
        arrived = swapped(out, "ctx", bit)
        rows = self.rows([kept[i] for i in stay], after)
        total = dot32(rows, self.weights) + jnp.concatenate([got[i] for i in stay], 0)
        kept = [kept[i] for i in stay]
        for bit in self.order[2:]:
            total = total + arrived.astype(F32)
            gone = [i for i, j in enumerate(kept) if j & bit]
            stay = [i for i, j in enumerate(kept) if not j & bit]
            parts = [total[i * size : (i + 1) * size] for i in range(len(kept))]
            out = jnp.concatenate([parts[i] for i in gone], 0).astype(BF16)
            total = jnp.concatenate([parts[i] for i in stay], 0)
            arrived = swapped(out, "ctx", bit)
            kept = [kept[i] for i in stay]
        self.total, self.last = total, arrived
        return mark


def finished(total, last, scale):
    return ((total + last.astype(F32)) * scale).astype(BF16)


def finish_kernel(count, *refs):
    totals, lasts, scale_ref, outs = refs[:count], refs[count : 2 * count], refs[2 * count], refs[-count:]
    for total, last, out in zip(totals, lasts, outs):
        out[...] = finished(total[...], last[: total.shape[0]], scale_ref[...])


def finish(name, totals, lasts, scale, after):
    count = len(totals)
    lasts = chained(lasts, after[0])
    return pl.pallas_call(
        functools.partial(finish_kernel, count),
        in_specs=[VMEM] * (2 * count + 1) + [ANY] * len(after),
        out_specs=[VMEM] * count,
        out_shape=[shape_of(t.shape, BF16) for t in totals],
        cost_estimate=cost(4 * count * totals[0].size, 8 * count * totals[0].size),
        name=name,
        compiler_params=params(12),
    )(*totals, *lasts, scale, *after)


def quarter_values(values, totals, lasts, scale):
    early = [v[...] for v in values]
    return early + [finished(t[...], l[...], scale) for t, l in zip(totals, lasts)]


def step_kernel(n, me_ref, tok_ref, *refs):
    weights, heads_ref = refs[:n], refs[n]
    shift_t_ref, cum_ref, fade_ref, log_ref, acc = refs[-5:]
    j = pl.program_id(0)

    @pl.when(j == 0)
    def _():
        acc[...] = jnp.zeros_like(acc)

    for i in range(n):

        @pl.when(j == i)
        def _():
            acc[...] += lax.dot_general(
                weights[i][...], tok_ref[...], (((1,), (1,)), ((), ())), preferred_element_type=F32
            )

    @pl.when(j == pl.num_programs(0) - 1)
    def _():
        v = acc[: heads_ref.shape[0]] + heads_ref[:, 0:1]
        step = jnp.maximum(v, 0.0) + jnp.log1p(jnp.exp(-jnp.abs(v)))
        rate = -jnp.exp(heads_ref[:, 1:2]) * step
        rows = rate.shape[1]
        up_to = lax.broadcasted_iota(jnp.int32, (rows, rows), 0) <= lax.broadcasted_iota(
            jnp.int32, (rows, rows), 1
        )
        cum = jnp.dot(
            rate, up_to.astype(F32), precision=lax.Precision.HIGHEST, preferred_element_type=F32
        )
        last = cum[:, rows - 1 : rows]
        shift_t_ref[...] = cum - jnp.log(step)
        cum_ref[...] = cum.T
        fade_ref[...] = (jnp.exp(last - cum) * step).T
        left = jnp.broadcast_to(last.T, (8, last.shape[0]))
        hits = head_spread(last.shape[0])
        index = lax.broadcasted_iota(jnp.int32, log_ref.shape, 0)
        block = jnp.zeros(log_ref.shape, F32)
        for i in range(LOG_PARTS):
            term = left.astype(BF16)
            left = left - term.astype(F32)
            block = jnp.where(index == i, dot32(term, hits)[0:1], block)
        log_ref[...] = block.astype(BF16)


def step_sizes(place, tokens, dt_t, payloads, heads, after):
    dt_rows, depth = dt_t.shape
    local_heads = heads.shape[0]
    n = len(payloads) + 1
    rows = tokens.shape[0]
    last = payloads[0].shape[0] // dt_rows - 1
    whole = lambda shape: pl.BlockSpec(shape, lambda j, place: (0, 0))
    return pl.pallas_call(
        functools.partial(step_kernel, n),
        grid_spec=pltpu.PrefetchScalarGridSpec(
            num_scalar_prefetch=1,
            grid=(n,),
            in_specs=[
                pl.BlockSpec((rows, depth), lambda j, place: (0, place[1] ^ j)),
                whole((dt_rows, depth)),
            ]
            + [pl.BlockSpec((dt_rows, depth), lambda j, place: (last, 0))] * (n - 1)
            + [whole((local_heads, 3))]
            + [ANY] * len(after),
            out_specs=[
                whole((local_heads, rows)),
                whole((rows, local_heads)),
                whole((rows, local_heads)),
                whole((EDGE, local_heads * P_SIZE)),
            ],
            scratch_shapes=[pltpu.VMEM((dt_rows, rows), F32)],
        ),
        out_shape=[
            shape_of((local_heads, rows), F32),
            shape_of((rows, local_heads), F32),
            shape_of((rows, local_heads), F32),
            shape_of((EDGE, local_heads * P_SIZE), BF16),
        ],
        cost_estimate=cost(2 * n * rows * depth * LANES, 2 * n * rows * depth),
        name="steps",
        compiler_params=params(MAIN_MIB),
    )(place, tokens, dt_t, *payloads, heads, *after)


def head_spread(local_heads):
    channels = local_heads * P_SIZE
    hit = (
        lax.broadcasted_iota(jnp.int32, (local_heads, channels), 1) // P_SIZE
        == lax.broadcasted_iota(jnp.int32, (local_heads, channels), 0)
    )
    return hit.astype(F32).astype(BF16)


def spread_heads(values, hits):
    high = values.astype(BF16)
    low = (values - high.astype(F32)).astype(BF16)
    return dot32(high, hits) + dot32(low, hits)


def conv_kernel(count, place_ref, *refs):
    values, totals, lasts = refs[:EARLY], refs[EARLY:SLOTS], refs[SLOTS : 2 * SLOTS - EARLY]
    arrived_ref, before_ref, scale_ref, taps_ref, fade_ref = refs[2 * SLOTS - EARLY : 2 * SLOTS - EARLY + 5]
    conv_ref, states, vals = refs[-2 - count], refs[-1 - count : -1], refs[-1]
    part, width = totals[0].shape
    rows = part * SLOTS
    channels = width - 2 * N
    slot = place_ref[0]
    first = place_ref[1] == 0
    vals[:EDGE] = jnp.where(first, before_ref[...].astype(F32), arrived_ref[...].astype(F32))
    for k, value in enumerate(quarter_values(values, totals, lasts, scale_ref[...])):
        start = pl.multiple_of(EDGE + (slot ^ k) * part, EDGE)
        vals[pl.ds(start, part)] = value[:part].astype(F32)
    for c in range(0, width, 2 * LANES):
        cols = slice(c, c + 2 * LANES)
        for r in range(0, rows, part):
            summed = taps_ref[K : K + 1, cols]
            for tap in range(K):
                at = r + EDGE - (K - 1) + tap
                summed = summed + taps_ref[tap : tap + 1, cols] * vals[at : at + part, cols]
            conv_ref[r : r + part, cols] = silu(summed).astype(BF16)
    hits = head_spread(channels // P_SIZE)
    faded = spread_heads(fade_ref[...], hits) * conv_ref[:, :channels].astype(F32)
    state = lax.dot_general(
        conv_ref[:, channels : channels + N],
        faded.astype(BF16),
        (((0,), (0,)), ((), ())),
        preferred_element_type=F32,
    ).astype(BF16)
    size = channels // len(states)
    for i, out in enumerate(states):
        out[...] = state[:, i * size : (i + 1) * size]


def conv_and_state(count, place, values, totals, lasts, arrived, before, scale, taps, fade, after):
    part, width = totals[0].shape
    rows = part * SLOTS
    lasts = chained(lasts, after[0])
    return pl.pallas_call(
        functools.partial(conv_kernel, count),
        in_specs=[SMEM] + [VMEM] * (2 * SLOTS - EARLY + 5) + [ANY] * len(after),
        out_specs=[VMEM] * (1 + count),
        out_shape=[shape_of((rows, width), BF16)] + [shape_of((N, (width - 2 * N) // count), BF16)] * count,
        scratch_shapes=[pltpu.VMEM((rows + EDGE, width), F32)],
        cost_estimate=cost(30 * rows * width, 12 * rows * width, 2 * rows * width),
        name="conv",
        compiler_params=params(MAIN_MIB),
    )(place, *values, *totals, *lasts, arrived, before, scale, taps, fade, *after)


def inner_kernel(conv_ref, cum_ref, shift_t_ref, skip_ref, *refs):
    y_ref, scores = refs[-2:]
    rows, width = conv_ref.shape
    channels = width - 2 * N
    size = LANES
    blocks = rows // size
    nt = (((1,), (1,)), ((), ()))
    scores[...] = lax.dot_general(
        conv_ref[:, channels + N :], conv_ref[:, channels : channels + N], nt, preferred_element_type=F32
    )
    lower = lax.broadcasted_iota(jnp.int32, (size, size), 0) >= lax.broadcasted_iota(
        jnp.int32, (size, size), 1
    )
    left = lax.broadcasted_iota(jnp.int32, (size, 2 * P_SIZE), 1) < P_SIZE
    for pair in range(channels // (2 * P_SIZE)):
        cols = slice(pair * 2 * P_SIZE, (pair + 1) * 2 * P_SIZE)
        for a in range(blocks):
            t = slice(a * size, (a + 1) * size)
            products = []
            for h in (2 * pair, 2 * pair + 1):
                here = cum_ref[t, h : h + 1]
                own = jnp.where(lower, here - shift_t_ref[h : h + 1, t], -jnp.inf)
                weights = jnp.exp(own) * scores[t, t]
                if a > 0:
                    before = slice(0, a * size)
                    earlier = jnp.exp(here - shift_t_ref[h : h + 1, before]) * scores[t, before]
                    weights = jnp.concatenate([earlier, weights], 1)
                products.append(dot32(weights.astype(BF16), conv_ref[: (a + 1) * size, cols]))
            y_ref[t, cols] = jnp.where(left, products[0], products[1]) + skip_ref[:, cols] * conv_ref[
                t, cols
            ].astype(F32)


def inner_output(conved, cum, shift_t, skip, after):
    rows, width = conved.shape
    channels = width - 2 * N
    return pl.pallas_call(
        inner_kernel,
        in_specs=[VMEM] * 4 + [ANY] * len(after),
        out_specs=VMEM,
        out_shape=shape_of((rows, channels), F32),
        scratch_shapes=[pltpu.VMEM((rows, rows), F32)],
        cost_estimate=cost(2 * rows * rows * channels, 8 * rows * width, rows * rows * channels // P_SIZE),
        name="inner",
        compiler_params=params(MAIN_MIB),
    )(conved, cum, shift_t, skip, *after)


def falls_kernel(n, plan, place_ref, *refs):
    logs, out_ref = refs[:n], refs[-1]
    values = []
    for log in logs:
        block = log[...].astype(F32)
        values.append(sum(block[i : i + 1] for i in range(LOG_PARTS)))
    index = lax.broadcasted_iota(jnp.int32, out_ref.shape, 0)
    block = jnp.zeros(out_ref.shape, F32)
    for i, (counts, parts) in enumerate(plan(place_ref[1], n)):
        total = jnp.zeros_like(values[0])
        for present, offset in parts:
            total = total + jnp.where(present, values[offset], 0.0)
        block = jnp.where(index == i, jnp.where(counts, jnp.exp(total), 0.0), block)
    out_ref[...] = block


def falls(plan, place, logs, after):
    n = len(logs)
    channels = logs[0][0].shape[1]
    rows = -(-len(plan(0, n)) // 8) * 8
    return pl.pallas_call(
        functools.partial(falls_kernel, n, plan),
        grid_spec=pltpu.PrefetchScalarGridSpec(
            num_scalar_prefetch=1,
            grid=(1,),
            in_specs=[pl.BlockSpec((EDGE, channels), lambda i, place, at=at: (at, 0)) for _, at in logs]
            + [ANY] * len(after),
            out_specs=pl.BlockSpec((rows, channels), lambda i, place: (0, 0)),
        ),
        out_shape=shape_of((rows, channels), F32),
        name="falls",
        compiler_params=params(8),
    )(place, *[array for array, _ in logs], *after)


def scan_plan(me, n):
    out, before = [], []
    bit = 1
    while bit < n:
        later = (me & bit) > 0
        own_span = [(True, j) for j in range(bit)]
        got_span = [(True, j) for j in range(bit, 2 * bit)]
        out.append((True, [(jnp.logical_not(later), j) for _, j in got_span]))
        out.append((True, [(later, j) for _, j in own_span]))
        out.append((later, list(before)))
        before += [(later, j) for _, j in got_span]
        bit *= 2
    return out + [(True, before)]


def swap_plan(me, n):
    low, high = (me & 1) > 0, (me & 2) > 0
    return [
        (jnp.logical_not(low), []),
        (high, [(jnp.logical_not(low), 0), (jnp.logical_not(low), 3)]),
        (high, [(low, 1), (jnp.logical_not(low), 3)]),
        (True, []),
        (True, []),
        (True, []),
    ]


def both_plans(me, n):
    return scan_plan(me, n) + (swap_plan(me, n) if n == 4 else [])


def merge_kernel(row, falls_ref, own_ref, got_ref, *refs):
    own_fall, got_fall = falls_ref[row : row + 1], falls_ref[row + 1 : row + 2]
    refs[-1][...] = (own_fall * own_ref[...].astype(F32) + got_fall * got_ref[...].astype(F32)).astype(BF16)


def merged(row, factors, own, got, after):
    return pl.pallas_call(
        functools.partial(merge_kernel, row),
        in_specs=[VMEM] * 3 + [ANY] * len(after),
        out_specs=VMEM,
        out_shape=shape_of(own.shape, BF16),
        cost_estimate=cost(4 * own.size, 6 * own.size),
        name="merge",
        compiler_params=params(12),
    )(factors, own, got, *after)


def final_kernel(whole_group, plans, init_row, place_ref, *refs):
    rounds = sum(len(rows) for rows in plans)
    values, totals, lasts = refs[:EARLY], refs[EARLY:SLOTS], refs[SLOTS : 2 * SLOTS - EARLY]
    refs = refs[2 * SLOTS - EARLY :]
    gots, refs = refs[:rounds], refs[rounds:]
    y_ref, conv_ref, init_ref, cum_ref, scale_ref, gain_ref, falls_ref = refs[:7]
    outs = refs[7:]
    part, channels = totals[0].shape
    slot = place_ref[0]
    hits = head_spread(channels // P_SIZE)
    size = channels // len(plans)
    states = []
    for i, rows in enumerate(plans):
        cols = slice(i * size, (i + 1) * size)
        states.append(
            sum(
                falls_ref[row : row + 1, cols] * got[...].astype(F32)
                for row, got in zip(rows, gots[i * len(rows) : (i + 1) * len(rows)])
            )
        )
    state = jnp.concatenate(states, 1).astype(BF16)
    init = init_ref[...].astype(BF16)
    init_fall = falls_ref[init_row : init_row + 1]
    nt = (((1,), (1,)), ((), ()))
    for k, value in enumerate(quarter_values(values, totals, lasts, scale_ref[...])):
        at = pl.ds(pl.multiple_of((slot ^ k) * part, part), part)
        c_part = conv_ref[at, channels + N :]
        carried = dot32(c_part, state)
        carried = carried + init_fall * lax.dot_general(c_part, init, nt, preferred_element_type=F32)
        y = y_ref[at] + carried * spread_heads(jnp.exp(cum_ref[at]), hits)
        gated = y * silu(value.astype(F32))
        squares = jnp.sum(gated * gated, axis=1, keepdims=True)
        if whole_group:
            meansq = squares / (H // G * P_SIZE)
            outs[0][at] = (gated * lax.rsqrt(meansq + 1e-05) * gain_ref[...]).astype(BF16)
        else:
            outs[0][at] = gated
            outs[1][at] = jnp.broadcast_to(squares, (part, LANES))


def final_output(whole_group, plans, init_row, place, values, totals, lasts, gots, y, conved, init, cum, scale, gain, factors):
    rows, channels = y.shape
    if whole_group:
        outs = [shape_of((rows, channels), BF16)]
    else:
        outs = [shape_of((rows, channels), F32), shape_of((rows, LANES), F32)]
    return pl.pallas_call(
        functools.partial(final_kernel, whole_group, plans, init_row),
        in_specs=[SMEM] + [VMEM] * (2 * SLOTS - EARLY + 7 + len(gots)),
        out_specs=[VMEM] * len(outs),
        out_shape=outs,
        cost_estimate=cost(2 * rows * channels * N, 12 * rows * channels, 2 * rows * channels),
        name="final",
        compiler_params=params(MAIN_MIB),
    )(place, *values, *totals, *lasts, *gots, y, conved, init, cum, scale, gain, factors)


def body(
    tokens,
    w_zx,
    zx_scale,
    w_bc,
    bc_scale,
    w_dt,
    conv_x,
    conv_bc,
    tail_x,
    tail_bc,
    head_params,
    init_state,
    norm_gain,
):
    tok_rows = tokens.shape[0]
    depth = w_zx.shape[0]
    local_heads = head_params.shape[1]
    channels = local_heads * P_SIZE
    per_group = H // G
    n_ctx = lax.axis_size("ctx")
    me = lax.axis_index("ctx")
    head_place = lax.axis_index("head")
    group_index = head_place * local_heads // per_group
    bits = [1 << i for i in range(n_ctx.bit_length() - 1)]
    part = tok_rows // SLOTS
    slot = head_place % SLOTS
    place = jnp.stack([slot.astype(jnp.int32), me.astype(jnp.int32)])

    dt_t = w_dt.T
    if local_heads % EDGE:
        dt_t = jnp.pad(dt_t, ((0, EDGE - local_heads % EDGE), (0, 0)))
    payloads = pack(place, tokens, dt_t, n_ctx)
    payloads = [swapped(one, "ctx", j) for j, one in enumerate(payloads, 1)]
    w_all = jnp.transpose(w_zx, (1, 0, 2))
    bc_rows = pick_group(w_bc, group_index, 1)
    scale = jnp.concatenate([zx_scale[1], pick_group(bc_scale, group_index, 0)], 0)[None]
    taps = jnp.concatenate([conv_x, pick_group(conv_bc, group_index, 1)], 1)
    before = jnp.concatenate([tail_x, pick_group(tail_bc, group_index, 1)], 1)
    before = jnp.pad(before, ((EDGE - (K - 1), 0), (0, 0)))
    skip = jnp.repeat(head_params[2], P_SIZE)[None]
    gate_w = chained([w_all[0]], bc_rows)[0]
    first_w = jnp.concatenate([w_all[1], bc_rows], 1)

    def blocks_of(rows):
        return [rows[i * part : (i + 1) * part] for i in range(n_ctx - 1)]

    one_way, other_way = bits, bits[::-1]
    gate0 = Reduction([one[:part] for one in payloads], one_way, gate_w)
    first0 = Reduction([one[: part + EDGE] for one in payloads], other_way, first_w)
    mark = gate0.send((first_w, scale, taps, before, skip))
    mark = first0.send(mark)
    fetched = join(payloads, part, (mark,))
    from_chip = swapped(fetched, "head", 2)
    from_core = swapped(fetched, "head", 1)
    first1 = Reduction(blocks_of(from_core), one_way, first_w)
    gate1 = Reduction(blocks_of(from_core), other_way, gate_w)
    mark = first1.send(fetched)
    shift_t, cum, fade, logs = step_sizes(place, tokens, dt_t, payloads, head_params.T, (mark,))
    mark = gate1.send(cum, logs if n_ctx == 4 else None)
    own_rows = lax.dynamic_slice_in_dim(chained([tokens], mark)[0], me * depth, depth, 1)
    own = [lax.dynamic_slice_in_dim(own_rows, (slot ^ k) * part, part, 0) for k in range(SLOTS)]
    mark = first0.keep(jnp.concatenate([own[0], own_rows[tok_rows - EDGE :]], 0), mark)
    mark = first1.keep(own[1], mark)
    mark = gate0.keep(own[0], mark)
    mark = gate1.keep(own[1], mark)
    firsts01 = finish(
        "fin_first", (first0.total, first1.total), (first0.last, first1.last), scale, (mark,)
    )
    mark = firsts01[0]
    from_chip = chained([from_chip], mark)[0]
    from_both = swapped(from_chip, "head", 1)
    first2, gate2 = (Reduction(blocks_of(from_chip), other_way, w) for w in (first_w, gate_w))
    first3, gate3 = (Reduction(blocks_of(from_both), one_way, w) for w in (first_w, gate_w))
    mark = first2.send(mark)
    mark = first3.send(mark)
    gates01 = finish(
        "fin_gate", (gate0.total, gate1.total), (gate0.last, gate1.last), zx_scale[0:1], (mark,)
    )
    if n_ctx == 4:
        at = part // EDGE
        got, last = chained([gate1.got, gate1.last], gates01[0])
        by_ctx = [(logs, 0), (last, at), (got, 2 * at), (last, at + 1)]
    else:
        by_ctx = [(logs, 0)] + [(swapped(logs, "ctx", j), 0) for j in range(1, n_ctx)]
    factors = falls(both_plans, place, by_ctx, (gates01[0],))
    mark = first2.keep(own[2], mark)
    mark = first3.keep(own[3], mark)
    arrived = passed_along(chained([firsts01[0][part:]], mark)[0], "ctx", 1)
    mark = gate2.send(mark)
    mark = gate3.send(mark)

    halves = 2 if n_ctx == 4 else 1
    conved, *local_states = conv_and_state(
        halves, place, firsts01, (first2.total, first3.total), (first2.last, first3.last), arrived, before, scale,
        taps, fade, (mark,),
    )
    mark = gate2.keep(own[2], conved)
    mark = gate3.keep(own[3], mark)
    gots, plans, runs, start = [], [], [], 0
    for half, run in enumerate(local_states):
        order = bits[::-1] if half else bits
        rows = []
        for i, bit in enumerate(order):
            if i < len(bits) - 1 or half:
                gots.append(swapped(run, "ctx", bit))
            else:
                gots.append(passed_along(run, "ctx", bit))
            if i < len(bits) - 1:
                size = run.shape[1]
                share = factors[:, half * size : (half + 1) * size]
                run = merged(start + 3 * i, share, run, gots[-1], (mark,))
            rows.append(start + 3 * i + 2)
        runs.append(run)
        plans.append(tuple(rows))
        start += 3 * len(bits) + 1
    init_row = 3 * len(bits)
    y_local = inner_output(conved, cum, shift_t, skip, tuple(runs))

    whole_group = local_heads >= per_group
    outs = final_output(
        whole_group,
        tuple(plans),
        init_row,
        place,
        gates01,
        (gate2.total, gate3.total),
        (gate2.last, gate3.last),
        gots,
        y_local,
        conved,
        init_state.reshape(channels, N),
        cum,
        zx_scale[0:1],
        norm_gain[None],
        factors,
    )
    if whole_group:
        return outs[0]
    gated, squares = outs
    slot_hits = (jnp.arange(G) == group_index).astype(F32)
    group_sums = lax.psum(slot_hits[:, None] * squares[:, 0][None, :], "head")
    totals = lax.dynamic_index_in_dim(group_sums, group_index, 0, keepdims=False)
    meansq = totals / (per_group * P_SIZE)
    return (gated * lax.rsqrt(meansq + 1e-05)[:, None] * norm_gain).astype(BF16)


def solution(mesh):
    return jax.shard_map(
        body,
        mesh=mesh,
        in_specs=(
            P("ctx", None),
            P("ctx", None, "head"),
            P(None, "head"),
            P("ctx", None, None),
            P(),
            P("ctx", "head"),
            P(None, "head"),
            P(),
            P(None, "head"),
            P(),
            P(None, "head"),
            P("head", None, None),
            P("head"),
        ),
        out_specs=P("ctx", "head"),
        check_vma=False,
    )
```
